32 devices in a mesh: dp: 16 (over z, y, x), mp: 2 (over core).
Axes of the slice: x: 2, y: 2, z: 4, core: 2. Of those that a mesh axis runs over, the one named last changes fastest.
Arguments:
- tokens: bfloat16 [48, 2048, 768], P('dp', None, 'mp'), may hold values from -6 to 6
- segments: int32 [48, 2048], P('dp'), may hold values from 0 to 3, never falling along the last dimension, each value on 1 to 1024 neighbouring positions
- present: int32 [48, 2048], P('dp'), may hold values 0 or 1
- chosen: int32 [48, 256], P('dp'), may hold values from 0 to 2047, as said below
- attention: bfloat16 [3, 768, 768], P(None, 'dp', 'mp'), may hold values from -0.21875 to 0.21875
- mixing: bfloat16 [768, 768], P('mp', 'dp'), may hold values from -0.875 to 0.875
- expand: bfloat16 [768, 3072], P('dp', 'mp'), may hold values from -0.21875 to 0.21875
- contract: bfloat16 [3072, 768], P('mp', 'dp'), may hold values from -0.109375 to 0.109375
- prenorm: bfloat16 [768], P('dp'), may hold values from 0.5 to 1.5
- midnorm: bfloat16 [768], P('dp'), may hold values from 0.5 to 1.5
- router: bfloat16 [768], P('dp'), may hold values from -0.21875 to 0.21875
- cotangent: bfloat16 [48, 2048, 768], P('dp', None, 'mp'), may hold values from -6 to 6
Outputs:
- result: bfloat16 [48, 2048, 768], P('dp', None, 'mp')
- tokens_grad: bfloat16 [48, 2048, 768], P('dp', None, 'mp')
- attention_grad: float32 [3, 768, 768], P(None, 'dp', 'mp')
- mixing_grad: float32 [768, 768], P('mp', 'dp')
- expand_grad: float32 [768, 3072], P('dp', 'mp')
- contract_grad: float32 [3072, 768], P('mp', 'dp')
- prenorm_grad: float32 [768], P('dp')
- midnorm_grad: float32 [768], P('dp')
- router_grad: float32 [768], P('dp')
The draws below stay inside these ranges and needn't reach their ends.
Inputs may be any that keep to these rules, and one draw needn't show every extreme that they name: `chosen`: in each row the 256 entries are distinct positions in increasing order.
All inputs are finite; a program needn't handle non-finite values. No bound on the sum of `present` on one device may be relied on, other than what follows from the above.
Results may differ from the reference program's by a relative error of at most 0.017.
Values may be sent and summed in bfloat16 or wider, within the bound.
No kernel may reach another device: no remote copies, remote signals or barrier semaphores. Data moves between devices by JAX's collectives and lax.ppermute only.
A program may use at most 192 MiB of HBM per device.

```python
import math
import jax
import jax.numpy as jnp
import numpy as np
from jax import lax

D = 768
HD = 64
FF = 3072
SEQ = 2048
SEL = 256
DOCS = 4
ROWS = 48


def draw_chosen(key, part):
    key = jax.random.fold_in(key, 5)
    row_keys = jax.random.split(key, ROWS)

    def one_row(row_key):
        return jnp.sort(jax.random.permutation(row_key, SEQ)[:SEL]).astype(jnp.int32)
    return jax.vmap(one_row)(row_keys)


def plant(values, key, low, high):
    shape = values.shape
    spot = [jax.random.randint(jax.random.fold_in(key, axis), (), 0, shape[axis]) for axis in range(len(shape))]
    values = values.at[tuple(spot)].set(low)
    longest = shape.index(max(shape))
    spot[longest] = (spot[longest] + 1) % shape[longest]
    return values.at[tuple(spot)].set(high)


def raised(values, rng, source, target, blocks, factor):
    def block_of(dim):
        return (jnp.arange(values.shape[dim]) // (values.shape[dim] // blocks)).reshape((-1,) + (1,) * (values.ndim - 1 - dim))

    first = jax.random.permutation(rng, blocks)[block_of(target)]
    second = (block_of(target) + blocks // 2) % blocks
    return jnp.where((block_of(source) == first) | (block_of(source) == second), factor * values, values)


def block_scale(rng, dims, pieces, low, top_value):
    factor_of = 1.0
    for axis_at, parts in pieces:
        steps = jax.random.uniform(jax.random.fold_in(jax.random.fold_in(rng, 6), axis_at), (parts,), jnp.float32, low / len(pieces), top_value / len(pieces))
        factor_of = factor_of * jnp.repeat(jnp.exp(steps), dims[axis_at] // parts).reshape((-1,) + (1,) * (len(dims) - 1 - axis_at))
    return factor_of


def profile(number_of, total, most, skew):
    portions = [(1 << 20) // math.isqrt(grade ** skew) + 1 for grade in range(2, number_of + 1)]
    rest, holding = total - most - (number_of - 1), [1] * (number_of - 1)
    while rest > 0:
        free = [i for i in range(number_of - 1) if holding[i] < most]
        whole, budget = sum([portions[i] for i in free]), rest
        for i in free:
            extra = min(most - holding[i], max(1, budget * portions[i] // whole), rest)
            holding[i] = holding[i] + extra
            rest = rest - extra
    return np.array([most] + holding)


def uneven(own_key, amount, total, bound, skew):
    if amount == 2:
        one = jax.random.randint(own_key, (), max(1, total - bound), min(bound, total - 1) + 1)
        return jnp.stack([one, total - one])
    tallies = jnp.asarray(profile(amount, total, bound, skew), jnp.int32)
    twos = (amount - 1) // 2
    source_of, sink = tallies[1:1 + 2 * twos:2], tallies[2:2 + 2 * twos:2]
    margin = jnp.minimum(source_of - 1, bound - sink)
    passed = jax.random.randint(jax.random.fold_in(own_key, 1), (twos,), 0, 1 << 20) % (margin + 1)
    tallies = tallies.at[1:1 + 2 * twos:2].set(source_of - passed).at[2:2 + 2 * twos:2].set(sink + passed)
    return tallies[jax.random.permutation(jax.random.fold_in(own_key, 2), amount)]


def bell_draw(stream_key, dims, scale, limit, cuts=(), held_as=jnp.bfloat16):
    loudness = block_scale(stream_key, dims, cuts, -0.22, 0.18) if cuts else 1.0
    values = jax.random.normal(stream_key, dims, jnp.float32) * scale * loudness
    return jnp.minimum(jnp.maximum(values, -limit), limit).astype(held_as)


def heavy_noise(stream_key, shape, scale, most, shards, heavy, held_as=jnp.bfloat16):
    entries = scale * jax.random.normal(stream_key, shape, jnp.float32)
    if shards:
        entries = entries * block_scale(stream_key, shape, shards, -0.22, 0.18)
    return jnp.clip(raised(entries, jax.random.fold_in(stream_key, 3), *heavy), -most, most).astype(held_as)


def setup_inputs(seed: int = 0) -> dict:
    splits = jax.random.split(jax.random.key(seed), 13)
    return {
        "tokens": bell_draw(splits[0], (ROWS, SEQ, D), 1.0, 6.0, ((0, 16), (2, 2))),
        "segments": jax.vmap(lambda own: jnp.searchsorted(jnp.cumsum(uneven(own, DOCS, SEQ, SEQ // 2, 0)), jnp.arange(SEQ), side="right"))(jax.random.split(splits[1], ROWS)).reshape((ROWS, SEQ)).astype(jnp.int32),
        "present": plant((jax.random.randint(splits[2], (ROWS, SEQ), 0, 8) < 7).astype(jnp.int32), jax.random.fold_in(splits[2], 1), 0, 1),
        "chosen": draw_chosen(jax.random.fold_in(splits[12], 71), 0),
        "attention": bell_draw(splits[4], (3, D, D), D ** -0.5, 0.21875, ((1, 16), (2, 2))),
        "mixing": bell_draw(splits[5], (D, D), (D // 16) ** -0.5, 0.875, ((0, 2), (1, 16))),
        "expand": bell_draw(splits[6], (D, FF), D ** -0.5, 0.21875, ((0, 16), (1, 2))),
        "contract": bell_draw(splits[7], (FF, D), FF ** -0.5, 0.109375, ((0, 2), (1, 16))),
        "prenorm": jnp.clip(1.0 + 0.1 * jax.random.normal(splits[8], (D,), jnp.float32), 0.5, 1.5).astype(jnp.bfloat16),
        "midnorm": jnp.clip(1.0 + 0.1 * jax.random.normal(splits[9], (D,), jnp.float32), 0.5, 1.5).astype(jnp.bfloat16),
        "router": bell_draw(splits[10], (D,), D ** -0.5, 0.21875, ((0, 16),)),
        "cotangent": heavy_noise(splits[11], (ROWS, SEQ, D), 1.0, 6.0, ((0, 16), (2, 2)), (0, 2, 16, 2.0)),
    }


EPSILON = 1e-06
highest = lax.Precision.HIGHEST

@jax.custom_vjp
def low(v):
    return lax.optimization_barrier(v.astype(jnp.bfloat16)).astype(jnp.float32)

@jax.custom_vjp
def low_back(v):
    return v

def low_keep(v):
    return (low(v), None)

def low_pass(kept, grad):
    return (grad,)

def back_keep(v):
    return (v, None)

def back_low(kept, grad):
    return (low(grad),)
low.defvjp(low_keep, low_pass)
low_back.defvjp(back_keep, back_low)

def normalize(values, scales):
    return values * lax.rsqrt(lax.optimization_barrier(jnp.mean(values * values, axis=-1, keepdims=True)) + EPSILON) * scales

def allowed_pairs(seg_rows, keep_rows):
    length = seg_rows.shape[-1]
    slot_ids = jnp.arange(length)
    diagonal = slot_ids[None, :] == slot_ids[:, None]
    causal = slot_ids[None, :] <= slot_ids[:, None]
    same_doc = seg_rows[:, :, None] == seg_rows[:, None, :]
    open_key = (keep_rows[:, None, :] > 0) | diagonal[None]
    return (causal[None] & same_doc & open_key)[:, None]

def layer_block(inputs, attention, mixing, expand, contract, prenorm, midnorm, router):
    states, seg_rows, keep_rows = inputs
    row_count, length, width = states.shape
    heads_all = width // HD
    normed = low(normalize(states, prenorm))
    packed = low_back(low(jnp.einsum('btd,cde->cbte', normed, attention, precision=highest)))
    shaped = packed.reshape(3, row_count, length, heads_all, HD)
    queries, key_rows, val_rows = (shaped[0], shaped[1], shaped[2])
    scores = low_back(jnp.einsum('bqhd,bkhd->bhqk', queries, key_rows, precision=highest) * HD ** (-0.5))
    permitted = allowed_pairs(seg_rows, keep_rows)
    scores = jnp.where(permitted, scores, -1e+30)
    row_max = lax.optimization_barrier(jnp.max(scores, axis=-1, keepdims=True))
    exponent = jnp.exp(scores - row_max)
    attn_weights = low(exponent / lax.optimization_barrier(jnp.sum(exponent, axis=-1, keepdims=True)))
    context = jnp.einsum('bhqk,bkhd->bqhd', attn_weights, val_rows, precision=highest)
    context = low_back(low(context.reshape(row_count, length, width)))
    attended = low_back(jnp.einsum('btd,de->bte', context, mixing, precision=highest))
    middle = states + attended
    normed_mid = low(normalize(middle, midnorm))
    hidden = low_back(jnp.einsum('btd,df->btf', normed_mid, expand, precision=highest))
    activated = low(jax.nn.gelu(hidden, approximate=True))
    feedfwd = low_back(jnp.einsum('btf,fd->btd', activated, contract, precision=highest))
    gate_value = jax.nn.sigmoid(jnp.einsum('btd,d->bt', states, router, precision=highest)) * keep_rows
    return states + gate_value[..., None] * (attended + feedfwd)

def reference(tokens, segments, present, chosen, attention, mixing, expand, contract, prenorm, midnorm, router, cotangent):
    row_ids = jnp.arange(ROWS)[:, None]
    picked = tokens[row_ids, chosen].astype(jnp.float32)
    upstream = cotangent[row_ids, chosen].astype(jnp.float32)
    seg_sel = jnp.take_along_axis(segments, chosen, axis=1)
    keep_sel = jnp.take_along_axis(present, chosen, axis=1).astype(jnp.float32)
    params = tuple((weight.astype(jnp.float32) for weight in (attention, mixing, expand, contract, prenorm, midnorm, router)))
    group_rows = 16
    groups = ROWS // group_rows

    def forward(states, attn_w, mix_w, expand_w, contract_w, pre_w, mid_w, router_w):

        def one_block(inputs):
            return layer_block(inputs, attn_w, mix_w, expand_w, contract_w, pre_w, mid_w, router_w)
        blocks = lax.map(jax.checkpoint(one_block), (states.reshape(groups, group_rows, SEL, D), seg_sel.reshape(groups, group_rows, SEL), keep_sel.reshape(groups, group_rows, SEL)))
        return blocks.reshape(ROWS, SEL, D)
    finished, pullback = jax.vjp(forward, picked, *params)
    gradients = pullback(upstream)
    result = tokens.at[row_ids, chosen].set(finished.astype(jnp.bfloat16))
    tokens_grad = cotangent.at[row_ids, chosen].set(gradients[0].astype(jnp.bfloat16))
    return (result, tokens_grad, gradients[1], gradients[2], gradients[3], gradients[4], gradients[5], gradients[6], gradients[7])
```

```python
import jax
import jax.numpy as jnp
from jax import lax
from jax.sharding import PartitionSpec as P

HD = 64
EPSILON = 1e-06
BF = jnp.bfloat16
F32 = jnp.float32


def normalize(values, scales):
    return values * lax.rsqrt(jnp.mean(values * values, axis=-1, keepdims=True) + EPSILON) * scales


def gelu_tanh(values):
    return jax.nn.gelu(values, approximate=True)


def allowed_pairs(seg_rows, keep_rows):
    length = seg_rows.shape[-1]
    slot_ids = jnp.arange(length)
    diagonal = slot_ids[None, :] == slot_ids[:, None]
    causal = slot_ids[None, :] <= slot_ids[:, None]
    same_doc = seg_rows[:, :, None] == seg_rows[:, None, :]
    open_key = (keep_rows[:, None, :] > 0) | diagonal[None]
    return (causal[None] & same_doc & open_key)[:, None]


class Line:
    def __init__(self, count, stride, size):
        self.count, self.stride, self.size = count, stride, size
        self.pos = (lax.axis_index("dp") // stride) % size

    def pairs(self, step):
        return [
            (i, i + step * self.stride)
            for i in range(self.count)
            if 0 <= (i // self.stride) % self.size + step < self.size
        ]

    def swap(self, value):
        return lax.ppermute(value, "dp", self.pairs(1) + self.pairs(-1))

    def gather(self, own):
        if self.size == 1:
            return own[None]
        if self.size == 2:
            other = self.swap(own)
            first = self.pos == 0
            return jnp.stack([jnp.where(first, own, other), jnp.where(first, other, own)])
        lower, upper, right, left = [], [], own, own
        for _ in range(self.size - 1):
            right = lax.ppermute(right, "dp", self.pairs(1))
            left = lax.ppermute(left, "dp", self.pairs(-1))
            lower.insert(0, right)
            upper.append(left)
        stack = jnp.stack(lower + [own] + upper)
        return lax.dynamic_slice_in_dim(stack, self.size - 1 - self.pos, self.size, 0)

    def scatter(self, value):
        def at(index):
            return lax.dynamic_index_in_dim(value, index, 0, keepdims=False)

        mine = at(self.pos)
        if self.size == 1:
            return mine
        if self.size == 2:
            return mine + self.swap(at(1 - self.pos).astype(BF)).astype(F32)
        right = left = None
        for away in range(self.size - 1, 0, -1):
            to_right = at(jnp.minimum(self.pos + away, self.size - 1))
            to_left = at(jnp.maximum(self.pos - away, 0))
            if right is not None:
                to_right = to_right + right
                to_left = to_left + left
            right = lax.ppermute(to_right.astype(BF), "dp", self.pairs(1)).astype(F32)
            left = lax.ppermute(to_left.astype(BF), "dp", self.pairs(-1)).astype(F32)
        return mine + right + left


def lines_of(count):
    bits = count.bit_length() - 1
    short = 2 ** (bits // 3) if count == 2**bits else 1
    return (
        Line(count, short * short, count // (short * short)),
        Line(count, short, short),
        Line(count, 1, short),
    )


def halves(width):
    return width // 2 // 128 * 128


def gather_weights(lines, own):
    along_z, along_y, along_x = lines
    rows, width = own.shape
    cut = halves(width)
    column = along_z.gather(own)
    first = along_y.gather(along_x.gather(column[..., :cut]))
    second = along_x.gather(along_y.gather(column[..., cut:]))
    first = first.transpose(2, 0, 1, 3, 4).reshape(-1, cut)
    second = second.transpose(2, 1, 0, 3, 4).reshape(-1, width - cut)
    return jnp.concatenate([first, second], axis=1)


def scatter_grads(lines, total):
    along_z, along_y, along_x = lines
    width = total.shape[1]
    cut = halves(width)
    view = total.reshape(along_z.size, along_y.size, along_x.size, -1, width)
    first = along_x.scatter(along_y.scatter(view[..., :cut].transpose(1, 2, 0, 3, 4)))
    second = along_y.scatter(along_x.scatter(view[..., cut:].transpose(2, 1, 0, 3, 4)))
    return along_z.scatter(jnp.concatenate([first, second], axis=-1))


def other_core(value):
    return lax.ppermute(value, "mp", [(0, 1), (1, 0)])


def both_halves(value):
    other = other_core(value)
    low = lax.axis_index("mp") == 0
    return jnp.concatenate([jnp.where(low, value, other), jnp.where(low, other, value)], axis=-1)


def add_cores(value):
    low = value.astype(BF)
    return low.astype(F32) + other_core(low).astype(F32)


def dot(a, b, contract, out=F32):
    return lax.dot_general(a, b, ((contract[:1], contract[1:]), ((), ())), preferred_element_type=F32).astype(out)


def shards(
    tokens,
    segments,
    present,
    chosen,
    attention,
    mixing,
    expand,
    contract,
    prenorm,
    midnorm,
    router,
    cotangent,
    count,
):
    lines = lines_of(count)
    row_count, length, half_width = tokens.shape
    sel_count = chosen.shape[1]
    token_count = row_count * sel_count
    own_rows = mixing.shape[1]
    hidden_here = expand.shape[1]
    heads_here = half_width // HD
    scale = HD ** (-0.5)

    vectors = jnp.stack([prenorm, midnorm, router], axis=1)
    vectors = jnp.pad(vectors, ((0, 0), (0, 125)))
    first_own = jnp.concatenate(
        [attention[0], attention[1], attention[2], mixing.T, vectors], axis=1
    )
    first = gather_weights(lines, first_own)
    full_up = gather_weights(lines, expand)
    full_down = gather_weights(lines, contract.T)
    full_in = first[:, : 3 * half_width]
    full_mix = first[:, 3 * half_width : 4 * half_width]
    gains = first[:, 4 * half_width : 4 * half_width + 3].astype(F32)
    pre_scale, mid_scale, router_vec = gains[:, 0], gains[:, 1], gains[:, 2]

    positions = jnp.arange(length, dtype=jnp.int32)
    hit = chosen[:, :, None] == positions[None, None, :]
    one_hot = hit.astype(BF)
    local_rows = jnp.einsum("bts,bsd->btd", one_hot, tokens, preferred_element_type=F32).astype(BF)
    local_grads = jnp.einsum("bts,bsd->btd", one_hot, cotangent, preferred_element_type=F32).astype(BF)
    seg_sel = jnp.sum(jnp.where(hit, segments[:, None, :], 0), axis=-1)
    keep_sel = jnp.sum(jnp.where(hit, present[:, None, :], 0), axis=-1).astype(F32)

    both = both_halves(jnp.stack([local_rows, local_grads]))
    states_flat = both[0].reshape(token_count, -1)
    states = states_flat.astype(F32)
    upstream = both[1].reshape(token_count, -1).astype(F32)
    keep_flat = keep_sel.reshape(token_count)
    permitted = allowed_pairs(seg_sel, keep_sel)

    normed = normalize(states, pre_scale).astype(BF)
    packed = dot(normed, full_in, (1, 0), BF)
    shaped = packed.reshape(row_count, sel_count, 3, heads_here, HD)
    queries, key_rows, val_rows = (shaped[:, :, 0], shaped[:, :, 1], shaped[:, :, 2])
    scores = jnp.einsum("bqhd,bkhd->bhqk", queries, key_rows, preferred_element_type=F32) * scale
    scores = jnp.where(permitted, scores, -1e30)
    row_max = jnp.max(scores, axis=-1, keepdims=True)
    exponent = jnp.exp(scores - row_max)
    attn_probs = exponent / jnp.sum(exponent, axis=-1, keepdims=True)
    attn_weights = attn_probs.astype(BF)
    context = jnp.einsum("bhqk,bkhd->bqhd", attn_weights, val_rows, preferred_element_type=F32)
    context = context.astype(BF).reshape(token_count, half_width)
    attended = add_cores(dot(context, full_mix, (1, 1)))
    middle = states + attended
    normed_mid = normalize(middle, mid_scale).astype(BF)
    hidden = dot(normed_mid, full_up, (1, 0))
    activated = gelu_tanh(hidden).astype(BF)
    feedfwd = add_cores(dot(activated, full_down, (1, 1)))
    branch = attended + feedfwd
    router_prob = jax.nn.sigmoid(jnp.sum(states * router_vec, axis=-1))
    gate_value = router_prob * keep_flat
    finished = states + gate_value[:, None] * branch

    gate_grad = jnp.sum(upstream * branch, axis=-1)
    logit_grad = gate_grad * keep_flat * router_prob * (1.0 - router_prob)
    router_grad = jnp.sum(logit_grad[:, None] * states, axis=0)
    branch_grad = gate_value[:, None] * upstream
    feed_grad = branch_grad.astype(BF)
    down_out = scatter_grads(lines, dot(feed_grad, activated, (0, 0)))
    act_grad = dot(feed_grad, full_down, (1, 0))
    _, gelu_pull = jax.vjp(gelu_tanh, hidden)
    hidden_grad = gelu_pull(act_grad)[0].astype(BF)
    up_out = scatter_grads(lines, dot(normed_mid, hidden_grad, (0, 0)))
    mid_in_grad = add_cores(dot(hidden_grad, full_up, (1, 1)))
    _, mid_pull = jax.vjp(normalize, middle, mid_scale)
    middle_grad, midnorm_grad = mid_pull(mid_in_grad)
    mixed_grad = (branch_grad + middle_grad).astype(BF)
    mixing_grad = dot(mixed_grad, context, (0, 0))
    context_grad = dot(mixed_grad, full_mix, (1, 0), BF)
    context_grad = context_grad.reshape(row_count, sel_count, heads_here, HD)
    prob_grad = jnp.einsum("bqhd,bkhd->bhqk", context_grad, val_rows, preferred_element_type=F32)
    centre = jnp.sum(attn_probs * prob_grad, axis=-1, keepdims=True)
    score_grad = (attn_probs * (prob_grad - centre)).astype(BF)
    query_grad = jnp.einsum("bhqk,bkhd->bqhd", score_grad, key_rows, preferred_element_type=F32) * scale
    key_grad = jnp.einsum("bhqk,bqhd->bkhd", score_grad, queries, preferred_element_type=F32) * scale
    value_grad = jnp.einsum("bhqk,bqhd->bkhd", attn_weights, context_grad, preferred_element_type=F32)
    packed_grad = jnp.concatenate(
        [v.astype(BF).reshape(token_count, half_width) for v in (query_grad, key_grad, value_grad)],
        axis=1,
    )
    attention_grad = dot(normed, packed_grad, (0, 0))
    pre_in_grad = add_cores(dot(packed_grad, full_in, (1, 1)))
    _, pre_pull = jax.vjp(normalize, states, pre_scale)
    states_grad, prenorm_grad = pre_pull(pre_in_grad)
    total_grad = upstream + logit_grad[:, None] * router_vec + middle_grad + states_grad

    vector_grads = jnp.stack([prenorm_grad, midnorm_grad, router_grad], axis=1)
    vector_grads = jnp.pad(vector_grads, ((0, 0), (0, 125)))
    first_out = scatter_grads(
        lines, jnp.concatenate([attention_grad, mixing_grad, vector_grads], axis=1)
    )

    offset = lax.axis_index("mp") * half_width

    def put(base, values):
        mine = lax.dynamic_slice_in_dim(values, offset, half_width, 1).astype(BF)
        mine = mine.reshape(row_count, sel_count, half_width)
        placed = jnp.einsum("bts,btd->bsd", one_hot, mine, preferred_element_type=F32).astype(BF)
        return jnp.where(jnp.any(hit, axis=1)[:, :, None], placed, base)

    attention_out = first_out[:, : 3 * half_width].reshape(own_rows, 3, half_width).transpose(1, 0, 2)
    vector_out = first_out[:, 4 * half_width : 4 * half_width + 3]
    return (
        put(tokens, finished),
        put(cotangent, total_grad),
        attention_out,
        first_out[:, 3 * half_width : 4 * half_width].T,
        up_out,
        down_out.T,
        vector_out[:, 0],
        vector_out[:, 1],
        vector_out[:, 2],
    )


def solution(mesh):
    in_specs = (
        P("dp", None, "mp"),
        P("dp", None),
        P("dp", None),
        P("dp", None),
        P(None, "dp", "mp"),
        P("mp", "dp"),
        P("dp", "mp"),
        P("mp", "dp"),
        P("dp"),
        P("dp"),
        P("dp"),
        P("dp", None, "mp"),
    )
    out_specs = (
        P("dp", None, "mp"),
        P("dp", None, "mp"),
        P(None, "dp", "mp"),
        P("mp", "dp"),
        P("dp", "mp"),
        P("mp", "dp"),
        P("dp"),
        P("dp"),
        P("dp"),
    )
    count = mesh.shape["dp"]

    def body(*args):
        return shards(*args, count)

    return jax.shard_map(body, mesh=mesh, in_specs=in_specs, out_specs=out_specs, check_vma=False)
```

```python
import jax
import jax.numpy as jnp
from jax import lax
from jax.experimental import pallas as pl
from jax.experimental.pallas import tpu as pltpu
from jax.sharding import PartitionSpec as P

HD = 64
EPSILON = 1e-06
BF = jnp.bfloat16
F32 = jnp.float32


def normalize(values, scales):
    return values * lax.rsqrt(jnp.mean(values * values, axis=-1, keepdims=True) + EPSILON) * scales


def gelu_tanh(values):
    return jax.nn.gelu(values, approximate=True)


def allowed_pairs(seg_rows, keep_rows):
    length = seg_rows.shape[-1]
    slot_ids = jnp.arange(length)
    diagonal = slot_ids[None, :] == slot_ids[:, None]
    causal = slot_ids[None, :] <= slot_ids[:, None]
    same_doc = seg_rows[:, :, None] == seg_rows[:, None, :]
    open_key = (keep_rows[:, None, :] > 0) | diagonal[None]
    return (causal[None] & same_doc & open_key)[:, None]


def untouched(*refs):
    pass


def tie(value, *others):
    if not others:
        return value
    anywhere = pl.BlockSpec(memory_space=pl.ANY)
    return pl.pallas_call(
        untouched,
        out_shape=jax.ShapeDtypeStruct(value.shape, value.dtype),
        in_specs=[anywhere] * (1 + len(others)),
        out_specs=anywhere,
        input_output_aliases={0: 0},
        compiler_params=pltpu.CompilerParams(vmem_limit_bytes=1 << 20),
        cost_estimate=pl.CostEstimate(flops=0, bytes_accessed=0, transcendentals=0),
    )(value, *others)


class Cube:
    def __init__(self, count):
        self.count, self.bits = count, count.bit_length() - 1
        self.index = lax.axis_index("dp").astype(jnp.uint32)
        short = self.bits // 3
        self.x, self.y = list(range(short)), list(range(short, 2 * short))
        self.z = list(range(2 * short, self.bits))

    def swap(self, value, bit):
        return lax.ppermute(value, "dp", [(i, i ^ (1 << bit)) for i in range(self.count)])

    def low(self, bit):
        return (self.index >> bit) % 2 == 0

    def double(self, value, bit):
        other, low = self.swap(value, bit), self.low(bit)
        return jnp.stack([jnp.where(low, value, other), jnp.where(low, other, value)])

    def halve(self, value, axis, bit):
        own = ((self.index >> bit) % 2).astype(jnp.int32)
        mine = lax.dynamic_index_in_dim(value, own, axis, keepdims=False)
        sent = lax.dynamic_index_in_dim(value, 1 - own, axis, keepdims=False)
        return mine + self.swap(sent.astype(BF), bit).astype(F32)


def halves(width):
    return width // 2 // 128 * 128


def gather_weights(cube, own, after=()):
    rows, width = own.shape
    cut = halves(width)
    column = tie(own, *after)
    for bit in cube.z[::-1]:
        column = cube.double(column, bit)
    marks, done = [column], []
    for part, order in ((column[..., :cut], cube.x + cube.y), (column[..., cut:], cube.y + cube.x)):
        for bit in order:
            part = cube.double(part, bit)
        axes = order[::-1] + cube.z
        bits = sorted(axes, reverse=True)
        part = part.transpose([axes.index(b) for b in bits] + [cube.bits, cube.bits + 1])
        done.append(part.reshape(-1, part.shape[-1]))
    return jnp.concatenate(done, axis=1), marks


def scatter_grads(cube, total):
    width = total.shape[1]
    cut = halves(width)
    parts = []
    for part, order in ((total[:, :cut], cube.y + cube.x), (total[:, cut:], cube.x + cube.y)):
        part = part.reshape([2] * cube.bits + [-1, part.shape[1]])
        axes = list(range(cube.bits))[::-1]
        for bit in order:
            part = cube.halve(part, axes.index(bit), bit)
            axes.remove(bit)
        parts.append(part)
    part = jnp.concatenate(parts, axis=-1)
    for bit in axes[::-1]:
        part = cube.halve(part, axes.index(bit), bit)
        axes.remove(bit)
    return part


def other_core(value):
    return lax.ppermute(value, "mp", [(0, 1), (1, 0)])


def both_halves(value):
    other = other_core(value)
    low = lax.axis_index("mp") == 0
    return jnp.concatenate([jnp.where(low, value, other), jnp.where(low, other, value)], axis=-1)


def add_cores(value):
    low = value.astype(BF)
    return low.astype(F32) + other_core(low).astype(F32)


def dot(a, b, contract, out=F32):
    return lax.dot_general(a, b, ((contract[:1], contract[1:]), ((), ())), preferred_element_type=F32).astype(out)


def shards(
    tokens,
    segments,
    present,
    chosen,
    attention,
    mixing,
    expand,
    contract,
    prenorm,
    midnorm,
    router,
    cotangent,
    count,
):
    cube = Cube(count)
    row_count, length, half_width = tokens.shape
    sel_count = chosen.shape[1]
    token_count = row_count * sel_count
    own_rows = mixing.shape[1]
    hidden_here = expand.shape[1]
    heads_here = half_width // HD
    scale = HD ** (-0.5)

    vectors = jnp.stack([prenorm, midnorm, router], axis=1)
    vectors = jnp.pad(vectors, ((0, 0), (0, 125)))
    first_own = jnp.concatenate(
        [attention[0], attention[1], attention[2], mixing.T, vectors], axis=1
    )
    first, marks = gather_weights(cube, first_own)
    full_up, marks = gather_weights(cube, expand, marks)
    full_down, marks = gather_weights(cube, contract.T, marks)
    full_in = first[:, : 3 * half_width]
    full_mix = first[:, 3 * half_width : 4 * half_width]
    gains = first[:, 4 * half_width : 4 * half_width + 3].astype(F32)
    pre_scale, mid_scale, router_vec = gains[:, 0], gains[:, 1], gains[:, 2]

    positions = jnp.arange(length, dtype=jnp.int32)
    hit = chosen[:, :, None] == positions[None, None, :]
    one_hot = hit.astype(BF)
    local_rows = jnp.einsum("bts,bsd->btd", one_hot, tokens, preferred_element_type=F32).astype(BF)
    local_grads = jnp.einsum("bts,bsd->btd", one_hot, cotangent, preferred_element_type=F32).astype(BF)
    seg_sel = jnp.sum(jnp.where(hit, segments[:, None, :], 0), axis=-1)
    keep_sel = jnp.sum(jnp.where(hit, present[:, None, :], 0), axis=-1).astype(F32)

    both = both_halves(jnp.stack([local_rows, local_grads]))
    states_flat = both[0].reshape(token_count, -1)
    states = states_flat.astype(F32)
    upstream = both[1].reshape(token_count, -1).astype(F32)
    keep_flat = keep_sel.reshape(token_count)
    permitted = allowed_pairs(seg_sel, keep_sel)

    normed = normalize(states, pre_scale).astype(BF)
    packed = dot(normed, full_in, (1, 0), BF)
    shaped = packed.reshape(row_count, sel_count, 3, heads_here, HD)
    queries, key_rows, val_rows = (shaped[:, :, 0], shaped[:, :, 1], shaped[:, :, 2])
    scores = jnp.einsum("bqhd,bkhd->bhqk", queries, key_rows, preferred_element_type=F32) * scale
    scores = jnp.where(permitted, scores, -1e30)
    row_max = jnp.max(scores, axis=-1, keepdims=True)
    exponent = jnp.exp(scores - row_max)
    attn_probs = exponent / jnp.sum(exponent, axis=-1, keepdims=True)
    attn_weights = attn_probs.astype(BF)
    context = jnp.einsum("bhqk,bkhd->bqhd", attn_weights, val_rows, preferred_element_type=F32)
    context = context.astype(BF).reshape(token_count, half_width)
    attended = add_cores(dot(context, full_mix, (1, 1)))
    middle = states + attended
    normed_mid = normalize(middle, mid_scale).astype(BF)
    hidden = dot(normed_mid, full_up, (1, 0))
    activated = gelu_tanh(hidden).astype(BF)
    feedfwd = add_cores(dot(activated, full_down, (1, 1)))
    branch = attended + feedfwd
    router_prob = jax.nn.sigmoid(jnp.sum(states * router_vec, axis=-1))
    gate_value = router_prob * keep_flat
    finished = states + gate_value[:, None] * branch

    gate_grad = jnp.sum(upstream * branch, axis=-1)
    logit_grad = gate_grad * keep_flat * router_prob * (1.0 - router_prob)
    router_grad = jnp.sum(logit_grad[:, None] * states, axis=0)
    branch_grad = gate_value[:, None] * upstream
    feed_grad = branch_grad.astype(BF)
    down_out = scatter_grads(cube, dot(feed_grad, activated, (0, 0)))
    act_grad = dot(feed_grad, full_down, (1, 0))
    _, gelu_pull = jax.vjp(gelu_tanh, hidden)
    hidden_grad = gelu_pull(act_grad)[0].astype(BF)
    up_out = scatter_grads(cube, dot(normed_mid, hidden_grad, (0, 0)))
    mid_in_grad = add_cores(dot(hidden_grad, full_up, (1, 1)))
    _, mid_pull = jax.vjp(normalize, middle, mid_scale)
    middle_grad, midnorm_grad = mid_pull(mid_in_grad)
    mixed_grad = (branch_grad + middle_grad).astype(BF)
    mixing_grad = dot(mixed_grad, context, (0, 0))
    context_grad = dot(mixed_grad, full_mix, (1, 0), BF)
    context_grad = context_grad.reshape(row_count, sel_count, heads_here, HD)
    prob_grad = jnp.einsum("bqhd,bkhd->bhqk", context_grad, val_rows, preferred_element_type=F32)
    centre = jnp.sum(attn_probs * prob_grad, axis=-1, keepdims=True)
    score_grad = (attn_probs * (prob_grad - centre)).astype(BF)
    query_grad = jnp.einsum("bhqk,bkhd->bqhd", score_grad, key_rows, preferred_element_type=F32) * scale
    key_grad = jnp.einsum("bhqk,bqhd->bkhd", score_grad, queries, preferred_element_type=F32) * scale
    value_grad = jnp.einsum("bhqk,bqhd->bkhd", attn_weights, context_grad, preferred_element_type=F32)
    packed_grad = jnp.concatenate(
        [v.astype(BF).reshape(token_count, half_width) for v in (query_grad, key_grad, value_grad)],
        axis=1,
    )
    attention_grad = dot(normed, packed_grad, (0, 0))
    pre_in_grad = add_cores(dot(packed_grad, full_in, (1, 1)))
    _, pre_pull = jax.vjp(normalize, states, pre_scale)
    states_grad, prenorm_grad = pre_pull(pre_in_grad)
    total_grad = upstream + logit_grad[:, None] * router_vec + middle_grad + states_grad

    vector_grads = jnp.stack([prenorm_grad, midnorm_grad, router_grad], axis=1)
    vector_grads = jnp.pad(vector_grads, ((0, 0), (0, 125)))
    first_out = scatter_grads(
        cube, jnp.concatenate([attention_grad, mixing_grad, vector_grads], axis=1)
    )

    offset = lax.axis_index("mp") * half_width

    def put(base, values):
        mine = lax.dynamic_slice_in_dim(values, offset, half_width, 1).astype(BF)
        mine = mine.reshape(row_count, sel_count, half_width)
        placed = jnp.einsum("bts,btd->bsd", one_hot, mine, preferred_element_type=F32).astype(BF)
        return jnp.where(jnp.any(hit, axis=1)[:, :, None], placed, base)

    attention_out = first_out[:, : 3 * half_width].reshape(own_rows, 3, half_width).transpose(1, 0, 2)
    vector_out = first_out[:, 4 * half_width : 4 * half_width + 3]
    return (
        put(tokens, finished),
        put(cotangent, total_grad),
        attention_out,
        first_out[:, 3 * half_width : 4 * half_width].T,
        up_out,
        down_out.T,
        vector_out[:, 0],
        vector_out[:, 1],
        vector_out[:, 2],
    )


def solution(mesh):
    in_specs = (
        P("dp", None, "mp"),
        P("dp", None),
        P("dp", None),
        P("dp", None),
        P(None, "dp", "mp"),
        P("mp", "dp"),
        P("dp", "mp"),
        P("mp", "dp"),
        P("dp"),
        P("dp"),
        P("dp"),
        P("dp", None, "mp"),
    )
    out_specs = (
        P("dp", None, "mp"),
        P("dp", None, "mp"),
        P(None, "dp", "mp"),
        P("mp", "dp"),
        P("dp", "mp"),
        P("mp", "dp"),
        P("dp"),
        P("dp"),
        P("dp"),
    )
    count = mesh.shape["dp"]

    def body(*args):
        return shards(*args, count)

    return jax.shard_map(body, mesh=mesh, in_specs=in_specs, out_specs=out_specs, check_vma=False)
```

```python
import functools
import math

import jax
import jax.numpy as jnp
from jax import lax
from jax.experimental import pallas as pl
from jax.experimental.pallas import tpu as pltpu
from jax.sharding import PartitionSpec as P

HD = 64
EPSILON = 1e-06
BF = jnp.bfloat16
F32 = jnp.float32
VMEM_SPARE = 6 << 20


def mm(a, b):
    return jnp.dot(a, b, preferred_element_type=F32)


def mm_nt(a, b):
    return lax.dot_general(a, b, (((1,), (1,)), ((), ())), preferred_element_type=F32)


def mm_tn(a, b):
    return lax.dot_general(a, b, (((0,), (0,)), ((), ())), preferred_element_type=F32)


def inverse_rms(values):
    return lax.rsqrt(jnp.mean(values * values, axis=-1, keepdims=True) + EPSILON)


def call(kernel, outs, args, after=(), flops=0, name=None):
    moved = sum(v.size * v.dtype.itemsize for v in (*args, *outs))

    def body(*refs):
        kernel(*refs[: len(args)], *refs[len(args) + len(after) :])

    return pl.pallas_call(
        body,
        out_shape=outs,
        in_specs=[pl.BlockSpec(memory_space=pltpu.VMEM)] * len(args)
        + [pl.BlockSpec(memory_space=pl.ANY)] * len(after),
        out_specs=[pl.BlockSpec(memory_space=pltpu.VMEM)] * len(outs),
        compiler_params=pltpu.CompilerParams(vmem_limit_bytes=moved + VMEM_SPARE),
        cost_estimate=pl.CostEstimate(flops=flops, bytes_accessed=moved, transcendentals=0),
        name=name,
    )(*args, *after)


def shape(dims, dtype=BF):
    return jax.ShapeDtypeStruct(tuple(dims), dtype)


def first_head(width=2 * HD):
    return lax.broadcasted_iota(jnp.int32, (1, width), 1) < HD


def attention_forward(rows, sel, states_ref, weights_ref, bias_ref, normed_ref, packed_ref, probs_ref, context_ref, gains_ref):
    width = states_ref.shape[1]
    half = context_ref.shape[1]
    gains_ref[...] = weights_ref[:, 3 * half :].astype(F32).T[:8]
    gain = gains_ref[0:1, :]
    scale = HD ** (-0.5)

    @pl.loop(0, rows)
    def _(row):
        here = pl.ds(pl.multiple_of(row * sel, sel), sel)
        states = states_ref[here, :].astype(F32)
        normed = (states * inverse_rms(states) * gain).astype(BF)
        normed_ref[here, :] = normed
        packed_ref[here, :] = mm(normed, weights_ref[:, : 3 * half]).astype(BF)
        bias = bias_ref[row]
        first = first_head()
        for pair in range(half // (2 * HD)):
            at = pair * 2 * HD
            queries = packed_ref[here, at : at + 2 * HD]
            keys = packed_ref[here, half + at : half + at + 2 * HD]
            vals = packed_ref[here, 2 * half + at : 2 * half + at + 2 * HD]
            found = []
            for head in range(2):
                mine = first if head == 0 else ~first
                scores = mm_nt(jnp.where(mine, queries, jnp.zeros_like(queries)), keys) * scale + bias
                exponent = jnp.exp(scores - jnp.max(scores, axis=-1, keepdims=True))
                probs = exponent / jnp.sum(exponent, axis=-1, keepdims=True)
                probs_ref[row, 2 * pair + head] = probs
                found.append(mm(probs.astype(BF), vals))
            context_ref[here, at : at + 2 * HD] = jnp.where(first, found[0], found[1]).astype(BF)


def mix_forward(context_ref, mix_ref, out_ref):
    out_ref[...] = mm_nt(context_ref[...], mix_ref[...]).astype(BF)


def up_forward(
    rows, sel, states_ref, upstream_ref, own_ref, other_ref, up_ref, gains_ref, keep_ref,
    normed_ref, activated_ref, slope_ref, feed_grad_ref, grad_ref,
):
    mid_gain, router = gains_ref[1:2, :], gains_ref[2:3, :]
    c, a = (2.0 / math.pi) ** 0.5, 0.044715

    @pl.loop(0, rows)
    def _(row):
        here = pl.ds(pl.multiple_of(row * sel, sel), sel)
        states = states_ref[here, :].astype(F32)
        prob = jax.nn.sigmoid(jnp.sum(states * router, axis=-1, keepdims=True))
        gate = prob * keep_ref[here, :]
        feed_grad_ref[here, :] = (gate * upstream_ref[here, :].astype(F32)).astype(BF)
        middle = states + (own_ref[here, :].astype(F32) + other_ref[here, :].astype(F32))
        normed = (middle * inverse_rms(middle) * mid_gain).astype(BF)
        normed_ref[here, :] = normed
        chunk = 512
        for at in range(0, up_ref.shape[1], chunk):
            hidden = mm(normed, up_ref[:, at : at + chunk])
            square = hidden * hidden
            bent = jnp.tanh(c * hidden * (1.0 + a * square))
            activated_ref[here, at : at + chunk] = (0.5 * hidden * (1.0 + bent)).astype(BF)
            slope = 0.5 * (1.0 + bent) + 0.5 * c * hidden * (1.0 - bent * bent) * (1.0 + 3.0 * a * square)
            slope_ref[here, at : at + chunk] = slope.astype(BF)

    tall = 256
    for at in range(0, grad_ref.shape[0], tall):
        grad_ref[at : at + tall, :] = mm_tn(feed_grad_ref[:, at : at + tall], activated_ref[...]).astype(BF)


def down_backward(rows, sel, feed_grad_ref, down_ref, slope_ref, up_ref, hidden_grad_ref, out_ref):
    @pl.loop(0, rows)
    def _(row):
        here = pl.ds(pl.multiple_of(row * sel, sel), sel)
        feed_grad = feed_grad_ref[here, :]
        chunk = 512
        for at in range(0, down_ref.shape[1], chunk):
            act_grad = mm(feed_grad, down_ref[:, at : at + chunk])
            hidden_grad_ref[here, at : at + chunk] = (
                act_grad * slope_ref[here, at : at + chunk].astype(F32)
            ).astype(BF)
        out_ref[here, :] = mm_nt(hidden_grad_ref[here, :], up_ref[...]).astype(BF)


def down_forward(normed_ref, hidden_grad_ref, activated_ref, down_ref, grad_ref, out_ref):
    tall = 256
    for at in range(0, grad_ref.shape[0], tall):
        grad_ref[at : at + tall, :] = mm_tn(normed_ref[:, at : at + tall], hidden_grad_ref[...]).astype(BF)
    for at in range(0, out_ref.shape[0], tall):
        out_ref[at : at + tall, :] = mm_nt(activated_ref[at : at + tall, :], down_ref[...]).astype(BF)


def norm_backward(values, grads, gain):
    rho = inverse_rms(values)
    unit = values * rho
    scaled = grads * gain
    back = rho * (scaled - unit * jnp.mean(scaled * unit, axis=-1, keepdims=True))
    return back, jnp.sum(grads * unit, axis=0, keepdims=True)


def attention_backward(
    rows, sel, states_ref, own_ref, other_ref, mid_own_ref, mid_other_ref, upstream_ref, keep_ref, gains_ref,
    mix_ref, weights_ref, packed_ref, probs_ref,
    mixed_ref, packed_grad_ref, out_ref, middle_grad_ref, gain_grad_ref,
):
    mid_gain, router = gains_ref[1:2, :], gains_ref[2:3, :]
    half = mix_ref.shape[1]
    scale = HD ** (-0.5)
    gain_grad_ref[...] = jnp.zeros_like(gain_grad_ref)

    @pl.loop(0, rows)
    def _(row):
        here = pl.ds(pl.multiple_of(row * sel, sel), sel)
        states = states_ref[here, :].astype(F32)
        middle = states + (own_ref[here, :].astype(F32) + other_ref[here, :].astype(F32))
        mid_in = mid_own_ref[here, :].astype(F32) + mid_other_ref[here, :].astype(F32)
        middle_grad, gain_grad = norm_backward(middle, mid_in, mid_gain)
        gain_grad_ref[0:1, :] += gain_grad
        middle_grad_ref[here, :] = middle_grad
        gate = jax.nn.sigmoid(jnp.sum(states * router, axis=-1, keepdims=True)) * keep_ref[here, :]
        mixed = (gate * upstream_ref[here, :].astype(F32) + middle_grad).astype(BF)
        mixed_ref[here, :] = mixed
        context_grad = mm(mixed, mix_ref[...]).astype(BF)
        first = first_head()
        for pair in range(half // (2 * HD)):
            at = pair * 2 * HD
            queries = packed_ref[here, at : at + 2 * HD]
            keys = packed_ref[here, half + at : half + at + 2 * HD]
            vals = packed_ref[here, 2 * half + at : 2 * half + at + 2 * HD]
            grads = context_grad[:, at : at + 2 * HD]
            by_query, by_key, by_value = [], [], []
            for head in range(2):
                mine = first if head == 0 else ~first
                probs = probs_ref[row, 2 * pair + head]
                prob_grad = mm_nt(jnp.where(mine, grads, jnp.zeros_like(grads)), vals)
                centre = jnp.sum(probs * prob_grad, axis=-1, keepdims=True)
                score_grad = (probs * (prob_grad - centre)).astype(BF)
                by_query.append(mm(score_grad, keys))
                by_key.append(mm_tn(score_grad, queries))
                by_value.append(mm_tn(probs.astype(BF), grads))
            packed_grad_ref[here, at : at + 2 * HD] = (
                jnp.where(first, by_query[0], by_query[1]) * scale
            ).astype(BF)
            packed_grad_ref[here, half + at : half + at + 2 * HD] = (
                jnp.where(first, by_key[0], by_key[1]) * scale
            ).astype(BF)
            packed_grad_ref[here, 2 * half + at : 2 * half + at + 2 * HD] = jnp.where(
                first, by_value[0], by_value[1]
            ).astype(BF)
        out_ref[here, :] = mm_nt(packed_grad_ref[here, :], weights_ref[:, : 3 * half]).astype(BF)


def projection_grads(normed_ref, packed_grad_ref, mixed_ref, context_ref, grad_ref):
    tall = 256
    wide = packed_grad_ref.shape[1]
    for at in range(0, grad_ref.shape[0], tall):
        grad_ref[at : at + tall, :wide] = mm_tn(normed_ref[:, at : at + tall], packed_grad_ref[...]).astype(BF)
        grad_ref[at : at + tall, wide:] = mm_tn(mixed_ref[:, at : at + tall], context_ref[...]).astype(BF)


def final_forward(
    rows, sel, states_ref, upstream_ref, own_ref, other_ref, feed_own_ref, feed_other_ref, gains_ref, keep_ref,
    finished_ref, logit_grad_ref, router_grad_ref,
):
    router = gains_ref[2:3, :]
    router_grad_ref[...] = jnp.zeros_like(router_grad_ref)

    @pl.loop(0, rows)
    def _(row):
        here = pl.ds(pl.multiple_of(row * sel, sel), sel)
        states = states_ref[here, :].astype(F32)
        attended = own_ref[here, :].astype(F32) + other_ref[here, :].astype(F32)
        branch = attended + (feed_own_ref[here, :].astype(F32) + feed_other_ref[here, :].astype(F32))
        prob = jax.nn.sigmoid(jnp.sum(states * router, axis=-1, keepdims=True))
        keep = keep_ref[here, :]
        finished_ref[here, :] = (states + prob * keep * branch).astype(BF)
        gate_grad = jnp.sum(upstream_ref[here, :].astype(F32) * branch, axis=-1, keepdims=True)
        logit_grad = gate_grad * keep * prob * (1.0 - prob)
        logit_grad_ref[here, :] = logit_grad
        router_grad_ref[0:1, :] += jnp.sum(logit_grad * states, axis=0, keepdims=True)


def final_backward(
    rows, sel, states_ref, upstream_ref, middle_grad_ref, pre_own_ref, pre_other_ref, logit_grad_ref, gains_ref,
    total_ref, gain_grad_ref,
):
    pre_gain, router = gains_ref[0:1, :], gains_ref[2:3, :]
    gain_grad_ref[...] = jnp.zeros_like(gain_grad_ref)

    @pl.loop(0, rows)
    def _(row):
        here = pl.ds(pl.multiple_of(row * sel, sel), sel)
        states = states_ref[here, :].astype(F32)
        pre_in = pre_own_ref[here, :].astype(F32) + pre_other_ref[here, :].astype(F32)
        back, gain_grad = norm_backward(states, pre_in, pre_gain)
        gain_grad_ref[0:1, :] += gain_grad
        total = upstream_ref[here, :].astype(F32) + logit_grad_ref[here, :] * router
        total_ref[here, :] = (total + middle_grad_ref[here, :] + back).astype(BF)


def untouched(*refs):
    pass


def tie(value, *others):
    if not others:
        return value
    anywhere = pl.BlockSpec(memory_space=pl.ANY)
    return pl.pallas_call(
        untouched,
        out_shape=jax.ShapeDtypeStruct(value.shape, value.dtype),
        in_specs=[anywhere] * (1 + len(others)),
        out_specs=anywhere,
        input_output_aliases={0: 0},
        compiler_params=pltpu.CompilerParams(vmem_limit_bytes=1 << 20),
        cost_estimate=pl.CostEstimate(flops=0, bytes_accessed=0, transcendentals=0),
    )(value, *others)


class Cube:
    def __init__(self, count):
        self.count, self.bits = count, count.bit_length() - 1
        self.index = lax.axis_index("dp").astype(jnp.uint32)
        short = self.bits // 3
        self.x, self.y = list(range(short)), list(range(short, 2 * short))
        self.z = list(range(2 * short, self.bits))

    def swap(self, value, bit):
        return lax.ppermute(value, "dp", [(i, i ^ (1 << bit)) for i in range(self.count)])

    def low(self, bit):
        return (self.index >> bit) % 2 == 0

    def double(self, value, bit, after=()):
        other, low = tie(self.swap(value, bit), *after), self.low(bit)
        return jnp.stack([jnp.where(low, value, other), jnp.where(low, other, value)])

    def halve(self, value, axis, bit, after=()):
        own = ((self.index >> bit) % 2).astype(jnp.int32)
        mine = lax.dynamic_index_in_dim(value, own, axis, keepdims=False)
        sent = lax.dynamic_index_in_dim(value, 1 - own, axis, keepdims=False)
        return mine.astype(F32) + tie(self.swap(sent.astype(BF), bit), *after).astype(F32)


def halves(width):
    return width // 2 // 128 * 128


def gather_z(cube, own, after=()):
    column = tie(own, *after)
    for bit in cube.z[::-1]:
        column = cube.double(column, bit)
    return column


def gather_first(cube, column):
    cut = halves(column.shape[-1])
    parts = []
    for part, order in ((column[..., :cut], cube.x), (column[..., cut:], cube.y)):
        for bit in order:
            part = cube.double(part, bit)
        parts.append(part)
    return parts


def gather_second(cube, parts, after=()):
    done = []
    for part, before, order in zip(parts, (cube.x, cube.y), (cube.y, cube.x)):
        for bit in order:
            part = cube.double(part, bit, after)
        axes = order[::-1] + before[::-1] + cube.z
        bits = sorted(axes, reverse=True)
        part = part.transpose([axes.index(b) for b in bits] + [cube.bits, cube.bits + 1])
        done.append(part.reshape(-1, part.shape[-1]))
    return jnp.concatenate(done, axis=1)


def reduce_first(cube, total, after=()):
    cut = halves(total.shape[1])
    pieces = [(total[:, :cut], cube.y), (total[:, cut:], cube.x)] if cut else [(total, cube.y)]
    parts = []
    for part, order in pieces:
        part = part.reshape([2] * cube.bits + [-1, part.shape[1]])
        axes = list(range(cube.bits))[::-1]
        for bit in order:
            part = cube.halve(part, axes.index(bit), bit, after)
            axes.remove(bit)
        parts.append(part)
    return parts


def reduce_second(cube, parts, after=()):
    done = []
    for part, order, gone in zip(parts, (cube.x, cube.y), (cube.y, cube.x)):
        axes = [b for b in range(cube.bits)[::-1] if b not in gone]
        for bit in order:
            part = cube.halve(part, axes.index(bit), bit, after)
            axes.remove(bit)
        done.append(part)
    return jnp.concatenate(done, axis=-1)


def reduce_z(cube, part, after=()):
    axes = cube.z[::-1]
    for bit in cube.z:
        part = cube.halve(part, axes.index(bit), bit, after.pop(0) if after else ())
        axes.remove(bit)
    return part


def other_core(value):
    return lax.ppermute(value, "mp", [(0, 1), (1, 0)])


def both_halves(value):
    other = other_core(value)
    low = lax.axis_index("mp") == 0
    return jnp.concatenate([jnp.where(low, value, other), jnp.where(low, other, value)], axis=-1)


def shards(
    tokens,
    segments,
    present,
    chosen,
    attention,
    mixing,
    expand,
    contract,
    prenorm,
    midnorm,
    router,
    cotangent,
    count,
):
    cube = Cube(count)
    row_count, length, half_width = tokens.shape
    sel_count = chosen.shape[1]
    token_count = row_count * sel_count
    own_rows = mixing.shape[1]
    width = 2 * half_width
    hidden_here = expand.shape[1]
    heads_here = half_width // HD
    by_row = (row_count, sel_count)

    vectors = jnp.pad(jnp.stack([prenorm, midnorm, router], axis=1), ((0, 0), (0, 125)))
    first_own = jnp.concatenate([attention[0], attention[1], attention[2], vectors], axis=1)
    second_own = jnp.concatenate([mixing.T, expand], axis=1)
    first_z = gather_z(cube, first_own)
    second_z = gather_z(cube, second_own, [first_z])
    down_z = gather_z(cube, contract.T, [second_z])
    first = gather_second(cube, gather_first(cube, first_z))
    second_parts = gather_first(cube, second_z)
    second = gather_second(cube, second_parts)
    mix, up = second[:, :half_width], second[:, half_width:]
    down_parts = gather_first(cube, down_z)

    positions = jnp.arange(length, dtype=jnp.int32)
    hit = chosen[:, :, None] == positions[None, None, :]
    one_hot = hit.astype(BF)
    local_rows = jnp.einsum("bts,bsd->btd", one_hot, tokens, preferred_element_type=F32).astype(BF)
    local_grads = jnp.einsum("bts,bsd->btd", one_hot, cotangent, preferred_element_type=F32).astype(BF)
    seg_sel = jnp.sum(jnp.where(hit, segments[:, None, :], 0), axis=-1)
    keep_sel = jnp.sum(jnp.where(hit, present[:, None, :], 0), axis=-1).astype(F32)
    taken = jnp.any(hit, axis=1)[:, :, None]

    both = both_halves(jnp.stack([local_rows, local_grads]))
    states = both[0].reshape(token_count, width)
    upstream = both[1].reshape(token_count, width)
    keep = keep_sel.reshape(token_count, 1)
    slots = jnp.arange(sel_count)
    diagonal = slots[None, :] == slots[:, None]
    causal = slots[None, :] <= slots[:, None]
    same_doc = seg_sel[:, :, None] == seg_sel[:, None, :]
    open_key = (keep_sel[:, None, :] > 0) | diagonal[None]
    bias = jnp.where(causal[None] & same_doc & open_key, 0.0, -1e30).astype(F32)

    wide = shape((token_count, width))
    tall = shape((token_count, hidden_here))
    vector = shape((8, width), F32)
    normed, packed, probs, context, gains = call(
        functools.partial(attention_forward, *by_row),
        (
            wide,
            shape((token_count, 3 * half_width)),
            shape((row_count, heads_here, sel_count, sel_count), F32),
            shape((token_count, half_width)),
            vector,
        ),
        (states, first, bias),
        after=second_parts,
        flops=token_count * width * half_width * 6,
        name="attention_forward",
    )
    (att_own,) = call(
        mix_forward, (wide,), (context, mix), flops=2 * token_count * width * half_width, name="mix_forward"
    )
    att_other = other_core(att_own)
    normed_mid, activated, slope, feed_grad, down_grad = call(
        functools.partial(up_forward, *by_row),
        (wide, tall, tall, wide, shape((width, hidden_here))),
        (states, upstream, att_own, att_other, up, gains, keep),
        flops=4 * token_count * width * hidden_here,
        name="up_forward",
    )
    down = gather_second(cube, down_parts, [activated])

    hidden_grad, mid_own = call(
        functools.partial(down_backward, *by_row),
        (tall, wide),
        (feed_grad, down, slope, up),
        flops=4 * token_count * width * hidden_here,
        name="down_backward",
    )
    up_grad, feed_own = call(
        down_forward,
        (shape((width, hidden_here)), wide),
        (normed_mid, hidden_grad, activated, down),
        flops=4 * token_count * width * hidden_here,
        name="down_forward",
    )
    feed_other = other_core(feed_own)
    mid_other = tie(other_core(mid_own), feed_own)
    down_grads = reduce_first(cube, down_grad, [feed_own])

    mixed, packed_grad, pre_own, middle_grad, mid_gain_grad = call(
        functools.partial(attention_backward, *by_row),
        (
            wide,
            shape((token_count, 3 * half_width)),
            wide,
            shape((token_count, width), F32),
            vector,
        ),
        (states, att_own, att_other, mid_own, mid_other, upstream, keep, gains, mix, first, packed, probs),
        flops=10 * token_count * width * half_width,
        name="attention_backward",
    )
    down_part = reduce_second(cube, down_grads, [packed_grad])
    up_grads = reduce_first(cube, up_grad, [packed_grad])
    (first_grad,) = call(
        projection_grads,
        (shape((width, 4 * half_width)),),
        (normed, packed_grad, mixed, context),
        flops=8 * token_count * width * half_width,
        name="projection_grads",
    )
    pre_other = tie(other_core(pre_own), first_grad)
    finished, logit_grad, router_grad = call(
        functools.partial(final_forward, *by_row),
        (wide, shape((token_count, 1), F32), vector),
        (states, upstream, att_own, att_other, feed_own, feed_other, gains, keep),
        name="final_forward",
    )
    total_grad, pre_gain_grad = call(
        functools.partial(final_backward, *by_row),
        (wide, vector),
        (states, upstream, middle_grad, pre_own, pre_other, logit_grad, gains),
        name="final_backward",
    )
    up_part = reduce_second(cube, up_grads, [total_grad])
    vector_grads = jnp.concatenate([pre_gain_grad[:1], mid_gain_grad[:1], router_grad[:1]])
    vector_grads = jnp.pad(vector_grads.T, ((0, 0), (0, 125)))
    vector_half = reduce_first(cube, vector_grads)
    down_out = reduce_z(cube, down_part, [[total_grad], vector_half])
    first_grads = reduce_first(cube, first_grad, vector_half)
    vector_part = reduce_second(cube, vector_half)
    first_part = reduce_second(cube, first_grads, [vector_part])
    up_out = reduce_z(cube, up_part, [[vector_part], []])
    first_out = reduce_z(cube, jnp.concatenate([first_part, vector_part], axis=-1))

    offset = lax.axis_index("mp") * half_width

    def put(base, values):
        mine = lax.dynamic_slice_in_dim(values, offset, half_width, 1)
        mine = mine.reshape(row_count, sel_count, half_width)
        placed = jnp.einsum("bts,btd->bsd", one_hot, mine, preferred_element_type=F32).astype(BF)
        return jnp.where(taken, placed, base)

    attention_out = first_out[:, : 3 * half_width].reshape(own_rows, 3, half_width).transpose(1, 0, 2)
    vector_out = first_out[:, 4 * half_width : 4 * half_width + 3]
    return (
        put(tokens, tie(finished, *vector_half)),
        put(cotangent, total_grad),
        attention_out,
        first_out[:, 3 * half_width : 4 * half_width].T,
        up_out,
        down_out.T,
        vector_out[:, 0],
        vector_out[:, 1],
        vector_out[:, 2],
    )


def solution(mesh):
    in_specs = (
        P("dp", None, "mp"),
        P("dp", None),
        P("dp", None),
        P("dp", None),
        P(None, "dp", "mp"),
        P("mp", "dp"),
        P("dp", "mp"),
        P("mp", "dp"),
        P("dp"),
        P("dp"),
        P("dp"),
        P("dp", None, "mp"),
    )
    out_specs = (
        P("dp", None, "mp"),
        P("dp", None, "mp"),
        P(None, "dp", "mp"),
        P("mp", "dp"),
        P("dp", "mp"),
        P("mp", "dp"),
        P("dp"),
        P("dp"),
        P("dp"),
    )
    count = mesh.shape["dp"]

    def body(*args):
        return shards(*args, count)

    return jax.shard_map(body, mesh=mesh, in_specs=in_specs, out_specs=out_specs, check_vma=False)
```

```python
import functools
import math

import jax
import jax.numpy as jnp
from jax import lax
from jax.experimental import pallas as pl
from jax.experimental.pallas import tpu as pltpu
from jax.sharding import PartitionSpec as P

HD = 64
EPSILON = 1e-06
BF = jnp.bfloat16
F32 = jnp.float32
VMEM_SPARE = 10 << 20


def mm(a, b):
    return jnp.dot(a, b, preferred_element_type=F32)


def mm_nt(a, b):
    return lax.dot_general(a, b, (((1,), (1,)), ((), ())), preferred_element_type=F32)


def mm_tn(a, b):
    return lax.dot_general(a, b, (((0,), (0,)), ((), ())), preferred_element_type=F32)


def inverse_rms(values):
    return lax.rsqrt(jnp.mean(values * values, axis=-1, keepdims=True) + EPSILON)


def call(kernel, outs, args, after=(), bits=None, scratch=(), flops=0, name=None):
    moved = sum(v.size * v.dtype.itemsize for v in (*args, *outs))
    scalars = [] if bits is None else [bits]
    count = len(scalars) + len(args)

    def body(*refs):
        kernel(*refs[:count], *refs[count + len(after) :])

    return pl.pallas_call(
        body,
        out_shape=outs,
        in_specs=[pl.BlockSpec(memory_space=pltpu.SMEM)] * len(scalars)
        + [pl.BlockSpec(memory_space=pltpu.VMEM)] * len(args)
        + [pl.BlockSpec(memory_space=pl.ANY)] * len(after),
        out_specs=[pl.BlockSpec(memory_space=pltpu.VMEM)] * len(outs),
        scratch_shapes=scratch,
        compiler_params=pltpu.CompilerParams(vmem_limit_bytes=VMEM_SPARE),
        cost_estimate=pl.CostEstimate(flops=flops, bytes_accessed=moved, transcendentals=0),
        name=name,
    )(*scalars, *args, *after)


def shape(dims, dtype=BF):
    return jax.ShapeDtypeStruct(tuple(dims), dtype)


def first_head(width=2 * HD):
    return lax.broadcasted_iota(jnp.int32, (1, width), 1) < HD


def attention_forward(rows, sel, states_ref, weights_ref, bias_ref, normed_ref, packed_ref, probs_ref, context_ref, gains_ref):
    width = states_ref.shape[1]
    half = context_ref.shape[1]
    gains_ref[...] = weights_ref[:, 4 * half :].astype(F32).T[:8]
    gain = gains_ref[0:1, :]
    scale = HD ** (-0.5)

    @pl.loop(0, rows)
    def _(row):
        here = pl.ds(pl.multiple_of(row * sel, sel), sel)
        states = states_ref[here, :].astype(F32)
        normed = (states * inverse_rms(states) * gain).astype(BF)
        normed_ref[here, :] = normed
        packed_ref[here, :] = mm(normed, weights_ref[:, : 3 * half]).astype(BF)
        bias = bias_ref[row]
        first = first_head()
        for pair in range(half // (2 * HD)):
            at = pair * 2 * HD
            queries = packed_ref[here, at : at + 2 * HD]
            keys = packed_ref[here, half + at : half + at + 2 * HD]
            vals = packed_ref[here, 2 * half + at : 2 * half + at + 2 * HD]
            found = []
            for head in range(2):
                mine = first if head == 0 else ~first
                scores = mm_nt(jnp.where(mine, queries, jnp.zeros_like(queries)), keys) * scale + bias
                exponent = jnp.exp(scores - jnp.max(scores, axis=-1, keepdims=True))
                probs = exponent / jnp.sum(exponent, axis=-1, keepdims=True)
                probs_ref[row, 2 * pair + head] = probs
                found.append(mm(probs.astype(BF), vals))
            context_ref[here, at : at + 2 * HD] = jnp.where(first, found[0], found[1]).astype(BF)


def mix_forward(context_ref, mix_ref, out_ref):
    out_ref[...] = mm_nt(context_ref[...], mix_ref[...]).astype(BF)


def up_forward(
    rows, sel, states_ref, upstream_ref, own_ref, other_ref, up_ref, gains_ref, keep_ref,
    normed_ref, activated_ref, slope_ref, feed_grad_ref, grad_ref,
):
    mid_gain, router = gains_ref[1:2, :], gains_ref[2:3, :]
    c, a = (2.0 / math.pi) ** 0.5, 0.044715

    @pl.loop(0, rows)
    def _(row):
        here = pl.ds(pl.multiple_of(row * sel, sel), sel)
        states = states_ref[here, :].astype(F32)
        prob = jax.nn.sigmoid(jnp.sum(states * router, axis=-1, keepdims=True))
        gate = prob * keep_ref[here, :]
        feed_grad_ref[here, :] = (gate * upstream_ref[here, :].astype(F32)).astype(BF)
        middle = states + (own_ref[here, :].astype(F32) + other_ref[here, :].astype(F32))
        normed = (middle * inverse_rms(middle) * mid_gain).astype(BF)
        normed_ref[here, :] = normed
        chunk = 512
        for at in range(0, up_ref.shape[1], chunk):
            hidden = mm(normed, up_ref[:, at : at + chunk])
            square = hidden * hidden
            bent = jnp.tanh(c * hidden * (1.0 + a * square))
            activated_ref[here, at : at + chunk] = (0.5 * hidden * (1.0 + bent)).astype(BF)
            slope = 0.5 * (1.0 + bent) + 0.5 * c * hidden * (1.0 - bent * bent) * (1.0 + 3.0 * a * square)
            slope_ref[here, at : at + chunk] = slope.astype(BF)

    tall = 256
    for at in range(0, grad_ref.shape[0], tall):
        grad_ref[at : at + tall, :] = mm_tn(feed_grad_ref[:, at : at + tall], activated_ref[...]).astype(BF)


def down_backward(rows, sel, feed_grad_ref, down_ref, slope_ref, up_ref, hidden_grad_ref, out_ref):
    @pl.loop(0, rows)
    def _(row):
        here = pl.ds(pl.multiple_of(row * sel, sel), sel)
        feed_grad = feed_grad_ref[here, :]
        chunk = 512
        for at in range(0, down_ref.shape[1], chunk):
            act_grad = mm(feed_grad, down_ref[:, at : at + chunk])
            hidden_grad_ref[here, at : at + chunk] = (
                act_grad * slope_ref[here, at : at + chunk].astype(F32)
            ).astype(BF)
        out_ref[here, :] = mm_nt(hidden_grad_ref[here, :], up_ref[...]).astype(BF)


def down_forward(normed_ref, hidden_grad_ref, activated_ref, down_ref, grad_ref, out_ref):
    tall = 256
    for at in range(0, grad_ref.shape[0], tall):
        grad_ref[at : at + tall, :] = mm_tn(normed_ref[:, at : at + tall], hidden_grad_ref[...]).astype(BF)
    for at in range(0, out_ref.shape[0], tall):
        out_ref[at : at + tall, :] = mm_nt(activated_ref[at : at + tall, :], down_ref[...]).astype(BF)


def norm_backward(values, grads, gain):
    rho = inverse_rms(values)
    unit = values * rho
    scaled = grads * gain
    back = rho * (scaled - unit * jnp.mean(scaled * unit, axis=-1, keepdims=True))
    return back, jnp.sum(grads * unit, axis=0, keepdims=True)


def attention_backward(
    rows, sel, states_ref, own_ref, other_ref, mid_own_ref, mid_other_ref, upstream_ref, keep_ref, gains_ref,
    mix_ref, weights_ref, packed_ref, probs_ref,
    mixed_ref, packed_grad_ref, out_ref, middle_grad_ref, gain_grad_ref,
):
    mid_gain, router = gains_ref[1:2, :], gains_ref[2:3, :]
    half = mix_ref.shape[1]
    scale = HD ** (-0.5)
    gain_grad_ref[...] = jnp.zeros_like(gain_grad_ref)

    @pl.loop(0, rows)
    def _(row):
        here = pl.ds(pl.multiple_of(row * sel, sel), sel)
        states = states_ref[here, :].astype(F32)
        middle = states + (own_ref[here, :].astype(F32) + other_ref[here, :].astype(F32))
        mid_in = mid_own_ref[here, :].astype(F32) + mid_other_ref[here, :].astype(F32)
        middle_grad, gain_grad = norm_backward(middle, mid_in, mid_gain)
        gain_grad_ref[0:1, :] += gain_grad
        middle_grad_ref[here, :] = middle_grad
        gate = jax.nn.sigmoid(jnp.sum(states * router, axis=-1, keepdims=True)) * keep_ref[here, :]
        mixed = (gate * upstream_ref[here, :].astype(F32) + middle_grad).astype(BF)
        mixed_ref[here, :] = mixed
        context_grad = mm(mixed, mix_ref[...]).astype(BF)
        first = first_head()
        for pair in range(half // (2 * HD)):
            at = pair * 2 * HD
            queries = packed_ref[here, at : at + 2 * HD]
            keys = packed_ref[here, half + at : half + at + 2 * HD]
            vals = packed_ref[here, 2 * half + at : 2 * half + at + 2 * HD]
            grads = context_grad[:, at : at + 2 * HD]
            by_query, by_key, by_value = [], [], []
            for head in range(2):
                mine = first if head == 0 else ~first
                probs = probs_ref[row, 2 * pair + head]
                prob_grad = mm_nt(jnp.where(mine, grads, jnp.zeros_like(grads)), vals)
                centre = jnp.sum(probs * prob_grad, axis=-1, keepdims=True)
                score_grad = (probs * (prob_grad - centre)).astype(BF)
                by_query.append(mm(score_grad, keys))
                by_key.append(mm_tn(score_grad, queries))
                by_value.append(mm_tn(probs.astype(BF), grads))
            packed_grad_ref[here, at : at + 2 * HD] = (
                jnp.where(first, by_query[0], by_query[1]) * scale
            ).astype(BF)
            packed_grad_ref[here, half + at : half + at + 2 * HD] = (
                jnp.where(first, by_key[0], by_key[1]) * scale
            ).astype(BF)
            packed_grad_ref[here, 2 * half + at : 2 * half + at + 2 * HD] = jnp.where(
                first, by_value[0], by_value[1]
            ).astype(BF)
        out_ref[here, :] = mm_nt(packed_grad_ref[here, :], weights_ref[:, : 3 * half]).astype(BF)


def projection_grads(normed_ref, packed_grad_ref, mixed_ref, context_ref, grad_ref):
    tall = 256
    wide = packed_grad_ref.shape[1]
    for at in range(0, grad_ref.shape[0], tall):
        grad_ref[at : at + tall, :wide] = mm_tn(normed_ref[:, at : at + tall], packed_grad_ref[...]).astype(BF)
        grad_ref[at : at + tall, wide:] = mm_tn(mixed_ref[:, at : at + tall], context_ref[...]).astype(BF)


def final_forward(
    rows, sel, states_ref, upstream_ref, own_ref, other_ref, feed_own_ref, feed_other_ref, gains_ref, keep_ref,
    finished_ref, logit_grad_ref, router_grad_ref,
):
    router = gains_ref[2:3, :]
    router_grad_ref[...] = jnp.zeros_like(router_grad_ref)

    @pl.loop(0, rows)
    def _(row):
        here = pl.ds(pl.multiple_of(row * sel, sel), sel)
        states = states_ref[here, :].astype(F32)
        attended = own_ref[here, :].astype(F32) + other_ref[here, :].astype(F32)
        branch = attended + (feed_own_ref[here, :].astype(F32) + feed_other_ref[here, :].astype(F32))
        prob = jax.nn.sigmoid(jnp.sum(states * router, axis=-1, keepdims=True))
        keep = keep_ref[here, :]
        finished_ref[here, :] = (states + prob * keep * branch).astype(BF)
        gate_grad = jnp.sum(upstream_ref[here, :].astype(F32) * branch, axis=-1, keepdims=True)
        logit_grad = gate_grad * keep * prob * (1.0 - prob)
        logit_grad_ref[here, :] = logit_grad
        router_grad_ref[0:1, :] += jnp.sum(logit_grad * states, axis=0, keepdims=True)


def final_backward(
    rows, sel, states_ref, upstream_ref, middle_grad_ref, pre_own_ref, pre_other_ref, logit_grad_ref, gains_ref,
    mid_gain_grad_ref, router_grad_ref, total_ref, vectors_ref, lines_ref,
):
    pre_gain, router = gains_ref[0:1, :], gains_ref[2:3, :]
    lines_ref[...] = jnp.zeros_like(lines_ref)
    lines_ref[1:2, :] = mid_gain_grad_ref[0:1, :]
    lines_ref[2:3, :] = router_grad_ref[0:1, :]

    @pl.loop(0, rows)
    def _(row):
        here = pl.ds(pl.multiple_of(row * sel, sel), sel)
        states = states_ref[here, :].astype(F32)
        pre_in = pre_own_ref[here, :].astype(F32) + pre_other_ref[here, :].astype(F32)
        back, gain_grad = norm_backward(states, pre_in, pre_gain)
        lines_ref[0:1, :] += gain_grad
        total = upstream_ref[here, :].astype(F32) + logit_grad_ref[here, :] * router
        total_ref[here, :] = (total + middle_grad_ref[here, :] + back).astype(BF)

    vectors_ref[...] = lines_ref[...].T.astype(BF)


def upright(row):
    return jnp.broadcast_to(row, (8, row.shape[1])).T[:, :1]


def select_rows(tokens_ref, cotangent_ref, chosen_ref, segments_ref, present_ref, picked_ref, bias_ref, keep_ref):
    sel, length = picked_ref.shape[2], tokens_ref.shape[1]
    row = pl.ds(pl.program_id(0), 1)
    chosen = upright(chosen_ref[row, :].astype(F32)).astype(jnp.int32)
    hit = chosen == lax.broadcasted_iota(jnp.int32, (sel, length), 1)
    one_hot = jnp.where(hit, 1.0, 0.0).astype(BF)
    picked_ref[0, 0] = mm(one_hot, tokens_ref[0]).astype(BF)
    picked_ref[1, 0] = mm(one_hot, cotangent_ref[0]).astype(BF)
    both = jnp.concatenate(
        [segments_ref[row, :].astype(F32), present_ref[row, :].astype(F32), jnp.zeros((6, length), F32)], axis=0
    ).astype(BF)
    along = mm_nt(both, one_hot)
    down = along.T
    slot = lax.broadcasted_iota(jnp.int32, (sel, sel), 0)
    seen = lax.broadcasted_iota(jnp.int32, (sel, sel), 1)
    open_key = (along[1:2, :] > 0.5) | (slot == seen)
    permitted = (seen <= slot) & (down[:, 0:1] == along[0:1, :]) & open_key
    bias_ref[0] = jnp.where(permitted, 0.0, -1e30)
    keep_ref[...] = down[:, 1:2]


def select(tokens, cotangent, chosen, segments, present):
    rows, length, half = tokens.shape
    sel = chosen.shape[1]
    by_row = pl.BlockSpec((1, length, half), lambda row: (row, 0, 0))
    all_of = lambda v: pl.BlockSpec(v.shape, lambda row: (0, 0))
    return pl.pallas_call(
        select_rows,
        grid=(rows,),
        out_shape=(shape((2, rows, sel, half)), shape((rows, sel, sel), F32), shape((rows * sel, 1), F32)),
        in_specs=[by_row, by_row, all_of(chosen), all_of(segments), all_of(present)],
        out_specs=[
            pl.BlockSpec((2, 1, sel, half), lambda row: (0, row, 0, 0)),
            pl.BlockSpec((1, sel, sel), lambda row: (row, 0, 0)),
            pl.BlockSpec((sel, 1), lambda row: (row, 0)),
        ],
        compiler_params=pltpu.CompilerParams(vmem_limit_bytes=60 << 20),
        cost_estimate=pl.CostEstimate(
            flops=4 * rows * sel * length * half, bytes_accessed=4 * tokens.size, transcendentals=0
        ),
        name="select_rows",
    )(tokens, cotangent, chosen, segments, present)


def put_rows(bits_ref, chosen_ref, values_ref, base_ref, out_ref):
    long, half = out_ref.shape[1:]
    sel = values_ref.shape[0]
    first = pl.program_id(1) * long
    chosen = chosen_ref[pl.ds(pl.program_id(0), 1), :]
    hit = first + lax.broadcasted_iota(jnp.int32, (long, sel), 0) == chosen
    one_hot = jnp.where(hit, 1.0, 0.0).astype(BF)
    offset = pl.multiple_of(bits_ref[-1 + bits_ref.shape[0]] * half, half)
    values = values_ref[:, pl.ds(offset, half)]
    placed = mm(one_hot, jnp.concatenate([values, jnp.ones((sel, 128), BF)], axis=1))
    taken = placed[:, half:] > 0.5
    for at in range(0, half, 128):
        here = slice(at, at + 128)
        out_ref[0, :, here] = jnp.where(taken, placed[:, here].astype(BF), base_ref[0, :, here])


def put(base, chosen, values, bits, after=()):
    rows, length, half = base.shape
    sel = chosen.shape[1]
    long = length // 2

    def body(*refs):
        put_rows(*refs[:4], refs[-1])

    return pl.pallas_call(
        body,
        grid=(rows, length // long),
        out_shape=shape(base.shape),
        in_specs=[
            pl.BlockSpec(memory_space=pltpu.SMEM),
            pl.BlockSpec(chosen.shape, lambda row, part: (0, 0)),
            pl.BlockSpec((sel, values.shape[1]), lambda row, part: (row, 0)),
            pl.BlockSpec((1, long, half), lambda row, part: (row, part, 0)),
        ]
        + [pl.BlockSpec(memory_space=pl.ANY)] * len(after),
        out_specs=pl.BlockSpec((1, long, half), lambda row, part: (row, part, 0)),
        compiler_params=pltpu.CompilerParams(vmem_limit_bytes=24 << 20),
        cost_estimate=pl.CostEstimate(
            flops=2 * rows * sel * length * half, bytes_accessed=4 * base.size, transcendentals=0
        ),
        name="put_rows",
    )(bits, chosen, values, base, *after)


def first_columns(attention_ref, mixing_ref, vectors_ref, out_ref):
    half = attention_ref.shape[2]
    for k in range(3):
        out_ref[:, k * half : (k + 1) * half] = attention_ref[k]
    out_ref[:, 3 * half : 4 * half] = mixing_ref[...]
    out_ref[:, 4 * half :] = vectors_ref[...]


def second_columns(cuts, expand_ref, contract_ref, out_ref):
    at = 0
    for start, end in cuts:
        out_ref[:, at : at + end - start] = expand_ref[:, start:end]
        at += end - start
        out_ref[:, at : at + end - start] = contract_ref[:, start:end]
        at += end - start


def untouched(*refs):
    pass


def tie(value, *others):
    if not others:
        return value
    anywhere = pl.BlockSpec(memory_space=pl.ANY)
    return pl.pallas_call(
        untouched,
        out_shape=jax.ShapeDtypeStruct(value.shape, value.dtype),
        in_specs=[anywhere] * (1 + len(others)),
        out_specs=anywhere,
        input_output_aliases={0: 0},
        compiler_params=pltpu.CompilerParams(vmem_limit_bytes=1 << 20),
        cost_estimate=pl.CostEstimate(flops=0, bytes_accessed=0, transcendentals=0),
    )(value, *others)


class Cube:
    def __init__(self, count):
        self.count, self.depth = count, count.bit_length() - 1
        index = lax.axis_index("dp").astype(jnp.int32)
        self.bits = jnp.append(
            (index >> jnp.arange(self.depth)) & 1, lax.axis_index("mp").astype(jnp.int32)
        )
        short = self.depth // 3
        self.x, self.y = list(range(short)), list(range(short, 2 * short))
        self.z = list(range(2 * short, self.depth))
        self.far = self.z[1:]
        near = [self.x, self.y, self.z[:1]]
        self.orders = [sum(near[k:] + near[:k], []) for k in range(3)]

    def swap(self, value, bit):
        return lax.ppermute(value, "dp", [(i, i ^ (1 << bit)) for i in range(self.count)])


class Part:
    def __init__(self, value, bits, sent=None, start=0, width=None):
        self.value, self.bits, self.sent = value, list(bits), sent
        self.start, self.width = start, width or value.shape[2]

    def columns(self, start, end):
        return Part(self.value, self.bits, self.sent, self.start + start, end - start)


def thirds(width):
    ends = [(k * width // 3 + 64) // 128 * 128 for k in range(4)]
    return list(zip(ends, ends[1:]))


def start_exchange(cube, part, bit):
    part.sent = cube.swap(part.value, bit)
    return part


def stack_parts(plan, bits_ref, *refs):
    ins, outs = refs[: 2 * len(plan)], refs[2 * len(plan) :]
    for k, (bit, blocks) in enumerate(plan):
        mine = bits_ref[bit]
        for block in range(blocks):
            outs[k][mine, block] = ins[2 * k][block]
            outs[k][1 - mine, block] = ins[2 * k + 1][block]


def stack(cube, parts, bits, after=()):
    outs, args, plan = [], [], []
    for part, bit in zip(parts, bits):
        outs.append(shape((2,) + part.value.shape))
        args += [part.value, part.sent]
        plan.append((bit, part.value.shape[0]))
    found = call(functools.partial(stack_parts, plan), outs, args, after, cube.bits, name="stack_parts")
    return [
        Part(v.reshape((-1,) + v.shape[2:]), [bit] + part.bits) for v, part, bit in zip(found, parts, bits)
    ]


def split_columns(plan, own_ref, *out_refs):
    for ref, (start, end) in zip(out_refs, plan):
        ref[...] = own_ref[:, :, start:end]


def whole_rows(plan, bits_ref, *refs):
    ins, out_ref = refs[:-1], refs[-1]
    column = 0
    for k, (bit, places, start, width) in enumerate(plan):
        mine = bits_ref[bit]
        for block, place in enumerate(places):
            here = slice(column, column + width)
            out_ref[place + (mine << bit), :, here] = ins[2 * k][block, :, start : start + width]
            out_ref[place + ((1 - mine) << bit), :, here] = ins[2 * k + 1][block, :, start : start + width]
        column += width


def whole(cube, parts, bits, after=()):
    args, plan, width = [], [], 0
    for part, bit in zip(parts, bits):
        places = []
        for block in range(part.value.shape[0]):
            digits = [(block >> k) & 1 for k in range(len(part.bits))][::-1]
            places.append(sum(digit << b for digit, b in zip(digits, part.bits)))
        args += [part.value, part.sent]
        plan.append((bit, places, part.start, part.width))
        width += part.width
    rows = parts[0].value.shape[1]
    (found,) = call(
        functools.partial(whole_rows, plan),
        (shape((cube.count, rows, width)),),
        args,
        after,
        cube.bits,
        name="whole_rows",
    )
    return found.reshape(-1, width)


def fold_parts(plan, bits_ref, *refs):
    refs = list(refs)
    taken = [[(refs.pop(0), refs.pop(0) if sent else None) for sent, _, _ in sources] for _, _, sources in plan]
    for (bit, (high, low), sources), ins in zip(plan, taken):
        sent_ref, kept_ref = refs.pop(0), refs.pop(0)
        mine = bits_ref[bit]
        column = 0
        for (_, start, width), (value_ref, other_ref) in zip(sources, ins):
            there = slice(start, start + width)
            here = slice(column, column + width)
            for a in range(high):
                for b in range(low):
                    for index, out_ref in ((1 - mine, sent_ref), (mine, kept_ref)):
                        found = value_ref[a, index, b, :, there].astype(F32)
                        if other_ref is not None:
                            found += other_ref[a, index, b, :, there].astype(F32)
                        out_ref[a * low + b, :, here] = found.astype(out_ref.dtype)
            column += width


def fold(cube, groups, bits, after=()):
    args, outs, plan = [], [], []
    for sources, bit in zip(groups, bits):
        at = sources[0].bits.index(bit)
        high, low = 1 << at, 1 << (len(sources[0].bits) - at - 1)
        listed = []
        for part in sources:
            for value in (part.value, part.sent):
                if value is not None:
                    args.append(value.reshape((high, 2, low) + value.shape[1:]))
            listed.append((part.sent is not None, part.start, part.width))
        plan.append((bit, (high, low), listed))
        dims = (high * low, sources[0].value.shape[1], sum(p.width for p in sources))
        outs += [shape(dims), shape(dims, F32)]
    found = call(functools.partial(fold_parts, plan), outs, args, after, cube.bits, name="fold_parts")
    done = []
    for k, (sources, bit) in enumerate(zip(groups, bits)):
        left = [b for b in sources[0].bits if b != bit]
        done.append(Part(found[2 * k + 1], left, cube.swap(found[2 * k], bit)))
    return done


def cut(cube, total):
    blocks = total.reshape(cube.count, -1, total.shape[1])
    bits = list(range(cube.depth))[::-1]
    return [Part(blocks, bits, None, start, end - start) for start, end in thirds(total.shape[1]) if end > start]


def arrived(parts):
    return [p.sent for p in parts]


def sum_first(value_ref, sent_ref, attention_ref, mixing_ref, vectors_ref):
    half = attention_ref.shape[2]
    total = value_ref[0] + sent_ref[0].astype(F32)
    for k in range(3):
        attention_ref[k] = total[:, k * half : (k + 1) * half]
    mixing_ref[...] = total[:, 3 * half : 4 * half]
    vectors_ref[...] = total[:, 4 * half :].T


def sum_second(cuts, value_ref, sent_ref, expand_ref, contract_ref):
    at = 0
    for start, end in cuts:
        for side in range(2):
            width = end - start
            total = value_ref[0, :, at : at + width] + sent_ref[0, :, at : at + width].astype(F32)
            (expand_ref if side else contract_ref)[:, start:end] = total
            at += width


def other_core(value):
    return lax.ppermute(value, "mp", [(0, 1), (1, 0)])


def both_halves(value):
    other = other_core(value)
    low = lax.axis_index("mp") == 0
    return jnp.concatenate([jnp.where(low, value, other), jnp.where(low, other, value)], axis=-1)


def shards(
    tokens,
    segments,
    present,
    chosen,
    attention,
    mixing,
    expand,
    contract,
    prenorm,
    midnorm,
    router,
    cotangent,
    count,
):
    cube = Cube(count)
    row_count, length, half_width = tokens.shape
    sel_count = chosen.shape[1]
    token_count = row_count * sel_count
    own_rows = mixing.shape[1]
    width = 2 * half_width
    hidden_here = expand.shape[1]
    heads_here = half_width // HD
    by_row = (row_count, sel_count)

    vectors = jnp.pad(jnp.stack([prenorm, midnorm, router], axis=1), ((0, 0), (0, 125)))
    cuts = thirds(hidden_here)
    (first_own,) = call(
        first_columns, (shape((own_rows, 4 * half_width + 128)),), (attention, mixing.T, vectors), name="first_columns"
    )
    first_far = start_exchange(cube, Part(first_own[None], []), cube.far[-1])
    (second_own,) = call(
        functools.partial(second_columns, cuts),
        (shape((own_rows, 2 * hidden_here)),),
        (expand, contract.T),
        name="second_columns",
    )
    picked, bias, keep = select(tokens, cotangent, chosen, segments, present)

    def spread(far, after, begin=()):
        for bit in cube.far[-2::-1]:
            far = start_exchange(cube, stack(cube, [far], [far_bit(far)], after)[0], bit)
        column = stack(cube, [far], [far_bit(far)], after)[0]
        ends = thirds(column.width)
        found = call(
            functools.partial(split_columns, ends),
            [shape(column.value.shape[:2] + (end - start,)) for start, end in ends],
            [column.value],
            begin,
            name="split_columns",
        )
        return [Part(v, column.bits) for v in found]

    def far_bit(part):
        return cube.far[-1 - len(part.bits)]

    def step_bits(step):
        return [order[step] for order in cube.orders]

    def send(parts, step):
        return [start_exchange(cube, p, bit) for p, bit in zip(parts, step_bits(step))]

    steps = len(cube.orders[0])
    first_parts = spread(first_far, [picked])
    both = both_halves(tie(picked, first_parts[0].value))
    states = both[0].reshape(token_count, width)
    upstream = both[1].reshape(token_count, width)
    first_parts = send(first_parts, 0)
    second_far = start_exchange(cube, Part(tie(second_own, *arrived([first_far]))[None], []), cube.far[-1])
    for step in range(1, steps):
        after = arrived([second_far]) if step == steps - 1 else []
        first_parts = send(stack(cube, first_parts, step_bits(step - 1), after), step)
    first_last = [p.value for p in first_parts]
    first = whole(cube, first_parts, step_bits(steps - 1))
    mix = first[:, 3 * half_width : 4 * half_width]
    second_parts = send(spread(second_far, [], first_last[:1]), 0)
    second_begun = []
    for step in range(1, steps - 1):
        second_parts = stack(cube, second_parts, step_bits(step - 1), [first] if step == 1 else [])
        second_begun = second_begun or [p.value for p in second_parts]
        second_parts = send(second_parts, step)
    second_parts = stack(cube, second_parts, step_bits(steps - 2))
    each = hidden_here // 3
    up_parts, down_parts = [], []
    for p in second_parts:
        up_parts.append(Part(p.value[..., :each], p.bits))
        down_parts.append(Part(p.value[..., each:], p.bits))
    up = whole(cube, send(up_parts, steps - 1), step_bits(steps - 1))
    down_parts = send(down_parts, steps - 1)

    wide = shape((token_count, width))
    tall = shape((token_count, hidden_here))
    vector = shape((8, width), F32)
    normed, packed, probs, context, gains = call(
        functools.partial(attention_forward, *by_row),
        (
            wide,
            shape((token_count, 3 * half_width)),
            shape((row_count, heads_here, sel_count, sel_count), F32),
            shape((token_count, half_width)),
            vector,
        ),
        (states, first, bias),
        after=second_begun,
        flops=token_count * width * half_width * 6,
        name="attention_forward",
    )
    (att_own,) = call(
        mix_forward, (wide,), (context, mix), flops=2 * token_count * width * half_width, name="mix_forward"
    )
    att_other = other_core(att_own)
    normed_mid, activated, slope, feed_grad, down_grad = call(
        functools.partial(up_forward, *by_row),
        (wide, tall, tall, wide, shape((width, hidden_here))),
        (states, upstream, att_own, att_other, up, gains, keep),
        flops=4 * token_count * width * hidden_here,
        name="up_forward",
    )
    down = whole(cube, down_parts, step_bits(steps - 1), [activated])

    hidden_grad, mid_own = call(
        functools.partial(down_backward, *by_row),
        (tall, wide),
        (feed_grad, down, slope, up),
        flops=4 * token_count * width * hidden_here,
        name="down_backward",
    )
    up_grad, feed_own = call(
        down_forward,
        (shape((width, hidden_here)), wide),
        (normed_mid, hidden_grad, activated, down),
        flops=4 * token_count * width * hidden_here,
        name="down_forward",
    )
    feed_other = other_core(feed_own)
    mid_other = tie(other_core(mid_own), feed_own)

    def back_bits(step):
        return [order[-1 - step] for order in cube.orders]

    def alone(parts):
        return [[p] for p in parts]

    both_grads = [list(pair) for pair in zip(cut(cube, down_grad), cut(cube, up_grad))]
    both_grads = fold(cube, both_grads, back_bits(0))

    mixed, packed_grad, pre_own, middle_grad, mid_gain_grad = call(
        functools.partial(attention_backward, *by_row),
        (
            wide,
            shape((token_count, 3 * half_width)),
            wide,
            shape((token_count, width), F32),
            vector,
        ),
        (states, att_own, att_other, mid_own, mid_other, upstream, keep, gains, mix, first, packed, probs),
        after=[both_grads[0].value],
        flops=10 * token_count * width * half_width,
        name="attention_backward",
    )
    finished, logit_grad, router_grad = call(
        functools.partial(final_forward, *by_row),
        (wide, shape((token_count, 1), F32), vector),
        (states, upstream, att_own, att_other, feed_own, feed_other, gains, keep),
        after=[packed_grad],
        name="final_forward",
    )
    (first_grad,) = call(
        projection_grads,
        (shape((width, 4 * half_width)),),
        (normed, packed_grad, mixed, context),
        after=[finished],
        flops=8 * token_count * width * half_width,
        name="projection_grads",
    )
    both_grads = fold(cube, alone(both_grads), back_bits(1), [first_grad])
    pre_other = other_core(tie(pre_own, both_grads[0].value))
    total_grad, vector_grads = call(
        functools.partial(final_backward, *by_row),
        (wide, shape((width, 128))),
        (states, upstream, middle_grad, pre_own, pre_other, logit_grad, gains, mid_gain_grad, router_grad),
        scratch=[pltpu.VMEM((128, width), F32)],
        name="final_backward",
    )
    first_grads = alone(cut(cube, first_grad))
    first_grads[-1] += cut(cube, vector_grads)
    first_grads = fold(cube, first_grads, back_bits(0))
    result = put(tokens, chosen, finished, cube.bits, [first_grads[0].value])
    tokens_grad = put(cotangent, chosen, total_grad, cube.bits, [result])
    for step in range(2, steps):
        both_grads = fold(cube, alone(both_grads), back_bits(step), [first_grad] if step == 2 else [])
    for step in range(1, steps):
        first_grads = fold(cube, alone(first_grads), back_bits(step), [result] if step == 1 else [])
    both_grads, first_grads = [both_grads], [first_grads]
    for bit in cube.far:
        both_grads = [fold(cube, both_grads, [bit])]
        first_grads = [fold(cube, first_grads, [bit])]
    (both_grad,), (first_grad,) = both_grads[0], first_grads[0]
    up_out, down_out = call(
        functools.partial(sum_second, cuts),
        (shape((own_rows, hidden_here), F32),) * 2,
        (both_grad.value, both_grad.sent),
        name="sum_second",
    )
    attention_out, mixing_out, vector_out = call(
        sum_first,
        (
            shape((3, own_rows, half_width), F32),
            shape((own_rows, half_width), F32),
            shape((128, own_rows), F32),
        ),
        (first_grad.value, first_grad.sent),
        name="sum_first",
    )
    return (
        result,
        tokens_grad,
        attention_out,
        mixing_out.T,
        up_out,
        down_out.T,
        vector_out[0],
        vector_out[1],
        vector_out[2],
    )


def solution(mesh):
    in_specs = (
        P("dp", None, "mp"),
        P("dp", None),
        P("dp", None),
        P("dp", None),
        P(None, "dp", "mp"),
        P("mp", "dp"),
        P("dp", "mp"),
        P("mp", "dp"),
        P("dp"),
        P("dp"),
        P("dp"),
        P("dp", None, "mp"),
    )
    out_specs = (
        P("dp", None, "mp"),
        P("dp", None, "mp"),
        P(None, "dp", "mp"),
        P("mp", "dp"),
        P("dp", "mp"),
        P("mp", "dp"),
        P("dp"),
        P("dp"),
        P("dp"),
    )
    count = mesh.shape["dp"]

    def body(*args):
        return shards(*args, count)

    return jax.shard_map(body, mesh=mesh, in_specs=in_specs, out_specs=out_specs, check_vma=False)
```

```python
import functools
import math

import jax
import jax.numpy as jnp
from jax import lax
from jax.experimental import pallas as pl
from jax.experimental.pallas import tpu as pltpu
from jax.sharding import PartitionSpec as P

HD = 64
EPSILON = 1e-06
BF = jnp.bfloat16
F32 = jnp.float32
VMEM_SPARE = 10 << 20


def mm(a, b):
    return jnp.dot(a, b, preferred_element_type=F32)


def mm_nt(a, b):
    return lax.dot_general(a, b, (((1,), (1,)), ((), ())), preferred_element_type=F32)


def mm_tn(a, b):
    return lax.dot_general(a, b, (((0,), (0,)), ((), ())), preferred_element_type=F32)


def inverse_rms(values):
    return lax.rsqrt(jnp.mean(values * values, axis=-1, keepdims=True) + EPSILON)


def call(kernel, outs, args, after=(), bits=None, scratch=(), flops=0, name=None):
    moved = sum(v.size * v.dtype.itemsize for v in (*args, *outs))
    scalars = [] if bits is None else [bits]
    count = len(scalars) + len(args)

    def body(*refs):
        kernel(*refs[:count], *refs[count + len(after) :])

    return pl.pallas_call(
        body,
        out_shape=outs,
        in_specs=[pl.BlockSpec(memory_space=pltpu.SMEM)] * len(scalars)
        + [pl.BlockSpec(memory_space=pltpu.VMEM)] * len(args)
        + [pl.BlockSpec(memory_space=pl.ANY)] * len(after),
        out_specs=[pl.BlockSpec(memory_space=pltpu.VMEM)] * len(outs),
        scratch_shapes=scratch,
        compiler_params=pltpu.CompilerParams(vmem_limit_bytes=VMEM_SPARE),
        cost_estimate=pl.CostEstimate(flops=flops, bytes_accessed=moved, transcendentals=0),
        name=name,
    )(*scalars, *args, *after)


def shape(dims, dtype=BF):
    return jax.ShapeDtypeStruct(tuple(dims), dtype)


def first_head(width=2 * HD):
    return lax.broadcasted_iota(jnp.int32, (1, width), 1) < HD


def attention_forward(rows, sel, states_ref, weights_ref, bias_ref, normed_ref, packed_ref, probs_ref, context_ref, gains_ref):
    width = states_ref.shape[1]
    half = context_ref.shape[1]
    gains_ref[...] = weights_ref[:, 4 * half :].astype(F32).T[:8]
    gain = gains_ref[0:1, :]
    scale = HD ** (-0.5)

    for row in range(rows):
        here = slice(row * sel, (row + 1) * sel)
        states = states_ref[here, :].astype(F32)
        normed_ref[here, :] = (states * inverse_rms(states) * gain).astype(BF)
    for start in range(0, 3 * half, 384):
        packed_ref[:, start : start + 384] = mm(normed_ref[...], weights_ref[:, start : start + 384]).astype(BF)
    first = first_head()

    @pl.loop(0, rows, unroll=True)
    def _(row):
        here = pl.ds(pl.multiple_of(row * sel, sel), sel)
        bias = bias_ref[row]
        for pair in range(half // (2 * HD)):
            at = pair * 2 * HD
            queries = packed_ref[here, at : at + 2 * HD]
            keys = packed_ref[here, half + at : half + at + 2 * HD]
            vals = packed_ref[here, 2 * half + at : 2 * half + at + 2 * HD]
            found = []
            for head in range(2):
                mine = first if head == 0 else ~first
                scores = mm_nt(jnp.where(mine, queries, jnp.zeros_like(queries)), keys) * scale + bias
                exponent = jnp.exp(scores - jnp.max(scores, axis=-1, keepdims=True))
                probs = exponent / jnp.sum(exponent, axis=-1, keepdims=True)
                probs_ref[row, 2 * pair + head] = probs
                found.append(mm(probs.astype(BF), vals))
            context_ref[here, at : at + 2 * HD] = jnp.where(first, found[0], found[1]).astype(BF)


def mix_forward(context_ref, mix_ref, out_ref):
    out_ref[...] = mm_nt(context_ref[...], mix_ref[...]).astype(BF)


def up_forward(
    rows, sel, states_ref, upstream_ref, own_ref, other_ref, up_ref, gains_ref, keep_ref,
    normed_ref, activated_ref, slope_ref, feed_grad_ref, grad_ref,
):
    mid_gain, router = gains_ref[1:2, :], gains_ref[2:3, :]
    c, a = (2.0 / math.pi) ** 0.5, 0.044715

    @pl.loop(0, rows)
    def _(row):
        here = pl.ds(pl.multiple_of(row * sel, sel), sel)
        states = states_ref[here, :].astype(F32)
        prob = jax.nn.sigmoid(jnp.sum(states * router, axis=-1, keepdims=True))
        gate = prob * keep_ref[here, :]
        feed_grad_ref[here, :] = (gate * upstream_ref[here, :].astype(F32)).astype(BF)
        middle = states + (own_ref[here, :].astype(F32) + other_ref[here, :].astype(F32))
        normed = (middle * inverse_rms(middle) * mid_gain).astype(BF)
        normed_ref[here, :] = normed

    upright_grad = feed_grad_ref[...].T
    chunk = 256
    for at in range(0, up_ref.shape[1], chunk):
        here = slice(at, at + chunk)
        hidden = mm(normed_ref[...], up_ref[:, here])
        square = hidden * hidden
        share = 0.5 * jnp.tanh(hidden * (c + c * a * square)) + 0.5
        activated = hidden * share
        activated_ref[:, here] = activated.astype(BF)
        slope = share + activated * (1.0 - share) * (2.0 * c + 6.0 * a * c * square)
        slope_ref[:, here] = slope.astype(BF)
        grad_ref[:, here] = mm(upright_grad, activated_ref[:, here]).astype(BF)


def down_backward(feed_grad_ref, down_ref, slope_ref, up_ref, hidden_grad_ref, out_ref):
    chunk = 256
    for at in range(0, down_ref.shape[1], chunk):
        here = slice(at, at + chunk)
        act_grad = mm(feed_grad_ref[...], down_ref[:, here])
        hidden_grad_ref[:, here] = (act_grad * slope_ref[:, here].astype(F32)).astype(BF)
    for at in range(0, out_ref.shape[1], chunk):
        here = slice(at, at + chunk)
        out_ref[:, here] = mm_nt(hidden_grad_ref[...], up_ref[here, :]).astype(BF)


def down_forward(normed_ref, hidden_grad_ref, activated_ref, down_ref, grad_ref, out_ref):
    upright_normed = normed_ref[...].T
    chunk = 256
    for at in range(0, grad_ref.shape[1], chunk):
        here = slice(at, at + chunk)
        grad_ref[:, here] = mm(upright_normed, hidden_grad_ref[:, here]).astype(BF)
    for at in range(0, out_ref.shape[1], chunk):
        here = slice(at, at + chunk)
        out_ref[:, here] = mm_nt(activated_ref[...], down_ref[here, :]).astype(BF)


def norm_backward(values, grads, gain):
    rho = inverse_rms(values)
    unit = values * rho
    scaled = grads * gain
    back = rho * (scaled - unit * jnp.mean(scaled * unit, axis=-1, keepdims=True))
    return back, jnp.sum(grads * unit, axis=0, keepdims=True)


def attention_backward(
    rows, sel, states_ref, own_ref, other_ref, mid_own_ref, mid_other_ref, upstream_ref, keep_ref, gains_ref,
    mix_ref, weights_ref, packed_ref, probs_ref,
    mixed_ref, packed_grad_ref, out_ref, middle_grad_ref, gain_grad_ref, context_grad_ref,
):
    mid_gain, router = gains_ref[1:2, :], gains_ref[2:3, :]
    half = mix_ref.shape[1]
    scale = HD ** (-0.5)
    gain_grad_ref[...] = jnp.zeros_like(gain_grad_ref)

    @pl.loop(0, rows)
    def _(row):
        here = pl.ds(pl.multiple_of(row * sel, sel), sel)
        states = states_ref[here, :].astype(F32)
        middle = states + (own_ref[here, :].astype(F32) + other_ref[here, :].astype(F32))
        mid_in = mid_own_ref[here, :].astype(F32) + mid_other_ref[here, :].astype(F32)
        middle_grad, gain_grad = norm_backward(middle, mid_in, mid_gain)
        gain_grad_ref[0:1, :] += gain_grad
        middle_grad_ref[here, :] = middle_grad
        gate = jax.nn.sigmoid(jnp.sum(states * router, axis=-1, keepdims=True)) * keep_ref[here, :]
        mixed = (gate * upstream_ref[here, :].astype(F32) + middle_grad).astype(BF)
        mixed_ref[here, :] = mixed

    context_grad_ref[...] = mm(mixed_ref[...], mix_ref[...]).astype(BF)
    first = first_head()

    @pl.loop(0, rows, unroll=True)
    def _(row):
        here = pl.ds(pl.multiple_of(row * sel, sel), sel)
        for pair in range(half // (2 * HD)):
            at = pair * 2 * HD
            queries = packed_ref[here, at : at + 2 * HD]
            keys = packed_ref[here, half + at : half + at + 2 * HD]
            vals = packed_ref[here, 2 * half + at : 2 * half + at + 2 * HD]
            grads = context_grad_ref[here, at : at + 2 * HD]
            queries_up, grads_up = queries.T, grads.T
            by_query, by_key, by_value = [], [], []
            for head in range(2):
                mine = first if head == 0 else ~first
                lanes = slice(head * HD, (head + 1) * HD)
                probs = probs_ref[row, 2 * pair + head]
                prob_grad = mm_nt(jnp.where(mine, grads, jnp.zeros_like(grads)), vals)
                centre = jnp.sum(probs * prob_grad, axis=-1, keepdims=True)
                score_grad = (probs * (prob_grad - centre)).astype(BF)
                by_query.append(mm(score_grad, keys))
                by_key.append(mm(queries_up[lanes], score_grad))
                by_value.append(mm(grads_up[lanes], probs.astype(BF)))
            packed_grad_ref[here, at : at + 2 * HD] = (
                jnp.where(first, by_query[0], by_query[1]) * scale
            ).astype(BF)
            packed_grad_ref[here, half + at : half + at + 2 * HD] = (
                (jnp.concatenate(by_key, axis=0) * scale).astype(BF).T
            )
            packed_grad_ref[here, 2 * half + at : 2 * half + at + 2 * HD] = (
                jnp.concatenate(by_value, axis=0).astype(BF).T
            )

    chunk = 256
    for at in range(0, out_ref.shape[1], chunk):
        here = slice(at, at + chunk)
        out_ref[:, here] = mm_nt(packed_grad_ref[...], weights_ref[here, : 3 * half]).astype(BF)


def projection_grads(normed_ref, packed_grad_ref, mixed_ref, context_ref, grad_ref):
    wide, chunk = packed_grad_ref.shape[1], 384
    upright_normed, upright_mixed = normed_ref[...].T, mixed_ref[...].T
    for at in range(0, wide, chunk):
        here = slice(at, at + chunk)
        grad_ref[:, here] = mm(upright_normed, packed_grad_ref[:, here]).astype(BF)
    grad_ref[:, wide:] = mm(upright_mixed, context_ref[...]).astype(BF)


def final_forward(
    rows, sel, states_ref, upstream_ref, own_ref, other_ref, feed_own_ref, feed_other_ref, gains_ref, keep_ref,
    finished_ref, logit_grad_ref, router_grad_ref,
):
    router = gains_ref[2:3, :]
    router_grad_ref[...] = jnp.zeros_like(router_grad_ref)

    @pl.loop(0, rows)
    def _(row):
        here = pl.ds(pl.multiple_of(row * sel, sel), sel)
        states = states_ref[here, :].astype(F32)
        attended = own_ref[here, :].astype(F32) + other_ref[here, :].astype(F32)
        branch = attended + (feed_own_ref[here, :].astype(F32) + feed_other_ref[here, :].astype(F32))
        prob = jax.nn.sigmoid(jnp.sum(states * router, axis=-1, keepdims=True))
        keep = keep_ref[here, :]
        finished_ref[here, :] = (states + prob * keep * branch).astype(BF)
        gate_grad = jnp.sum(upstream_ref[here, :].astype(F32) * branch, axis=-1, keepdims=True)
        logit_grad = gate_grad * keep * prob * (1.0 - prob)
        logit_grad_ref[here, :] = logit_grad
        router_grad_ref[0:1, :] += jnp.sum(logit_grad * states, axis=0, keepdims=True)


def final_backward(
    rows, sel, states_ref, upstream_ref, middle_grad_ref, pre_own_ref, pre_other_ref, logit_grad_ref, gains_ref,
    mid_gain_grad_ref, router_grad_ref, total_ref, vectors_ref, lines_ref,
):
    pre_gain, router = gains_ref[0:1, :], gains_ref[2:3, :]
    lines_ref[...] = jnp.zeros_like(lines_ref)
    lines_ref[1:2, :] = mid_gain_grad_ref[0:1, :]
    lines_ref[2:3, :] = router_grad_ref[0:1, :]

    @pl.loop(0, rows)
    def _(row):
        here = pl.ds(pl.multiple_of(row * sel, sel), sel)
        states = states_ref[here, :].astype(F32)
        pre_in = pre_own_ref[here, :].astype(F32) + pre_other_ref[here, :].astype(F32)
        back, gain_grad = norm_backward(states, pre_in, pre_gain)
        lines_ref[0:1, :] += gain_grad
        total = upstream_ref[here, :].astype(F32) + logit_grad_ref[here, :] * router
        total_ref[here, :] = (total + middle_grad_ref[here, :] + back).astype(BF)

    vectors_ref[...] = lines_ref[...].T.astype(BF)


def upright(row):
    return jnp.broadcast_to(row, (8, row.shape[1])).T[:, :1]


def select_rows(tokens_ref, cotangent_ref, chosen_ref, segments_ref, present_ref, picked_ref, bias_ref, keep_ref):
    sel, length = picked_ref.shape[2], tokens_ref.shape[1]
    row = pl.ds(pl.program_id(0), 1)
    chosen = upright(chosen_ref[row, :].astype(F32)).astype(jnp.int32)
    hit = chosen == lax.broadcasted_iota(jnp.int32, (sel, length), 1)
    one_hot = jnp.where(hit, 1.0, 0.0).astype(BF)
    picked_ref[0, 0] = mm(one_hot, tokens_ref[0]).astype(BF)
    picked_ref[1, 0] = mm(one_hot, cotangent_ref[0]).astype(BF)
    both = jnp.concatenate(
        [segments_ref[row, :].astype(F32), present_ref[row, :].astype(F32), jnp.zeros((6, length), F32)], axis=0
    ).astype(BF)
    along = mm_nt(both, one_hot)
    down = along.T
    slot = lax.broadcasted_iota(jnp.int32, (sel, sel), 0)
    seen = lax.broadcasted_iota(jnp.int32, (sel, sel), 1)
    open_key = (along[1:2, :] > 0.5) | (slot == seen)
    permitted = (seen <= slot) & (down[:, 0:1] == along[0:1, :]) & open_key
    bias_ref[0] = jnp.where(permitted, 0.0, -1e30)
    keep_ref[...] = down[:, 1:2]


def select(tokens, cotangent, chosen, segments, present):
    rows, length, half = tokens.shape
    sel = chosen.shape[1]
    by_row = pl.BlockSpec((1, length, half), lambda row: (row, 0, 0))
    all_of = lambda v: pl.BlockSpec(v.shape, lambda row: (0, 0))
    return pl.pallas_call(
        select_rows,
        grid=(rows,),
        out_shape=(shape((2, rows, sel, half)), shape((rows, sel, sel), F32), shape((rows * sel, 1), F32)),
        in_specs=[by_row, by_row, all_of(chosen), all_of(segments), all_of(present)],
        out_specs=[
            pl.BlockSpec((2, 1, sel, half), lambda row: (0, row, 0, 0)),
            pl.BlockSpec((1, sel, sel), lambda row: (row, 0, 0)),
            pl.BlockSpec((sel, 1), lambda row: (row, 0)),
        ],
        compiler_params=pltpu.CompilerParams(vmem_limit_bytes=60 << 20),
        cost_estimate=pl.CostEstimate(
            flops=4 * rows * sel * length * half, bytes_accessed=4 * tokens.size, transcendentals=0
        ),
        name="select_rows",
    )(tokens, cotangent, chosen, segments, present)


def put_rows(bits_ref, chosen_ref, values_ref, base_ref, out_ref):
    long, half = out_ref.shape[1:]
    sel = values_ref.shape[0]
    first = pl.program_id(1) * long
    chosen = chosen_ref[pl.ds(pl.program_id(0), 1), :]
    hit = first + lax.broadcasted_iota(jnp.int32, (long, sel), 0) == chosen
    one_hot = jnp.where(hit, 1.0, 0.0).astype(BF)
    offset = pl.multiple_of(bits_ref[-1 + bits_ref.shape[0]] * half, half)
    values = values_ref[:, pl.ds(offset, half)]
    placed = mm(one_hot, jnp.concatenate([values, jnp.ones((sel, 128), BF)], axis=1))
    taken = placed[:, half:] > 0.5
    for at in range(0, half, 128):
        here = slice(at, at + 128)
        out_ref[0, :, here] = jnp.where(taken, placed[:, here].astype(BF), base_ref[0, :, here])


def put(base, chosen, values, bits, after=()):
    rows, length, half = base.shape
    sel = chosen.shape[1]
    long = length // 2

    def body(*refs):
        put_rows(*refs[:4], refs[-2])
        refs[-1][...] = jnp.zeros_like(refs[-1])

    return pl.pallas_call(
        body,
        grid=(rows, length // long),
        out_shape=(shape(base.shape), shape((8, 128), F32)),
        in_specs=[
            pl.BlockSpec(memory_space=pltpu.SMEM),
            pl.BlockSpec(chosen.shape, lambda row, part: (0, 0)),
            pl.BlockSpec((sel, values.shape[1]), lambda row, part: (row, 0)),
            pl.BlockSpec((1, long, half), lambda row, part: (row, part, 0)),
        ]
        + [pl.BlockSpec(memory_space=pl.ANY)] * len(after),
        out_specs=[
            pl.BlockSpec((1, long, half), lambda row, part: (row, part, 0)),
            pl.BlockSpec((8, 128), lambda row, part: (0, 0)),
        ],
        compiler_params=pltpu.CompilerParams(vmem_limit_bytes=24 << 20),
        cost_estimate=pl.CostEstimate(
            flops=2 * rows * sel * length * half, bytes_accessed=4 * base.size, transcendentals=0
        ),
        name="put_rows",
    )(bits, chosen, values, base, *after)


def first_columns(attention_ref, mixing_ref, vectors_ref, out_ref):
    half = attention_ref.shape[2]
    for k in range(3):
        out_ref[:, k * half : (k + 1) * half] = attention_ref[k]
    out_ref[:, 3 * half : 4 * half] = mixing_ref[...]
    out_ref[:, 4 * half :] = vectors_ref[...]


def second_columns(cuts, expand_ref, contract_ref, out_ref):
    at = 0
    for start, end in cuts:
        out_ref[:, at : at + end - start] = expand_ref[:, start:end]
        at += end - start
        out_ref[:, at : at + end - start] = contract_ref[:, start:end]
        at += end - start


def untouched(*refs):
    pass


def tie(value, *others):
    if not others:
        return value
    anywhere = pl.BlockSpec(memory_space=pl.ANY)
    return pl.pallas_call(
        untouched,
        out_shape=jax.ShapeDtypeStruct(value.shape, value.dtype),
        in_specs=[anywhere] * (1 + len(others)),
        out_specs=anywhere,
        input_output_aliases={0: 0},
        compiler_params=pltpu.CompilerParams(vmem_limit_bytes=1 << 20),
        cost_estimate=pl.CostEstimate(flops=0, bytes_accessed=0, transcendentals=0),
    )(value, *others)


class Cube:
    def __init__(self, count):
        self.count, self.depth = count, count.bit_length() - 1
        index = lax.axis_index("dp").astype(jnp.int32)
        self.bits = jnp.append(
            (index >> jnp.arange(self.depth)) & 1, lax.axis_index("mp").astype(jnp.int32)
        )
        short = self.depth // 3
        self.x, self.y = list(range(short)), list(range(short, 2 * short))
        self.z = list(range(2 * short, self.depth))
        self.far = self.z[1:]
        near = [self.x, self.y, self.z[:1]]
        self.orders = [sum(near[k:] + near[:k], []) for k in range(3)]

    def swap(self, value, bit):
        return lax.ppermute(value, "dp", [(i, i ^ (1 << bit)) for i in range(self.count)])


class Part:
    def __init__(self, value, bits, sent=None, start=0, width=None):
        self.value, self.bits, self.sent = value, list(bits), sent
        self.start, self.width = start, width or value.shape[2]

    def columns(self, start, end):
        return Part(self.value, self.bits, self.sent, self.start + start, end - start)


def thirds(width):
    ends = [(k * width // 3 + 64) // 128 * 128 for k in range(4)]
    return list(zip(ends, ends[1:]))


def start_exchange(cube, part, bit):
    part.sent = cube.swap(part.value, bit)
    return part


def stack_parts(plan, bits_ref, *refs):
    ins, outs = refs[: 2 * len(plan)], refs[2 * len(plan) :]
    for k, (bit, blocks) in enumerate(plan):
        mine = bits_ref[bit]
        for block in range(blocks):
            outs[k][mine, block] = ins[2 * k][block]
            outs[k][1 - mine, block] = ins[2 * k + 1][block]


def stack(cube, parts, bits, after=()):
    outs, args, plan = [], [], []
    for part, bit in zip(parts, bits):
        outs.append(shape((2,) + part.value.shape))
        args += [part.value, part.sent]
        plan.append((bit, part.value.shape[0]))
    found = call(functools.partial(stack_parts, plan), outs, args, after, cube.bits, name="stack_parts")
    return [
        Part(v.reshape((-1,) + v.shape[2:]), [bit] + part.bits) for v, part, bit in zip(found, parts, bits)
    ]


def split_columns(plan, own_ref, *out_refs):
    for ref, (start, end) in zip(out_refs, plan):
        ref[...] = own_ref[:, :, start:end]


def whole_rows(plan, bits_ref, *refs):
    ins, out_ref = refs[:-1], refs[-1]
    column = 0
    for k, (bit, places, start, width) in enumerate(plan):
        mine = bits_ref[bit]
        for block, place in enumerate(places):
            here = slice(column, column + width)
            out_ref[place + (mine << bit), :, here] = ins[2 * k][block, :, start : start + width]
            out_ref[place + ((1 - mine) << bit), :, here] = ins[2 * k + 1][block, :, start : start + width]
        column += width


def whole(cube, parts, bits, after=()):
    args, plan, width = [], [], 0
    for part, bit in zip(parts, bits):
        places = []
        for block in range(part.value.shape[0]):
            digits = [(block >> k) & 1 for k in range(len(part.bits))][::-1]
            places.append(sum(digit << b for digit, b in zip(digits, part.bits)))
        args += [part.value, part.sent]
        plan.append((bit, places, part.start, part.width))
        width += part.width
    rows = parts[0].value.shape[1]
    (found,) = call(
        functools.partial(whole_rows, plan),
        (shape((cube.count, rows, width)),),
        args,
        after,
        cube.bits,
        name="whole_rows",
    )
    return found.reshape(-1, width)


def fold_parts(plan, bits_ref, *refs):
    refs = list(refs)
    taken = [[(refs.pop(0), refs.pop(0) if sent else None) for sent, _, _ in sources] for _, _, sources in plan]
    for (bit, (high, low), sources), ins in zip(plan, taken):
        sent_ref, kept_ref = refs.pop(0), refs.pop(0)
        mine = bits_ref[bit]
        column = 0
        for (_, start, width), (value_ref, other_ref) in zip(sources, ins):
            there = slice(start, start + width)
            here = slice(column, column + width)
            for a in range(high):
                for b in range(low):
                    for index, out_ref in ((1 - mine, sent_ref), (mine, kept_ref)):
                        found = value_ref[a, index, b, :, there].astype(F32)
                        if other_ref is not None:
                            found += other_ref[a, index, b, :, there].astype(F32)
                        out_ref[a * low + b, :, here] = found.astype(out_ref.dtype)
            column += width


def fold(cube, groups, bits, after=()):
    args, outs, plan = [], [], []
    for sources, bit in zip(groups, bits):
        at = sources[0].bits.index(bit)
        high, low = 1 << at, 1 << (len(sources[0].bits) - at - 1)
        listed = []
        for part in sources:
            for value in (part.value, part.sent):
                if value is not None:
                    args.append(value.reshape((high, 2, low) + value.shape[1:]))
            listed.append((part.sent is not None, part.start, part.width))
        plan.append((bit, (high, low), listed))
        dims = (high * low, sources[0].value.shape[1], sum(p.width for p in sources))
        outs += [shape(dims), shape(dims, F32)]
    found = call(functools.partial(fold_parts, plan), outs, args, after, cube.bits, name="fold_parts")
    done = []
    for k, (sources, bit) in enumerate(zip(groups, bits)):
        left = [b for b in sources[0].bits if b != bit]
        done.append(Part(found[2 * k + 1], left, cube.swap(found[2 * k], bit)))
    return done


def cut(cube, total):
    blocks = total.reshape(cube.count, -1, total.shape[1])
    bits = list(range(cube.depth))[::-1]
    return [Part(blocks, bits, None, start, end - start) for start, end in thirds(total.shape[1]) if end > start]


def arrived(parts):
    return [p.sent for p in parts]


def sum_first(value_ref, sent_ref, attention_ref, mixing_ref, vectors_ref):
    half = attention_ref.shape[2]
    total = value_ref[0] + sent_ref[0].astype(F32)
    for k in range(3):
        attention_ref[k] = total[:, k * half : (k + 1) * half]
    mixing_ref[...] = total[:, 3 * half : 4 * half]
    vectors_ref[...] = total[:, 4 * half :].T


def sum_second(cuts, value_ref, sent_ref, expand_ref, contract_ref):
    at = 0
    for start, end in cuts:
        for side in range(2):
            width = end - start
            total = value_ref[0, :, at : at + width] + sent_ref[0, :, at : at + width].astype(F32)
            (expand_ref if side else contract_ref)[:, start:end] = total
            at += width


def other_core(value):
    return lax.ppermute(value, "mp", [(0, 1), (1, 0)])


def both_halves(value):
    other = other_core(value)
    low = lax.axis_index("mp") == 0
    return jnp.concatenate([jnp.where(low, value, other), jnp.where(low, other, value)], axis=-1)


def shards(
    tokens,
    segments,
    present,
    chosen,
    attention,
    mixing,
    expand,
    contract,
    prenorm,
    midnorm,
    router,
    cotangent,
    count,
):
    cube = Cube(count)
    row_count, length, half_width = tokens.shape
    sel_count = chosen.shape[1]
    token_count = row_count * sel_count
    own_rows = mixing.shape[1]
    width = 2 * half_width
    hidden_here = expand.shape[1]
    heads_here = half_width // HD
    by_row = (row_count, sel_count)

    vectors = jnp.pad(jnp.stack([prenorm, midnorm, router], axis=1), ((0, 0), (0, 125)))
    cuts = thirds(hidden_here)
    (first_own,) = call(
        first_columns, (shape((own_rows, 4 * half_width + 128)),), (attention, mixing.T, vectors), name="first_columns"
    )
    first_far = start_exchange(cube, Part(first_own[None], []), cube.far[-1])
    (second_own,) = call(
        functools.partial(second_columns, cuts),
        (shape((own_rows, 2 * hidden_here)),),
        (expand, contract.T),
        name="second_columns",
    )
    picked, bias, keep = select(tokens, cotangent, chosen, segments, present)

    def spread(far, after, begin=()):
        for bit in cube.far[-2::-1]:
            far = start_exchange(cube, stack(cube, [far], [far_bit(far)], after)[0], bit)
        column = stack(cube, [far], [far_bit(far)], after)[0]
        ends = thirds(column.width)
        found = call(
            functools.partial(split_columns, ends),
            [shape(column.value.shape[:2] + (end - start,)) for start, end in ends],
            [column.value],
            begin,
            name="split_columns",
        )
        return [Part(v, column.bits) for v in found]

    def far_bit(part):
        return cube.far[-1 - len(part.bits)]

    def step_bits(step):
        return [order[step] for order in cube.orders]

    def send(parts, step):
        return [start_exchange(cube, p, bit) for p, bit in zip(parts, step_bits(step))]

    steps = len(cube.orders[0])
    first_parts = spread(first_far, [picked])
    both = both_halves(tie(picked, first_parts[0].value))
    states = both[0].reshape(token_count, width)
    upstream = both[1].reshape(token_count, width)
    first_parts = send(first_parts, 0)
    second_far = start_exchange(cube, Part(tie(second_own, *arrived([first_far]))[None], []), cube.far[-1])
    for step in range(1, steps):
        after = arrived([second_far]) if step == steps - 1 else [states, upstream] if step == 1 else []
        first_parts = send(stack(cube, first_parts, step_bits(step - 1), after), step)
    first_last = [p.value for p in first_parts]
    first = whole(cube, first_parts, step_bits(steps - 1))
    mix = first[:, 3 * half_width : 4 * half_width]
    second_parts = send(spread(second_far, [], first_last[:1]), 0)
    second_begun = []
    for step in range(1, steps - 1):
        second_parts = stack(cube, second_parts, step_bits(step - 1), [first] if step == 1 else [])
        second_begun = second_begun or [p.value for p in second_parts]
        second_parts = send(second_parts, step)
    second_parts = stack(cube, second_parts, step_bits(steps - 2))
    each = hidden_here // 3
    up_parts, down_parts = [], []
    for p in second_parts:
        up_parts.append(Part(p.value[..., :each], p.bits))
        down_parts.append(Part(p.value[..., each:], p.bits))
    up = whole(cube, send(up_parts, steps - 1), step_bits(steps - 1))
    down_parts = send(down_parts, steps - 1)

    wide = shape((token_count, width))
    tall = shape((token_count, hidden_here))
    vector = shape((8, width), F32)
    normed, packed, probs, context, gains = call(
        functools.partial(attention_forward, *by_row),
        (
            wide,
            shape((token_count, 3 * half_width)),
            shape((row_count, heads_here, sel_count, sel_count), F32),
            shape((token_count, half_width)),
            vector,
        ),
        (states, first, bias),
        after=second_begun,
        flops=token_count * width * half_width * 6,
        name="attention_forward",
    )
    (att_own,) = call(
        mix_forward, (wide,), (context, mix), flops=2 * token_count * width * half_width, name="mix_forward"
    )
    att_other = other_core(att_own)
    normed_mid, activated, slope, feed_grad, down_grad = call(
        functools.partial(up_forward, *by_row),
        (wide, tall, tall, wide, shape((width, hidden_here))),
        (states, upstream, att_own, att_other, up, gains, keep),
        flops=4 * token_count * width * hidden_here,
        name="up_forward",
    )
    down = whole(cube, down_parts, step_bits(steps - 1), [activated])

    hidden_grad, mid_own = call(
        down_backward,
        (tall, wide),
        (feed_grad, down, slope, up),
        flops=4 * token_count * width * hidden_here,
        name="down_backward",
    )
    up_grad, feed_own = call(
        down_forward,
        (shape((width, hidden_here)), wide),
        (normed_mid, hidden_grad, activated, down),
        flops=4 * token_count * width * hidden_here,
        name="down_forward",
    )
    feed_other = other_core(feed_own)
    mid_other = tie(other_core(mid_own), feed_own)

    def back_bits(step):
        return [order[-1 - step] for order in cube.orders]

    def alone(parts):
        return [[p] for p in parts]

    both_grads = [list(pair) for pair in zip(cut(cube, down_grad), cut(cube, up_grad))]
    both_grads = fold(cube, both_grads, back_bits(0))

    mixed, packed_grad, pre_own, middle_grad, mid_gain_grad = call(
        functools.partial(attention_backward, *by_row),
        (
            wide,
            shape((token_count, 3 * half_width)),
            wide,
            shape((token_count, width), F32),
            vector,
        ),
        (states, att_own, att_other, mid_own, mid_other, upstream, keep, gains, mix, first, packed, probs),
        after=[both_grads[0].value],
        scratch=[pltpu.VMEM((token_count, half_width), BF)],
        flops=10 * token_count * width * half_width,
        name="attention_backward",
    )
    (first_grad,) = call(
        projection_grads,
        (shape((width, 4 * half_width)),),
        (normed, packed_grad, mixed, context),
        flops=8 * token_count * width * half_width,
        name="projection_grads",
    )
    both_grads = fold(cube, alone(both_grads), back_bits(1), [first_grad])
    pre_other = other_core(tie(pre_own, both_grads[0].value))
    finished, logit_grad, router_grad = call(
        functools.partial(final_forward, *by_row),
        (wide, shape((token_count, 1), F32), vector),
        (states, upstream, att_own, att_other, feed_own, feed_other, gains, keep),
        after=[both_grads[0].value],
        name="final_forward",
    )
    total_grad, vector_grads = call(
        functools.partial(final_backward, *by_row),
        (wide, shape((width, 128))),
        (states, upstream, middle_grad, pre_own, pre_other, logit_grad, gains, mid_gain_grad, router_grad),
        scratch=[pltpu.VMEM((128, width), F32)],
        name="final_backward",
    )
    first_grads = alone(cut(cube, first_grad))
    first_grads[-1] += cut(cube, vector_grads)
    first_grads = fold(cube, first_grads, back_bits(0))
    result, done = put(tokens, chosen, finished, cube.bits, [first_grads[0].value])
    tokens_grad, _ = put(cotangent, chosen, total_grad, cube.bits, [done])
    for step in range(2, steps):
        both_grads = fold(cube, alone(both_grads), back_bits(step), [first_grad] if step == 2 else [])
    for step in range(1, steps):
        first_grads = fold(cube, alone(first_grads), back_bits(step), [done] if step == 1 else [])
    both_grads, first_grads = [both_grads], [first_grads]
    for bit in cube.far:
        both_grads = [fold(cube, both_grads, [bit])]
        first_grads = [fold(cube, first_grads, [bit])]
    (both_grad,), (first_grad,) = both_grads[0], first_grads[0]
    up_out, down_out = call(
        functools.partial(sum_second, cuts),
        (shape((own_rows, hidden_here), F32),) * 2,
        (both_grad.value, both_grad.sent),
        name="sum_second",
    )
    attention_out, mixing_out, vector_out = call(
        sum_first,
        (
            shape((3, own_rows, half_width), F32),
            shape((own_rows, half_width), F32),
            shape((128, own_rows), F32),
        ),
        (first_grad.value, first_grad.sent),
        name="sum_first",
    )
    return (
        result,
        tokens_grad,
        attention_out,
        mixing_out.T,
        up_out,
        down_out.T,
        vector_out[0],
        vector_out[1],
        vector_out[2],
    )


def solution(mesh):
    in_specs = (
        P("dp", None, "mp"),
        P("dp", None),
        P("dp", None),
        P("dp", None),
        P(None, "dp", "mp"),
        P("mp", "dp"),
        P("dp", "mp"),
        P("mp", "dp"),
        P("dp"),
        P("dp"),
        P("dp"),
        P("dp", None, "mp"),
    )
    out_specs = (
        P("dp", None, "mp"),
        P("dp", None, "mp"),
        P(None, "dp", "mp"),
        P("mp", "dp"),
        P("dp", "mp"),
        P("mp", "dp"),
        P("dp"),
        P("dp"),
        P("dp"),
    )
    count = mesh.shape["dp"]

    def body(*args):
        return shards(*args, count)

    return jax.shard_map(body, mesh=mesh, in_specs=in_specs, out_specs=out_specs, check_vma=False)
```

```python
import functools
import math

import jax
import jax.numpy as jnp
from jax import lax
from jax.experimental import pallas as pl
from jax.experimental.pallas import tpu as pltpu
from jax.sharding import PartitionSpec as P

HD = 64
EPSILON = 1e-06
BF = jnp.bfloat16
F32 = jnp.float32
VMEM_SPARE = 10 << 20


def mm(a, b):
    return jnp.dot(a, b, preferred_element_type=F32)


def mm_nt(a, b):
    return lax.dot_general(a, b, (((1,), (1,)), ((), ())), preferred_element_type=F32)


def mm_tn(a, b):
    return lax.dot_general(a, b, (((0,), (0,)), ((), ())), preferred_element_type=F32)


def inverse_rms(values):
    return lax.rsqrt(jnp.mean(values * values, axis=-1, keepdims=True) + EPSILON)


def call(kernel, outs, args, after=(), bits=None, scratch=(), flops=0, name=None):
    moved = sum(v.size * v.dtype.itemsize for v in (*args, *outs))
    scalars = [] if bits is None else [bits]
    count = len(scalars) + len(args)

    def body(*refs):
        kernel(*refs[:count], *refs[count + len(after) :])

    return pl.pallas_call(
        body,
        out_shape=outs,
        in_specs=[pl.BlockSpec(memory_space=pltpu.SMEM)] * len(scalars)
        + [pl.BlockSpec(memory_space=pltpu.VMEM)] * len(args)
        + [pl.BlockSpec(memory_space=pl.ANY)] * len(after),
        out_specs=[pl.BlockSpec(memory_space=pltpu.VMEM)] * len(outs),
        scratch_shapes=scratch,
        compiler_params=pltpu.CompilerParams(vmem_limit_bytes=VMEM_SPARE),
        cost_estimate=pl.CostEstimate(flops=flops, bytes_accessed=moved, transcendentals=0),
        name=name,
    )(*scalars, *args, *after)


def shape(dims, dtype=BF):
    return jax.ShapeDtypeStruct(tuple(dims), dtype)


def first_head(width=2 * HD):
    return lax.broadcasted_iota(jnp.int32, (1, width), 1) < HD


def attention_forward(rows, sel, states_ref, weights_ref, bias_ref, normed_ref, packed_ref, probs_ref, context_ref, gains_ref):
    width = states_ref.shape[1]
    half = context_ref.shape[1]
    gains_ref[...] = weights_ref[:, 4 * half :].astype(F32).T[:8]
    gain = gains_ref[0:1, :]
    scale = HD ** (-0.5)

    for row in range(rows):
        here = slice(row * sel, (row + 1) * sel)
        states = states_ref[here, :].astype(F32)
        normed_ref[here, :] = (states * inverse_rms(states) * gain).astype(BF)
    for start in range(0, 3 * half, 384):
        packed_ref[:, start : start + 384] = mm(normed_ref[...], weights_ref[:, start : start + 384]).astype(BF)
    first = first_head()

    @pl.loop(0, rows, unroll=True)
    def _(row):
        here = pl.ds(pl.multiple_of(row * sel, sel), sel)
        bias = bias_ref[row]
        for pair in range(half // (2 * HD)):
            at = pair * 2 * HD
            queries = packed_ref[here, at : at + 2 * HD]
            keys = packed_ref[here, half + at : half + at + 2 * HD]
            vals = packed_ref[here, 2 * half + at : 2 * half + at + 2 * HD]
            found = []
            for head in range(2):
                mine = first if head == 0 else ~first
                scores = mm_nt(jnp.where(mine, queries, jnp.zeros_like(queries)), keys) * scale + bias
                exponent = jnp.exp(scores - jnp.max(scores, axis=-1, keepdims=True))
                probs = exponent / jnp.sum(exponent, axis=-1, keepdims=True)
                probs_ref[row, 2 * pair + head] = probs
                found.append(mm(probs.astype(BF), vals))
            context_ref[here, at : at + 2 * HD] = jnp.where(first, found[0], found[1]).astype(BF)


def mix_forward(context_ref, mix_ref, out_ref):
    out_ref[...] = mm_nt(context_ref[...], mix_ref[...]).astype(BF)


def up_forward(
    rows, sel, states_ref, upstream_ref, own_ref, other_ref, up_ref, gains_ref, keep_ref,
    normed_ref, activated_ref, slope_ref, feed_grad_ref, grad_ref,
):
    mid_gain, router = gains_ref[1:2, :], gains_ref[2:3, :]
    c, a = (2.0 / math.pi) ** 0.5, 0.044715

    @pl.loop(0, rows)
    def _(row):
        here = pl.ds(pl.multiple_of(row * sel, sel), sel)
        states = states_ref[here, :].astype(F32)
        prob = jax.nn.sigmoid(jnp.sum(states * router, axis=-1, keepdims=True))
        gate = prob * keep_ref[here, :]
        feed_grad_ref[here, :] = (gate * upstream_ref[here, :].astype(F32)).astype(BF)
        middle = states + (own_ref[here, :].astype(F32) + other_ref[here, :].astype(F32))
        normed = (middle * inverse_rms(middle) * mid_gain).astype(BF)
        normed_ref[here, :] = normed

    upright_grad = feed_grad_ref[...].T
    chunk = 256
    for at in range(0, up_ref.shape[1], chunk):
        here = slice(at, at + chunk)
        hidden = mm(normed_ref[...], up_ref[:, here])
        square = hidden * hidden
        share = 0.5 * jnp.tanh(hidden * (c + c * a * square)) + 0.5
        activated = hidden * share
        activated_ref[:, here] = activated.astype(BF)
        slope = share + activated * (1.0 - share) * (2.0 * c + 6.0 * a * c * square)
        slope_ref[:, here] = slope.astype(BF)
        grad_ref[:, here] = mm(upright_grad, activated_ref[:, here]).astype(BF)


def down_backward(feed_grad_ref, down_ref, slope_ref, up_ref, hidden_grad_ref, out_ref):
    chunk = 256
    for at in range(0, down_ref.shape[1], chunk):
        here = slice(at, at + chunk)
        act_grad = mm(feed_grad_ref[...], down_ref[:, here])
        hidden_grad_ref[:, here] = (act_grad * slope_ref[:, here].astype(F32)).astype(BF)
    for at in range(0, out_ref.shape[1], chunk):
        here = slice(at, at + chunk)
        out_ref[:, here] = mm_nt(hidden_grad_ref[...], up_ref[here, :]).astype(BF)


def down_forward(normed_ref, hidden_grad_ref, activated_ref, down_ref, grad_ref, out_ref):
    upright_normed = normed_ref[...].T
    chunk = 256
    for at in range(0, grad_ref.shape[1], chunk):
        here = slice(at, at + chunk)
        grad_ref[:, here] = mm(upright_normed, hidden_grad_ref[:, here]).astype(BF)
    for at in range(0, out_ref.shape[1], chunk):
        here = slice(at, at + chunk)
        out_ref[:, here] = mm_nt(activated_ref[...], down_ref[here, :]).astype(BF)


def norm_backward(values, grads, gain):
    rho = inverse_rms(values)
    unit = values * rho
    scaled = grads * gain
    back = rho * (scaled - unit * jnp.mean(scaled * unit, axis=-1, keepdims=True))
    return back, jnp.sum(grads * unit, axis=0, keepdims=True)


def attention_backward(
    rows, sel, states_ref, own_ref, other_ref, mid_own_ref, mid_other_ref, upstream_ref, keep_ref, gains_ref,
    mix_ref, weights_ref, packed_ref, probs_ref,
    mixed_ref, packed_grad_ref, out_ref, middle_grad_ref, gain_grad_ref, context_grad_ref,
):
    mid_gain, router = gains_ref[1:2, :], gains_ref[2:3, :]
    half = mix_ref.shape[1]
    scale = HD ** (-0.5)
    gain_grad_ref[...] = jnp.zeros_like(gain_grad_ref)

    @pl.loop(0, rows)
    def _(row):
        here = pl.ds(pl.multiple_of(row * sel, sel), sel)
        states = states_ref[here, :].astype(F32)
        middle = states + (own_ref[here, :].astype(F32) + other_ref[here, :].astype(F32))
        mid_in = mid_own_ref[here, :].astype(F32) + mid_other_ref[here, :].astype(F32)
        middle_grad, gain_grad = norm_backward(middle, mid_in, mid_gain)
        gain_grad_ref[0:1, :] += gain_grad
        middle_grad_ref[here, :] = middle_grad
        gate = jax.nn.sigmoid(jnp.sum(states * router, axis=-1, keepdims=True)) * keep_ref[here, :]
        mixed = (gate * upstream_ref[here, :].astype(F32) + middle_grad).astype(BF)
        mixed_ref[here, :] = mixed

    context_grad_ref[...] = mm(mixed_ref[...], mix_ref[...]).astype(BF)
    first = first_head()

    @pl.loop(0, rows, unroll=True)
    def _(row):
        here = pl.ds(pl.multiple_of(row * sel, sel), sel)
        for pair in range(half // (2 * HD)):
            at = pair * 2 * HD
            queries = packed_ref[here, at : at + 2 * HD]
            keys = packed_ref[here, half + at : half + at + 2 * HD]
            vals = packed_ref[here, 2 * half + at : 2 * half + at + 2 * HD]
            grads = context_grad_ref[here, at : at + 2 * HD]
            queries_up, grads_up = queries.T, grads.T
            by_query, by_key, by_value = [], [], []
            for head in range(2):
                mine = first if head == 0 else ~first
                lanes = slice(head * HD, (head + 1) * HD)
                probs = probs_ref[row, 2 * pair + head]
                prob_grad = mm_nt(jnp.where(mine, grads, jnp.zeros_like(grads)), vals)
                centre = jnp.sum(probs * prob_grad, axis=-1, keepdims=True)
                score_grad = (probs * (prob_grad - centre)).astype(BF)
                by_query.append(mm(score_grad, keys))
                by_key.append(mm(queries_up[lanes], score_grad))
                by_value.append(mm(grads_up[lanes], probs.astype(BF)))
            packed_grad_ref[here, at : at + 2 * HD] = (
                jnp.where(first, by_query[0], by_query[1]) * scale
            ).astype(BF)
            packed_grad_ref[here, half + at : half + at + 2 * HD] = (
                (jnp.concatenate(by_key, axis=0) * scale).astype(BF).T
            )
            packed_grad_ref[here, 2 * half + at : 2 * half + at + 2 * HD] = (
                jnp.concatenate(by_value, axis=0).astype(BF).T
            )

    chunk = 256
    for at in range(0, out_ref.shape[1], chunk):
        here = slice(at, at + chunk)
        out_ref[:, here] = mm_nt(packed_grad_ref[...], weights_ref[here, : 3 * half]).astype(BF)


def projection_grads(normed_ref, packed_grad_ref, mixed_ref, context_ref, grad_ref):
    wide, chunk = packed_grad_ref.shape[1], 384
    upright_normed, upright_mixed = normed_ref[...].T, mixed_ref[...].T
    for at in range(0, wide, chunk):
        here = slice(at, at + chunk)
        grad_ref[:, here] = mm(upright_normed, packed_grad_ref[:, here]).astype(BF)
    grad_ref[:, wide:] = mm(upright_mixed, context_ref[...]).astype(BF)


def final_forward(
    rows, sel, states_ref, upstream_ref, own_ref, other_ref, feed_own_ref, feed_other_ref, gains_ref, keep_ref,
    finished_ref, logit_grad_ref, router_grad_ref,
):
    router = gains_ref[2:3, :]
    router_grad_ref[...] = jnp.zeros_like(router_grad_ref)

    @pl.loop(0, rows)
    def _(row):
        here = pl.ds(pl.multiple_of(row * sel, sel), sel)
        states = states_ref[here, :].astype(F32)
        attended = own_ref[here, :].astype(F32) + other_ref[here, :].astype(F32)
        branch = attended + (feed_own_ref[here, :].astype(F32) + feed_other_ref[here, :].astype(F32))
        prob = jax.nn.sigmoid(jnp.sum(states * router, axis=-1, keepdims=True))
        keep = keep_ref[here, :]
        finished_ref[here, :] = (states + prob * keep * branch).astype(BF)
        gate_grad = jnp.sum(upstream_ref[here, :].astype(F32) * branch, axis=-1, keepdims=True)
        logit_grad = gate_grad * keep * prob * (1.0 - prob)
        logit_grad_ref[here, :] = logit_grad
        router_grad_ref[0:1, :] += jnp.sum(logit_grad * states, axis=0, keepdims=True)


def final_backward(
    rows, sel, states_ref, upstream_ref, middle_grad_ref, pre_own_ref, pre_other_ref, logit_grad_ref, gains_ref,
    mid_gain_grad_ref, router_grad_ref, total_ref, vectors_ref, lines_ref,
):
    pre_gain, router = gains_ref[0:1, :], gains_ref[2:3, :]
    lines_ref[...] = jnp.zeros_like(lines_ref)
    lines_ref[1:2, :] = mid_gain_grad_ref[0:1, :]
    lines_ref[2:3, :] = router_grad_ref[0:1, :]

    @pl.loop(0, rows)
    def _(row):
        here = pl.ds(pl.multiple_of(row * sel, sel), sel)
        states = states_ref[here, :].astype(F32)
        pre_in = pre_own_ref[here, :].astype(F32) + pre_other_ref[here, :].astype(F32)
        back, gain_grad = norm_backward(states, pre_in, pre_gain)
        lines_ref[0:1, :] += gain_grad
        total = upstream_ref[here, :].astype(F32) + logit_grad_ref[here, :] * router
        total_ref[here, :] = (total + middle_grad_ref[here, :] + back).astype(BF)

    vectors_ref[...] = lines_ref[...].T.astype(BF)


def upright(row):
    return jnp.broadcast_to(row, (8, row.shape[1])).T[:, :1]


def one_hot_rows(chosen_ref, sel, length):
    row = pl.ds(pl.program_id(0), 1)
    chosen = upright(chosen_ref[row, :].astype(F32)).astype(jnp.int32)
    return jnp.where(chosen == lax.broadcasted_iota(jnp.int32, (sel, length), 1), 1.0, 0.0).astype(BF)


def pick_rows(base_ref, chosen_ref, picked_ref):
    one_hot = one_hot_rows(chosen_ref, picked_ref.shape[1], base_ref.shape[1])
    picked_ref[0] = mm(one_hot, base_ref[0]).astype(BF)


def pick_and_mask(base_ref, chosen_ref, segments_ref, present_ref, picked_ref, bias_ref, keep_ref):
    sel, length = picked_ref.shape[1], base_ref.shape[1]
    row = pl.ds(pl.program_id(0), 1)
    one_hot = one_hot_rows(chosen_ref, sel, length)
    picked_ref[0] = mm(one_hot, base_ref[0]).astype(BF)
    both = jnp.concatenate(
        [segments_ref[row, :].astype(F32), present_ref[row, :].astype(F32), jnp.zeros((6, length), F32)], axis=0
    ).astype(BF)
    along = mm_nt(both, one_hot)
    down = along.T
    slot = lax.broadcasted_iota(jnp.int32, (sel, sel), 0)
    seen = lax.broadcasted_iota(jnp.int32, (sel, sel), 1)
    open_key = (along[1:2, :] > 0.5) | (slot == seen)
    permitted = (seen <= slot) & (down[:, 0:1] == along[0:1, :]) & open_key
    bias_ref[0] = jnp.where(permitted, 0.0, -1e30)
    keep_ref[...] = down[:, 1:2]


def select(base, tables, mask=False, after=()):
    rows, length, half = base.shape
    sel = tables[0].shape[1]
    count = 1 + len(tables)
    kernel = pick_and_mask if mask else pick_rows

    def body(*refs):
        kernel(*refs[:count], *refs[count + len(after) :])

    outs = [shape((rows, sel, half)), shape((rows, sel, sel), F32), shape((rows * sel, 1), F32)]
    specs = [
        pl.BlockSpec((1, sel, half), lambda row: (row, 0, 0)),
        pl.BlockSpec((1, sel, sel), lambda row: (row, 0, 0)),
        pl.BlockSpec((sel, 1), lambda row: (row, 0)),
    ]
    return pl.pallas_call(
        body,
        grid=(rows,),
        out_shape=outs if mask else outs[:1],
        in_specs=[pl.BlockSpec((1, length, half), lambda row: (row, 0, 0))]
        + [pl.BlockSpec(v.shape, lambda row: (0, 0)) for v in tables]
        + [pl.BlockSpec(memory_space=pl.ANY)] * len(after),
        out_specs=specs if mask else specs[:1],
        compiler_params=pltpu.CompilerParams(vmem_limit_bytes=2 * VMEM_SPARE),
        cost_estimate=pl.CostEstimate(
            flops=2 * rows * sel * length * half, bytes_accessed=2 * base.size, transcendentals=0
        ),
        name="select_rows",
    )(base, *tables, *after)


def put_rows(bits_ref, chosen_ref, values_ref, base_ref, out_ref):
    long, half = out_ref.shape[1:]
    sel = values_ref.shape[0]
    first = pl.program_id(1) * long
    chosen = chosen_ref[pl.ds(pl.program_id(0), 1), :]
    hit = first + lax.broadcasted_iota(jnp.int32, (long, sel), 0) == chosen
    one_hot = jnp.where(hit, 1.0, 0.0).astype(BF)
    offset = pl.multiple_of(bits_ref[-1 + bits_ref.shape[0]] * half, half)
    values = values_ref[:, pl.ds(offset, half)]
    placed = mm(one_hot, jnp.concatenate([values, jnp.ones((sel, 128), BF)], axis=1))
    taken = placed[:, half:] > 0.5
    for at in range(0, half, 128):
        here = slice(at, at + 128)
        out_ref[0, :, here] = jnp.where(taken, placed[:, here].astype(BF), base_ref[0, :, here])


def put(base, chosen, values, bits, after=()):
    rows, length, half = base.shape
    sel = chosen.shape[1]
    long = length

    def body(*refs):
        put_rows(*refs[:4], refs[-2])
        refs[-1][...] = jnp.zeros_like(refs[-1])

    return pl.pallas_call(
        body,
        grid=(rows, length // long),
        out_shape=(shape(base.shape), shape((8, 128), F32)),
        in_specs=[
            pl.BlockSpec(memory_space=pltpu.SMEM),
            pl.BlockSpec(chosen.shape, lambda row, part: (0, 0)),
            pl.BlockSpec((sel, values.shape[1]), lambda row, part: (row, 0)),
            pl.BlockSpec((1, long, half), lambda row, part: (row, part, 0)),
        ]
        + [pl.BlockSpec(memory_space=pl.ANY)] * len(after),
        out_specs=[
            pl.BlockSpec((1, long, half), lambda row, part: (row, part, 0)),
            pl.BlockSpec((8, 128), lambda row, part: (0, 0)),
        ],
        compiler_params=pltpu.CompilerParams(vmem_limit_bytes=24 << 20),
        cost_estimate=pl.CostEstimate(
            flops=2 * rows * sel * length * half, bytes_accessed=4 * base.size, transcendentals=0
        ),
        name="put_rows",
    )(bits, chosen, values, base, *after)


def first_columns(attention_ref, mixing_ref, vectors_ref, out_ref):
    half = attention_ref.shape[2]
    for k in range(3):
        out_ref[:, k * half : (k + 1) * half] = attention_ref[k]
    out_ref[:, 3 * half : 4 * half] = mixing_ref[...]
    out_ref[:, 4 * half :] = vectors_ref[...]


def second_columns(cuts, expand_ref, contract_ref, out_ref):
    at = 0
    for start, end in cuts:
        out_ref[:, at : at + end - start] = expand_ref[:, start:end]
        at += end - start
        out_ref[:, at : at + end - start] = contract_ref[:, start:end]
        at += end - start


def untouched(*refs):
    pass


def tie(value, *others):
    if not others:
        return value
    anywhere = pl.BlockSpec(memory_space=pl.ANY)
    return pl.pallas_call(
        untouched,
        out_shape=jax.ShapeDtypeStruct(value.shape, value.dtype),
        in_specs=[anywhere] * (1 + len(others)),
        out_specs=anywhere,
        input_output_aliases={0: 0},
        compiler_params=pltpu.CompilerParams(vmem_limit_bytes=1 << 20),
        cost_estimate=pl.CostEstimate(flops=0, bytes_accessed=0, transcendentals=0),
    )(value, *others)


class Cube:
    def __init__(self, count):
        self.count, self.depth = count, count.bit_length() - 1
        index = lax.axis_index("dp").astype(jnp.int32)
        self.bits = jnp.append(
            (index >> jnp.arange(self.depth)) & 1, lax.axis_index("mp").astype(jnp.int32)
        )
        short = self.depth // 3
        self.x, self.y = list(range(short)), list(range(short, 2 * short))
        self.z = list(range(2 * short, self.depth))
        self.far = self.z[1:]
        near = [self.x, self.y, self.z[:1]]
        self.orders = [sum(near[k:] + near[:k], []) for k in range(3)]

    def swap(self, value, bit):
        return lax.ppermute(value, "dp", [(i, i ^ (1 << bit)) for i in range(self.count)])


class Part:
    def __init__(self, value, bits, sent=None, start=0, width=None):
        self.value, self.bits, self.sent = value, list(bits), sent
        self.start, self.width = start, width or value.shape[2]

    def columns(self, start, end):
        return Part(self.value, self.bits, self.sent, self.start + start, end - start)


def thirds(width):
    ends = [(k * width // 3 + 64) // 128 * 128 for k in range(4)]
    return list(zip(ends, ends[1:]))


def start_exchange(cube, part, bit):
    part.sent = cube.swap(part.value, bit)
    return part


def stack_parts(plan, bits_ref, *refs):
    ins, outs = refs[: 2 * len(plan)], refs[2 * len(plan) :]
    for k, (bit, blocks) in enumerate(plan):
        mine = bits_ref[bit]
        for block in range(blocks):
            outs[k][mine, block] = ins[2 * k][block]
            outs[k][1 - mine, block] = ins[2 * k + 1][block]


def stack(cube, parts, bits, after=()):
    outs, args, plan = [], [], []
    for part, bit in zip(parts, bits):
        outs.append(shape((2,) + part.value.shape))
        args += [part.value, part.sent]
        plan.append((bit, part.value.shape[0]))
    found = call(functools.partial(stack_parts, plan), outs, args, after, cube.bits, name="stack_parts")
    return [
        Part(v.reshape((-1,) + v.shape[2:]), [bit] + part.bits) for v, part, bit in zip(found, parts, bits)
    ]


def split_columns(plan, own_ref, *out_refs):
    for ref, (start, end) in zip(out_refs, plan):
        ref[...] = own_ref[:, :, start:end]


def whole_rows(plan, bits_ref, *refs):
    ins, out_ref = refs[:-1], refs[-1]
    column = 0
    for k, (bit, places, start, width) in enumerate(plan):
        mine = bits_ref[bit]
        for block, place in enumerate(places):
            here = slice(column, column + width)
            out_ref[place + (mine << bit), :, here] = ins[2 * k][block, :, start : start + width]
            out_ref[place + ((1 - mine) << bit), :, here] = ins[2 * k + 1][block, :, start : start + width]
        column += width


def whole(cube, parts, bits, after=()):
    args, plan, width = [], [], 0
    for part, bit in zip(parts, bits):
        places = []
        for block in range(part.value.shape[0]):
            digits = [(block >> k) & 1 for k in range(len(part.bits))][::-1]
            places.append(sum(digit << b for digit, b in zip(digits, part.bits)))
        args += [part.value, part.sent]
        plan.append((bit, places, part.start, part.width))
        width += part.width
    rows = parts[0].value.shape[1]
    (found,) = call(
        functools.partial(whole_rows, plan),
        (shape((cube.count, rows, width)),),
        args,
        after,
        cube.bits,
        name="whole_rows",
    )
    return found.reshape(-1, width)


def fold_parts(plan, bits_ref, *refs):
    refs = list(refs)
    taken = [[(refs.pop(0), refs.pop(0) if sent else None) for sent, _, _ in sources] for _, _, sources in plan]
    for (bit, (high, low), sources), ins in zip(plan, taken):
        sent_ref, kept_ref = refs.pop(0), refs.pop(0)
        mine = bits_ref[bit]
        column = 0
        for (_, start, width), (value_ref, other_ref) in zip(sources, ins):
            there = slice(start, start + width)
            here = slice(column, column + width)
            for a in range(high):
                for b in range(low):
                    for index, out_ref in ((1 - mine, sent_ref), (mine, kept_ref)):
                        found = value_ref[a, index, b, :, there].astype(F32)
                        if other_ref is not None:
                            found += other_ref[a, index, b, :, there].astype(F32)
                        out_ref[a * low + b, :, here] = found.astype(out_ref.dtype)
            column += width


def fold(cube, groups, bits, after=()):
    args, outs, plan = [], [], []
    for sources, bit in zip(groups, bits):
        at = sources[0].bits.index(bit)
        high, low = 1 << at, 1 << (len(sources[0].bits) - at - 1)
        listed = []
        for part in sources:
            for value in (part.value, part.sent):
                if value is not None:
                    args.append(value.reshape((high, 2, low) + value.shape[1:]))
            listed.append((part.sent is not None, part.start, part.width))
        plan.append((bit, (high, low), listed))
        dims = (high * low, sources[0].value.shape[1], sum(p.width for p in sources))
        outs += [shape(dims), shape(dims, F32)]
    found = call(functools.partial(fold_parts, plan), outs, args, after, cube.bits, name="fold_parts")
    done = []
    for k, (sources, bit) in enumerate(zip(groups, bits)):
        left = [b for b in sources[0].bits if b != bit]
        done.append(Part(found[2 * k + 1], left, cube.swap(found[2 * k], bit)))
    return done


def cut(cube, total):
    blocks = total.reshape(cube.count, -1, total.shape[1])
    bits = list(range(cube.depth))[::-1]
    return [Part(blocks, bits, None, start, end - start) for start, end in thirds(total.shape[1]) if end > start]


def arrived(parts):
    return [p.sent for p in parts]


def sum_first(value_ref, sent_ref, attention_ref, mixing_ref, vectors_ref):
    half = attention_ref.shape[2]
    total = value_ref[0] + sent_ref[0].astype(F32)
    for k in range(3):
        attention_ref[k] = total[:, k * half : (k + 1) * half]
    mixing_ref[...] = total[:, 3 * half : 4 * half]
    vectors_ref[...] = total[:, 4 * half :].T


def sum_second(cuts, value_ref, sent_ref, expand_ref, contract_ref):
    at = 0
    for start, end in cuts:
        for side in range(2):
            width = end - start
            total = value_ref[0, :, at : at + width] + sent_ref[0, :, at : at + width].astype(F32)
            (expand_ref if side else contract_ref)[:, start:end] = total
            at += width


def other_core(value):
    return lax.ppermute(value, "mp", [(0, 1), (1, 0)])


def both_halves(value):
    other = other_core(value)
    low = lax.axis_index("mp") == 0
    return jnp.concatenate([jnp.where(low, value, other), jnp.where(low, other, value)], axis=-1)


def shards(
    tokens,
    segments,
    present,
    chosen,
    attention,
    mixing,
    expand,
    contract,
    prenorm,
    midnorm,
    router,
    cotangent,
    count,
):
    cube = Cube(count)
    row_count, length, half_width = tokens.shape
    sel_count = chosen.shape[1]
    token_count = row_count * sel_count
    own_rows = mixing.shape[1]
    width = 2 * half_width
    hidden_here = expand.shape[1]
    heads_here = half_width // HD
    by_row = (row_count, sel_count)

    vectors = jnp.pad(jnp.stack([prenorm, midnorm, router], axis=1), ((0, 0), (0, 125)))
    cuts = thirds(hidden_here)
    (first_own,) = call(
        first_columns, (shape((own_rows, 4 * half_width + 128)),), (attention, mixing.T, vectors), name="first_columns"
    )
    first_far = start_exchange(cube, Part(first_own[None], []), cube.far[-1])
    (second_own,) = call(
        functools.partial(second_columns, cuts),
        (shape((own_rows, 2 * hidden_here)),),
        (expand, contract.T),
        name="second_columns",
    )
    picked, bias, keep = select(tokens, [chosen, segments, present], True)

    def spread(far, after, begin=()):
        for bit in cube.far[-2::-1]:
            far = start_exchange(cube, stack(cube, [far], [far_bit(far)], after)[0], bit)
        column = stack(cube, [far], [far_bit(far)], after)[0]
        ends = thirds(column.width)
        found = call(
            functools.partial(split_columns, ends),
            [shape(column.value.shape[:2] + (end - start,)) for start, end in ends],
            [column.value],
            begin,
            name="split_columns",
        )
        return [Part(v, column.bits) for v in found]

    def far_bit(part):
        return cube.far[-1 - len(part.bits)]

    def step_bits(step):
        return [order[step] for order in cube.orders]

    def send(parts, step):
        return [start_exchange(cube, p, bit) for p, bit in zip(parts, step_bits(step))]

    steps = len(cube.orders[0])
    first_parts = spread(first_far, [picked])
    states = both_halves(tie(picked, first_parts[0].value)).reshape(token_count, width)
    first_parts = send(first_parts, 0)
    second_far = start_exchange(cube, Part(tie(second_own, *arrived([first_far]))[None], []), cube.far[-1])
    for step in range(1, steps):
        if step == steps - 1:
            (picked_grads,) = select(cotangent, [chosen], False, [first_parts[0].value])
            after = arrived([second_far]) + [picked_grads]
        else:
            after = [states] if step == 1 else []
        first_parts = send(stack(cube, first_parts, step_bits(step - 1), after), step)
    first_last = [p.value for p in first_parts]
    first = whole(cube, first_parts, step_bits(steps - 1))
    mix = first[:, 3 * half_width : 4 * half_width]
    second_parts = send(spread(second_far, [], first_last[:1]), 0)
    second_begun = []
    for step in range(1, steps - 1):
        second_parts = stack(cube, second_parts, step_bits(step - 1), [first] if step == 1 else [])
        second_begun = second_begun or [p.value for p in second_parts]
        second_parts = send(second_parts, step)
    upstream = both_halves(tie(picked_grads, *second_begun)).reshape(token_count, width)
    second_parts = stack(cube, second_parts, step_bits(steps - 2))
    each = hidden_here // 3
    up_parts, down_parts = [], []
    for p in second_parts:
        up_parts.append(Part(p.value[..., :each], p.bits))
        down_parts.append(Part(p.value[..., each:], p.bits))
    up = whole(cube, send(up_parts, steps - 1), step_bits(steps - 1))
    down_parts = send(down_parts, steps - 1)

    wide = shape((token_count, width))
    tall = shape((token_count, hidden_here))
    vector = shape((8, width), F32)
    normed, packed, probs, context, gains = call(
        functools.partial(attention_forward, *by_row),
        (
            wide,
            shape((token_count, 3 * half_width)),
            shape((row_count, heads_here, sel_count, sel_count), F32),
            shape((token_count, half_width)),
            vector,
        ),
        (states, first, bias),
        after=second_begun,
        flops=token_count * width * half_width * 6,
        name="attention_forward",
    )
    (att_own,) = call(
        mix_forward, (wide,), (context, mix), flops=2 * token_count * width * half_width, name="mix_forward"
    )
    att_other = other_core(att_own)
    normed_mid, activated, slope, feed_grad, down_grad = call(
        functools.partial(up_forward, *by_row),
        (wide, tall, tall, wide, shape((width, hidden_here))),
        (states, upstream, att_own, att_other, up, gains, keep),
        flops=4 * token_count * width * hidden_here,
        name="up_forward",
    )
    down = whole(cube, down_parts, step_bits(steps - 1), [activated])

    hidden_grad, mid_own = call(
        down_backward,
        (tall, wide),
        (feed_grad, down, slope, up),
        flops=4 * token_count * width * hidden_here,
        name="down_backward",
    )
    up_grad, feed_own = call(
        down_forward,
        (shape((width, hidden_here)), wide),
        (normed_mid, hidden_grad, activated, down),
        flops=4 * token_count * width * hidden_here,
        name="down_forward",
    )
    feed_other = other_core(feed_own)
    mid_other = tie(other_core(mid_own), feed_own)

    def back_bits(step):
        return [order[-1 - step] for order in cube.orders]

    def alone(parts):
        return [[p] for p in parts]

    both_grads = [list(pair) for pair in zip(cut(cube, down_grad), cut(cube, up_grad))]
    both_grads = fold(cube, both_grads, back_bits(0))

    mixed, packed_grad, pre_own, middle_grad, mid_gain_grad = call(
        functools.partial(attention_backward, *by_row),
        (
            wide,
            shape((token_count, 3 * half_width)),
            wide,
            shape((token_count, width), F32),
            vector,
        ),
        (states, att_own, att_other, mid_own, mid_other, upstream, keep, gains, mix, first, packed, probs),
        after=[both_grads[0].value],
        scratch=[pltpu.VMEM((token_count, half_width), BF)],
        flops=10 * token_count * width * half_width,
        name="attention_backward",
    )
    (first_grad,) = call(
        projection_grads,
        (shape((width, 4 * half_width)),),
        (normed, packed_grad, mixed, context),
        flops=8 * token_count * width * half_width,
        name="projection_grads",
    )
    both_grads = fold(cube, alone(both_grads), back_bits(1), [first_grad])
    pre_other = other_core(tie(pre_own, both_grads[0].value))
    finished, logit_grad, router_grad = call(
        functools.partial(final_forward, *by_row),
        (wide, shape((token_count, 1), F32), vector),
        (states, upstream, att_own, att_other, feed_own, feed_other, gains, keep),
        after=[both_grads[0].value],
        name="final_forward",
    )
    total_grad, vector_grads = call(
        functools.partial(final_backward, *by_row),
        (wide, shape((width, 128))),
        (states, upstream, middle_grad, pre_own, pre_other, logit_grad, gains, mid_gain_grad, router_grad),
        scratch=[pltpu.VMEM((128, width), F32)],
        name="final_backward",
    )
    first_grads = alone(cut(cube, first_grad))
    first_grads[-1] += cut(cube, vector_grads)
    first_grads = fold(cube, first_grads, back_bits(0))
    result, done = put(tokens, chosen, finished, cube.bits, [first_grads[0].value])
    tokens_grad, _ = put(cotangent, chosen, total_grad, cube.bits, [done])
    for step in range(2, steps):
        both_grads = fold(cube, alone(both_grads), back_bits(step), [first_grad] if step == 2 else [])
    for step in range(1, steps):
        first_grads = fold(cube, alone(first_grads), back_bits(step), [done] if step == 1 else [])
    both_grads, first_grads = [both_grads], [first_grads]
    for bit in cube.far:
        both_grads = [fold(cube, both_grads, [bit])]
        first_grads = [fold(cube, first_grads, [bit])]
    (both_grad,), (first_grad,) = both_grads[0], first_grads[0]
    up_out, down_out = call(
        functools.partial(sum_second, cuts),
        (shape((own_rows, hidden_here), F32),) * 2,
        (both_grad.value, both_grad.sent),
        name="sum_second",
    )
    attention_out, mixing_out, vector_out = call(
        sum_first,
        (
            shape((3, own_rows, half_width), F32),
            shape((own_rows, half_width), F32),
            shape((128, own_rows), F32),
        ),
        (first_grad.value, first_grad.sent),
        name="sum_first",
    )
    return (
        result,
        tokens_grad,
        attention_out,
        mixing_out.T,
        up_out,
        down_out.T,
        vector_out[0],
        vector_out[1],
        vector_out[2],
    )


def solution(mesh):
    in_specs = (
        P("dp", None, "mp"),
        P("dp", None),
        P("dp", None),
        P("dp", None),
        P(None, "dp", "mp"),
        P("mp", "dp"),
        P("dp", "mp"),
        P("mp", "dp"),
        P("dp"),
        P("dp"),
        P("dp"),
        P("dp", None, "mp"),
    )
    out_specs = (
        P("dp", None, "mp"),
        P("dp", None, "mp"),
        P(None, "dp", "mp"),
        P("mp", "dp"),
        P("dp", "mp"),
        P("mp", "dp"),
        P("dp"),
        P("dp"),
        P("dp"),
    )
    count = mesh.shape["dp"]

    def body(*args):
        return shards(*args, count)

    return jax.shard_map(body, mesh=mesh, in_specs=in_specs, out_specs=out_specs, check_vma=False)
```

```python
import functools
import math

import jax
import jax.numpy as jnp
from jax import lax
from jax.experimental import pallas as pl
from jax.experimental.pallas import tpu as pltpu
from jax.sharding import PartitionSpec as P

HD = 64
EPSILON = 1e-06
BF = jnp.bfloat16
F32 = jnp.float32
VMEM_SPARE = 10 << 20


def mm(a, b):
    return jnp.dot(a, b, preferred_element_type=F32)


def mm_nt(a, b):
    return lax.dot_general(a, b, (((1,), (1,)), ((), ())), preferred_element_type=F32)


def mm_tn(a, b):
    return lax.dot_general(a, b, (((0,), (0,)), ((), ())), preferred_element_type=F32)


def inverse_rms(values):
    return lax.rsqrt(jnp.mean(values * values, axis=-1, keepdims=True) + EPSILON)


def call(kernel, outs, args, after=(), bits=None, scratch=(), flops=0, name=None):
    moved = sum(v.size * v.dtype.itemsize for v in (*args, *outs))
    scalars = [] if bits is None else [bits]
    count = len(scalars) + len(args)

    def body(*refs):
        kernel(*refs[:count], *refs[count + len(after) :])

    return pl.pallas_call(
        body,
        out_shape=outs,
        in_specs=[pl.BlockSpec(memory_space=pltpu.SMEM)] * len(scalars)
        + [pl.BlockSpec(memory_space=pltpu.VMEM)] * len(args)
        + [pl.BlockSpec(memory_space=pl.ANY)] * len(after),
        out_specs=[pl.BlockSpec(memory_space=pltpu.VMEM)] * len(outs),
        scratch_shapes=scratch,
        compiler_params=pltpu.CompilerParams(vmem_limit_bytes=VMEM_SPARE),
        cost_estimate=pl.CostEstimate(flops=flops, bytes_accessed=moved, transcendentals=0),
        name=name,
    )(*scalars, *args, *after)


def shape(dims, dtype=BF):
    return jax.ShapeDtypeStruct(tuple(dims), dtype)


def first_head(width=2 * HD):
    return lax.broadcasted_iota(jnp.int32, (1, width), 1) < HD


def attention_forward(rows, sel, states_ref, weights_ref, bias_ref, normed_ref, packed_ref, probs_ref, context_ref, gains_ref):
    width = states_ref.shape[1]
    half = context_ref.shape[1]
    gains_ref[...] = weights_ref[:, 4 * half :].astype(F32).T[:8]
    gain = gains_ref[0:1, :]
    scale = HD ** (-0.5)

    for row in range(rows):
        here = slice(row * sel, (row + 1) * sel)
        states = states_ref[here, :].astype(F32)
        normed_ref[here, :] = (states * inverse_rms(states) * gain).astype(BF)
    for start in range(0, 3 * half, 384):
        packed_ref[:, start : start + 384] = mm(normed_ref[...], weights_ref[:, start : start + 384]).astype(BF)
    first = first_head()

    @pl.loop(0, rows, unroll=True)
    def _(row):
        here = pl.ds(pl.multiple_of(row * sel, sel), sel)
        bias = bias_ref[row]
        for pair in range(half // (2 * HD)):
            at = pair * 2 * HD
            queries = packed_ref[here, at : at + 2 * HD]
            keys = packed_ref[here, half + at : half + at + 2 * HD]
            vals = packed_ref[here, 2 * half + at : 2 * half + at + 2 * HD]
            found = []
            for head in range(2):
                mine = first if head == 0 else ~first
                scores = mm_nt(jnp.where(mine, queries, jnp.zeros_like(queries)), keys) * scale + bias
                exponent = jnp.exp(scores - jnp.max(scores, axis=-1, keepdims=True))
                probs = exponent / jnp.sum(exponent, axis=-1, keepdims=True)
                probs_ref[row, 2 * pair + head] = probs
                found.append(mm(probs.astype(BF), vals))
            context_ref[here, at : at + 2 * HD] = jnp.where(first, found[0], found[1]).astype(BF)


def mix_forward(context_ref, mix_ref, out_ref):
    out_ref[...] = mm_nt(context_ref[...], mix_ref[...]).astype(BF)


def up_forward(
    rows, sel, states_ref, upstream_ref, own_ref, other_ref, up_ref, gains_ref, keep_ref,
    normed_ref, activated_ref, slope_ref, feed_grad_ref, grad_ref,
):
    mid_gain, router = gains_ref[1:2, :], gains_ref[2:3, :]
    c, a = (2.0 / math.pi) ** 0.5, 0.044715

    @pl.loop(0, rows)
    def _(row):
        here = pl.ds(pl.multiple_of(row * sel, sel), sel)
        states = states_ref[here, :].astype(F32)
        prob = jax.nn.sigmoid(jnp.sum(states * router, axis=-1, keepdims=True))
        gate = prob * keep_ref[here, :]
        feed_grad_ref[here, :] = (gate * upstream_ref[here, :].astype(F32)).astype(BF)
        middle = states + (own_ref[here, :].astype(F32) + other_ref[here, :].astype(F32))
        normed = (middle * inverse_rms(middle) * mid_gain).astype(BF)
        normed_ref[here, :] = normed

    upright_grad = feed_grad_ref[...].T
    chunk = 256
    for at in range(0, up_ref.shape[1], chunk):
        here = slice(at, at + chunk)
        hidden = mm(normed_ref[...], up_ref[:, here])
        square = hidden * hidden
        share = 0.5 * jnp.tanh(hidden * (c + c * a * square)) + 0.5
        activated = hidden * share
        activated_ref[:, here] = activated.astype(BF)
        slope = share + activated * (1.0 - share) * (2.0 * c + 6.0 * a * c * square)
        slope_ref[:, here] = slope.astype(BF)
        grad_ref[:, here] = mm(upright_grad, activated_ref[:, here]).astype(BF)


def down_backward(feed_grad_ref, down_ref, slope_ref, up_ref, hidden_grad_ref, out_ref):
    chunk = 256
    for at in range(0, down_ref.shape[1], chunk):
        here = slice(at, at + chunk)
        act_grad = mm(feed_grad_ref[...], down_ref[:, here])
        hidden_grad_ref[:, here] = (act_grad * slope_ref[:, here].astype(F32)).astype(BF)
    for at in range(0, out_ref.shape[1], chunk):
        here = slice(at, at + chunk)
        out_ref[:, here] = mm_nt(hidden_grad_ref[...], up_ref[here, :]).astype(BF)


def down_forward(normed_ref, hidden_grad_ref, activated_ref, down_ref, grad_ref, out_ref):
    upright_normed = normed_ref[...].T
    chunk = 256
    for at in range(0, grad_ref.shape[1], chunk):
        here = slice(at, at + chunk)
        grad_ref[:, here] = mm(upright_normed, hidden_grad_ref[:, here]).astype(BF)
    for at in range(0, out_ref.shape[1], chunk):
        here = slice(at, at + chunk)
        out_ref[:, here] = mm_nt(activated_ref[...], down_ref[here, :]).astype(BF)


def norm_backward(values, grads, gain):
    rho = inverse_rms(values)
    unit = values * rho
    scaled = grads * gain
    back = rho * (scaled - unit * jnp.mean(scaled * unit, axis=-1, keepdims=True))
    return back, jnp.sum(grads * unit, axis=0, keepdims=True)


def attention_backward(
    rows, sel, states_ref, own_ref, other_ref, mid_own_ref, mid_other_ref, upstream_ref, keep_ref, gains_ref,
    mix_ref, weights_ref, packed_ref, probs_ref,
    mixed_ref, packed_grad_ref, out_ref, middle_grad_ref, gain_grad_ref, context_grad_ref,
):
    mid_gain, router = gains_ref[1:2, :], gains_ref[2:3, :]
    half = mix_ref.shape[1]
    scale = HD ** (-0.5)
    gain_grad_ref[...] = jnp.zeros_like(gain_grad_ref)

    @pl.loop(0, rows)
    def _(row):
        here = pl.ds(pl.multiple_of(row * sel, sel), sel)
        states = states_ref[here, :].astype(F32)
        middle = states + (own_ref[here, :].astype(F32) + other_ref[here, :].astype(F32))
        mid_in = mid_own_ref[here, :].astype(F32) + mid_other_ref[here, :].astype(F32)
        middle_grad, gain_grad = norm_backward(middle, mid_in, mid_gain)
        gain_grad_ref[0:1, :] += gain_grad
        middle_grad_ref[here, :] = middle_grad
        gate = jax.nn.sigmoid(jnp.sum(states * router, axis=-1, keepdims=True)) * keep_ref[here, :]
        mixed = (gate * upstream_ref[here, :].astype(F32) + middle_grad).astype(BF)
        mixed_ref[here, :] = mixed

    context_grad_ref[...] = mm(mixed_ref[...], mix_ref[...]).astype(BF)
    first = first_head()

    @pl.loop(0, rows, unroll=True)
    def _(row):
        here = pl.ds(pl.multiple_of(row * sel, sel), sel)
        for pair in range(half // (2 * HD)):
            at = pair * 2 * HD
            queries = packed_ref[here, at : at + 2 * HD]
            keys = packed_ref[here, half + at : half + at + 2 * HD]
            vals = packed_ref[here, 2 * half + at : 2 * half + at + 2 * HD]
            grads = context_grad_ref[here, at : at + 2 * HD]
            queries_up, grads_up = queries.T, grads.T
            by_query, by_key, by_value = [], [], []
            for head in range(2):
                mine = first if head == 0 else ~first
                lanes = slice(head * HD, (head + 1) * HD)
                probs = probs_ref[row, 2 * pair + head]
                prob_grad = mm_nt(jnp.where(mine, grads, jnp.zeros_like(grads)), vals)
                centre = jnp.sum(probs * prob_grad, axis=-1, keepdims=True)
                score_grad = (probs * (prob_grad - centre)).astype(BF)
                by_query.append(mm(score_grad, keys))
                by_key.append(mm(queries_up[lanes], score_grad))
                by_value.append(mm(grads_up[lanes], probs.astype(BF)))
            packed_grad_ref[here, at : at + 2 * HD] = (
                jnp.where(first, by_query[0], by_query[1]) * scale
            ).astype(BF)
            packed_grad_ref[here, half + at : half + at + 2 * HD] = (
                (jnp.concatenate(by_key, axis=0) * scale).astype(BF).T
            )
            packed_grad_ref[here, 2 * half + at : 2 * half + at + 2 * HD] = (
                jnp.concatenate(by_value, axis=0).astype(BF).T
            )

    chunk = 256
    for at in range(0, out_ref.shape[1], chunk):
        here = slice(at, at + chunk)
        out_ref[:, here] = mm_nt(packed_grad_ref[...], weights_ref[here, : 3 * half]).astype(BF)


def projection_grads(normed_ref, packed_grad_ref, mixed_ref, context_ref, grad_ref):
    wide, chunk = packed_grad_ref.shape[1], 384
    upright_normed, upright_mixed = normed_ref[...].T, mixed_ref[...].T
    for at in range(0, wide, chunk):
        here = slice(at, at + chunk)
        grad_ref[:, here] = mm(upright_normed, packed_grad_ref[:, here]).astype(BF)
    grad_ref[:, wide:] = mm(upright_mixed, context_ref[...]).astype(BF)


def final_forward(
    rows, sel, states_ref, upstream_ref, own_ref, other_ref, feed_own_ref, feed_other_ref, gains_ref, keep_ref,
    finished_ref, logit_grad_ref, router_grad_ref,
):
    router = gains_ref[2:3, :]
    router_grad_ref[...] = jnp.zeros_like(router_grad_ref)

    @pl.loop(0, rows)
    def _(row):
        here = pl.ds(pl.multiple_of(row * sel, sel), sel)
        states = states_ref[here, :].astype(F32)
        attended = own_ref[here, :].astype(F32) + other_ref[here, :].astype(F32)
        branch = attended + (feed_own_ref[here, :].astype(F32) + feed_other_ref[here, :].astype(F32))
        prob = jax.nn.sigmoid(jnp.sum(states * router, axis=-1, keepdims=True))
        keep = keep_ref[here, :]
        finished_ref[here, :] = (states + prob * keep * branch).astype(BF)
        gate_grad = jnp.sum(upstream_ref[here, :].astype(F32) * branch, axis=-1, keepdims=True)
        logit_grad = gate_grad * keep * prob * (1.0 - prob)
        logit_grad_ref[here, :] = logit_grad
        router_grad_ref[0:1, :] += jnp.sum(logit_grad * states, axis=0, keepdims=True)


def final_backward(
    rows, sel, states_ref, upstream_ref, middle_grad_ref, pre_own_ref, pre_other_ref, logit_grad_ref, gains_ref,
    mid_gain_grad_ref, router_grad_ref, total_ref, vectors_ref, lines_ref,
):
    pre_gain, router = gains_ref[0:1, :], gains_ref[2:3, :]
    lines_ref[...] = jnp.zeros_like(lines_ref)
    lines_ref[1:2, :] = mid_gain_grad_ref[0:1, :]
    lines_ref[2:3, :] = router_grad_ref[0:1, :]

    @pl.loop(0, rows)
    def _(row):
        here = pl.ds(pl.multiple_of(row * sel, sel), sel)
        states = states_ref[here, :].astype(F32)
        pre_in = pre_own_ref[here, :].astype(F32) + pre_other_ref[here, :].astype(F32)
        back, gain_grad = norm_backward(states, pre_in, pre_gain)
        lines_ref[0:1, :] += gain_grad
        total = upstream_ref[here, :].astype(F32) + logit_grad_ref[here, :] * router
        total_ref[here, :] = (total + middle_grad_ref[here, :] + back).astype(BF)

    vectors_ref[...] = lines_ref[...].T.astype(BF)


def upright(row):
    return jnp.broadcast_to(row, (8, row.shape[1])).T[:, :1]


def one_hot_rows(chosen_ref, sel, length):
    row = pl.ds(pl.program_id(0), 1)
    chosen = upright(chosen_ref[row, :].astype(F32)).astype(jnp.int32)
    return jnp.where(chosen == lax.broadcasted_iota(jnp.int32, (sel, length), 1), 1.0, 0.0).astype(BF)


def pick_rows(base_ref, chosen_ref, picked_ref):
    one_hot = one_hot_rows(chosen_ref, picked_ref.shape[1], base_ref.shape[1])
    picked_ref[0] = mm(one_hot, base_ref[0]).astype(BF)


def pick_and_mask(base_ref, chosen_ref, segments_ref, present_ref, picked_ref, bias_ref, keep_ref):
    sel, length = picked_ref.shape[1], base_ref.shape[1]
    row = pl.ds(pl.program_id(0), 1)
    one_hot = one_hot_rows(chosen_ref, sel, length)
    picked_ref[0] = mm(one_hot, base_ref[0]).astype(BF)
    both = jnp.concatenate(
        [segments_ref[row, :].astype(F32), present_ref[row, :].astype(F32), jnp.zeros((6, length), F32)], axis=0
    ).astype(BF)
    along = mm_nt(both, one_hot)
    down = along.T
    slot = lax.broadcasted_iota(jnp.int32, (sel, sel), 0)
    seen = lax.broadcasted_iota(jnp.int32, (sel, sel), 1)
    open_key = (along[1:2, :] > 0.5) | (slot == seen)
    permitted = (seen <= slot) & (down[:, 0:1] == along[0:1, :]) & open_key
    bias_ref[0] = jnp.where(permitted, 0.0, -1e30)
    keep_ref[...] = down[:, 1:2]


def select(base, tables, mask=False, after=()):
    rows, length, half = base.shape
    sel = tables[0].shape[1]
    count = 1 + len(tables)
    kernel = pick_and_mask if mask else pick_rows

    def body(*refs):
        kernel(*refs[:count], *refs[count + len(after) :])

    outs = [shape((rows, sel, half)), shape((rows, sel, sel), F32), shape((rows * sel, 1), F32)]
    specs = [
        pl.BlockSpec((1, sel, half), lambda row: (row, 0, 0)),
        pl.BlockSpec((1, sel, sel), lambda row: (row, 0, 0)),
        pl.BlockSpec((sel, 1), lambda row: (row, 0)),
    ]
    return pl.pallas_call(
        body,
        grid=(rows,),
        out_shape=outs if mask else outs[:1],
        in_specs=[pl.BlockSpec((1, length, half), lambda row: (row, 0, 0))]
        + [pl.BlockSpec(v.shape, lambda row: (0, 0)) for v in tables]
        + [pl.BlockSpec(memory_space=pl.ANY)] * len(after),
        out_specs=specs if mask else specs[:1],
        compiler_params=pltpu.CompilerParams(vmem_limit_bytes=2 * VMEM_SPARE),
        cost_estimate=pl.CostEstimate(
            flops=2 * rows * sel * length * half, bytes_accessed=2 * base.size, transcendentals=0
        ),
        name="select_rows",
    )(base, *tables, *after)


def put_rows(bits_ref, chosen_ref, values_ref, base_ref, out_ref):
    long, half = out_ref.shape[1:]
    sel = values_ref.shape[0]
    first = pl.program_id(1) * long
    chosen = chosen_ref[pl.ds(pl.program_id(0), 1), :]
    hit = first + lax.broadcasted_iota(jnp.int32, (long, sel), 0) == chosen
    one_hot = jnp.where(hit, 1.0, 0.0).astype(BF)
    offset = pl.multiple_of(bits_ref[-1 + bits_ref.shape[0]] * half, half)
    values = values_ref[:, pl.ds(offset, half)]
    placed = mm(one_hot, jnp.concatenate([values, jnp.ones((sel, 128), BF)], axis=1))
    taken = placed[:, half:] > 0.5
    for at in range(0, half, 128):
        here = slice(at, at + 128)
        out_ref[0, :, here] = jnp.where(taken, placed[:, here].astype(BF), base_ref[0, :, here])


def put(base, chosen, values, bits, after=()):
    rows, length, half = base.shape
    sel = chosen.shape[1]
    long = length // 2

    def body(*refs):
        put_rows(*refs[:4], refs[-2])
        refs[-1][...] = jnp.zeros_like(refs[-1])

    return pl.pallas_call(
        body,
        grid=(rows, length // long),
        out_shape=(shape(base.shape), shape((8, 128), F32)),
        in_specs=[
            pl.BlockSpec(memory_space=pltpu.SMEM),
            pl.BlockSpec(chosen.shape, lambda row, part: (0, 0)),
            pl.BlockSpec((sel, values.shape[1]), lambda row, part: (row, 0)),
            pl.BlockSpec((1, long, half), lambda row, part: (row, part, 0)),
        ]
        + [pl.BlockSpec(memory_space=pl.ANY)] * len(after),
        out_specs=[
            pl.BlockSpec((1, long, half), lambda row, part: (row, part, 0)),
            pl.BlockSpec((8, 128), lambda row, part: (0, 0)),
        ],
        compiler_params=pltpu.CompilerParams(vmem_limit_bytes=24 << 20),
        cost_estimate=pl.CostEstimate(
            flops=2 * rows * sel * length * half, bytes_accessed=4 * base.size, transcendentals=0
        ),
        name="put_rows",
    )(bits, chosen, values, base, *after)


def first_columns(attention_ref, mixing_ref, vectors_ref, out_ref):
    half = attention_ref.shape[2]
    for k in range(3):
        out_ref[:, k * half : (k + 1) * half] = attention_ref[k]
    out_ref[:, 3 * half : 4 * half] = mixing_ref[...]
    out_ref[:, 4 * half :] = vectors_ref[...]


def second_columns(cuts, expand_ref, contract_ref, out_ref):
    at = 0
    for start, end in cuts:
        out_ref[:, at : at + end - start] = expand_ref[:, start:end]
        at += end - start
        out_ref[:, at : at + end - start] = contract_ref[:, start:end]
        at += end - start


def untouched(*refs):
    pass


def tie(value, *others):
    if not others:
        return value
    anywhere = pl.BlockSpec(memory_space=pl.ANY)
    return pl.pallas_call(
        untouched,
        out_shape=jax.ShapeDtypeStruct(value.shape, value.dtype),
        in_specs=[anywhere] * (1 + len(others)),
        out_specs=anywhere,
        input_output_aliases={0: 0},
        compiler_params=pltpu.CompilerParams(vmem_limit_bytes=1 << 20),
        cost_estimate=pl.CostEstimate(flops=0, bytes_accessed=0, transcendentals=0),
    )(value, *others)


class Cube:
    def __init__(self, count):
        self.count, self.depth = count, count.bit_length() - 1
        index = lax.axis_index("dp").astype(jnp.int32)
        self.bits = jnp.append(
            (index >> jnp.arange(self.depth)) & 1, lax.axis_index("mp").astype(jnp.int32)
        )
        short = self.depth // 3
        self.x, self.y = list(range(short)), list(range(short, 2 * short))
        self.z = list(range(2 * short, self.depth))
        self.far = self.z[1:]
        near = [self.x, self.y, self.z[:1]]
        self.orders = [sum(near[k:] + near[:k], []) for k in range(3)]

    def swap(self, value, bit):
        return lax.ppermute(value, "dp", [(i, i ^ (1 << bit)) for i in range(self.count)])


class Part:
    def __init__(self, value, bits, sent=None, start=0, width=None):
        self.value, self.bits, self.sent = value, list(bits), sent
        self.start, self.width = start, width or value.shape[2]

    def columns(self, start, end):
        return Part(self.value, self.bits, self.sent, self.start + start, end - start)


def thirds(width):
    ends = [(k * width // 3 + 64) // 128 * 128 for k in range(4)]
    return list(zip(ends, ends[1:]))


def start_exchange(cube, part, bit):
    part.sent = cube.swap(part.value, bit)
    return part


def stack_parts(plan, bits_ref, *refs):
    ins, outs = refs[: 2 * len(plan)], refs[2 * len(plan) :]
    for k, (bit, blocks) in enumerate(plan):
        mine = bits_ref[bit]
        for block in range(blocks):
            outs[k][mine, block] = ins[2 * k][block]
            outs[k][1 - mine, block] = ins[2 * k + 1][block]


def stack(cube, parts, bits, after=()):
    outs, args, plan = [], [], []
    for part, bit in zip(parts, bits):
        outs.append(shape((2,) + part.value.shape))
        args += [part.value, part.sent]
        plan.append((bit, part.value.shape[0]))
    found = call(functools.partial(stack_parts, plan), outs, args, after, cube.bits, name="stack_parts")
    return [
        Part(v.reshape((-1,) + v.shape[2:]), [bit] + part.bits) for v, part, bit in zip(found, parts, bits)
    ]


def split_columns(plan, own_ref, *out_refs):
    for ref, (start, end) in zip(out_refs, plan):
        ref[...] = own_ref[:, :, start:end]


def whole_rows(plan, bits_ref, *refs):
    ins, out_ref = refs[:-1], refs[-1]
    column = 0
    for k, (bit, places, start, width) in enumerate(plan):
        mine = bits_ref[bit]
        for block, place in enumerate(places):
            here = slice(column, column + width)
            out_ref[place + (mine << bit), :, here] = ins[2 * k][block, :, start : start + width]
            out_ref[place + ((1 - mine) << bit), :, here] = ins[2 * k + 1][block, :, start : start + width]
        column += width


def whole(cube, parts, bits, after=()):
    args, plan, width = [], [], 0
    for part, bit in zip(parts, bits):
        places = []
        for block in range(part.value.shape[0]):
            digits = [(block >> k) & 1 for k in range(len(part.bits))][::-1]
            places.append(sum(digit << b for digit, b in zip(digits, part.bits)))
        args += [part.value, part.sent]
        plan.append((bit, places, part.start, part.width))
        width += part.width
    rows = parts[0].value.shape[1]
    (found,) = call(
        functools.partial(whole_rows, plan),
        (shape((cube.count, rows, width)),),
        args,
        after,
        cube.bits,
        name="whole_rows",
    )
    return found.reshape(-1, width)


def fold_parts(plan, bits_ref, *refs):
    refs = list(refs)
    taken = [[(refs.pop(0), refs.pop(0) if sent else None) for sent, _, _ in sources] for _, _, sources in plan]
    for (bit, (high, low), sources), ins in zip(plan, taken):
        sent_ref, kept_ref = refs.pop(0), refs.pop(0)
        mine = bits_ref[bit]
        column = 0
        for (_, start, width), (value_ref, other_ref) in zip(sources, ins):
            there = slice(start, start + width)
            here = slice(column, column + width)
            for a in range(high):
                for b in range(low):
                    for index, out_ref in ((1 - mine, sent_ref), (mine, kept_ref)):
                        found = value_ref[a, index, b, :, there].astype(F32)
                        if other_ref is not None:
                            found += other_ref[a, index, b, :, there].astype(F32)
                        out_ref[a * low + b, :, here] = found.astype(out_ref.dtype)
            column += width


def fold(cube, groups, bits, after=()):
    args, outs, plan = [], [], []
    for sources, bit in zip(groups, bits):
        at = sources[0].bits.index(bit)
        high, low = 1 << at, 1 << (len(sources[0].bits) - at - 1)
        listed = []
        for part in sources:
            for value in (part.value, part.sent):
                if value is not None:
                    args.append(value.reshape((high, 2, low) + value.shape[1:]))
            listed.append((part.sent is not None, part.start, part.width))
        plan.append((bit, (high, low), listed))
        dims = (high * low, sources[0].value.shape[1], sum(p.width for p in sources))
        outs += [shape(dims), shape(dims, F32)]
    found = call(functools.partial(fold_parts, plan), outs, args, after, cube.bits, name="fold_parts")
    done = []
    for k, (sources, bit) in enumerate(zip(groups, bits)):
        left = [b for b in sources[0].bits if b != bit]
        done.append(Part(found[2 * k + 1], left, cube.swap(found[2 * k], bit)))
    return done


def cut(cube, total):
    blocks = total.reshape(cube.count, -1, total.shape[1])
    bits = list(range(cube.depth))[::-1]
    return [Part(blocks, bits, None, start, end - start) for start, end in thirds(total.shape[1]) if end > start]


def arrived(parts):
    return [p.sent for p in parts]


def sum_first(value_ref, sent_ref, attention_ref, mixing_ref, vectors_ref):
    half = attention_ref.shape[2]
    total = value_ref[0] + sent_ref[0].astype(F32)
    for k in range(3):
        attention_ref[k] = total[:, k * half : (k + 1) * half]
    mixing_ref[...] = total[:, 3 * half : 4 * half]
    vectors_ref[...] = total[:, 4 * half :].T


def sum_second(cuts, value_ref, sent_ref, expand_ref, contract_ref):
    at = 0
    for start, end in cuts:
        for side in range(2):
            width = end - start
            total = value_ref[0, :, at : at + width] + sent_ref[0, :, at : at + width].astype(F32)
            (expand_ref if side else contract_ref)[:, start:end] = total
            at += width


def other_core(value):
    return lax.ppermute(value, "mp", [(0, 1), (1, 0)])


def both_halves(value):
    other = other_core(value)
    low = lax.axis_index("mp") == 0
    return jnp.concatenate([jnp.where(low, value, other), jnp.where(low, other, value)], axis=-1)


def shards(
    tokens,
    segments,
    present,
    chosen,
    attention,
    mixing,
    expand,
    contract,
    prenorm,
    midnorm,
    router,
    cotangent,
    count,
):
    cube = Cube(count)
    row_count, length, half_width = tokens.shape
    sel_count = chosen.shape[1]
    token_count = row_count * sel_count
    own_rows = mixing.shape[1]
    width = 2 * half_width
    hidden_here = expand.shape[1]
    heads_here = half_width // HD
    by_row = (row_count, sel_count)

    vectors = jnp.pad(jnp.stack([prenorm, midnorm, router], axis=1), ((0, 0), (0, 125)))
    cuts = thirds(hidden_here)
    (first_own,) = call(
        first_columns, (shape((own_rows, 4 * half_width + 128)),), (attention, mixing.T, vectors), name="first_columns"
    )
    first_far = start_exchange(cube, Part(first_own[None], []), cube.far[-1])
    (second_own,) = call(
        functools.partial(second_columns, cuts),
        (shape((own_rows, 2 * hidden_here)),),
        (expand, contract.T),
        name="second_columns",
    )
    picked, bias, keep = select(tokens, [chosen, segments, present], True)

    def spread(far, after, begin=()):
        for bit in cube.far[-2::-1]:
            far = start_exchange(cube, stack(cube, [far], [far_bit(far)], after)[0], bit)
        column = stack(cube, [far], [far_bit(far)], after)[0]
        ends = thirds(column.width)
        found = call(
            functools.partial(split_columns, ends),
            [shape(column.value.shape[:2] + (end - start,)) for start, end in ends],
            [column.value],
            begin,
            name="split_columns",
        )
        return [Part(v, column.bits) for v in found]

    def far_bit(part):
        return cube.far[-1 - len(part.bits)]

    def step_bits(step):
        return [order[step] for order in cube.orders]

    def send(parts, step):
        return [start_exchange(cube, p, bit) for p, bit in zip(parts, step_bits(step))]

    steps = len(cube.orders[0])
    first_parts = spread(first_far, [picked])
    states = both_halves(tie(picked, first_parts[0].value)).reshape(token_count, width)
    first_parts = send(first_parts, 0)
    second_far = start_exchange(cube, Part(tie(second_own, *arrived([first_far]))[None], []), cube.far[-1])
    for step in range(1, steps):
        if step == steps - 1:
            (picked_grads,) = select(cotangent, [chosen], False, [first_parts[0].value])
            after = arrived([second_far]) + [picked_grads]
        else:
            after = [states] if step == 1 else []
        first_parts = send(stack(cube, first_parts, step_bits(step - 1), after), step)
    first_last = [p.value for p in first_parts]
    first = whole(cube, first_parts, step_bits(steps - 1))
    mix = first[:, 3 * half_width : 4 * half_width]
    second_parts = send(spread(second_far, [], first_last[:1]), 0)
    second_begun = []
    for step in range(1, steps - 1):
        second_parts = stack(cube, second_parts, step_bits(step - 1), [first] if step == 1 else [])
        second_begun = second_begun or [p.value for p in second_parts]
        second_parts = send(second_parts, step)
    upstream = both_halves(tie(picked_grads, *second_begun)).reshape(token_count, width)
    second_parts = stack(cube, second_parts, step_bits(steps - 2))
    each = hidden_here // 3
    up_parts, down_parts = [], []
    for p in second_parts:
        up_parts.append(Part(p.value[..., :each], p.bits))
        down_parts.append(Part(p.value[..., each:], p.bits))
    up = whole(cube, send(up_parts, steps - 1), step_bits(steps - 1))
    down_parts = send(down_parts, steps - 1)

    wide = shape((token_count, width))
    tall = shape((token_count, hidden_here))
    vector = shape((8, width), F32)
    normed, packed, probs, context, gains = call(
        functools.partial(attention_forward, *by_row),
        (
            wide,
            shape((token_count, 3 * half_width)),
            shape((row_count, heads_here, sel_count, sel_count), F32),
            shape((token_count, half_width)),
            vector,
        ),
        (states, first, bias),
        after=second_begun,
        flops=token_count * width * half_width * 6,
        name="attention_forward",
    )
    (att_own,) = call(
        mix_forward, (wide,), (context, mix), flops=2 * token_count * width * half_width, name="mix_forward"
    )
    att_other = other_core(att_own)
    normed_mid, activated, slope, feed_grad, down_grad = call(
        functools.partial(up_forward, *by_row),
        (wide, tall, tall, wide, shape((width, hidden_here))),
        (states, upstream, att_own, att_other, up, gains, keep),
        flops=4 * token_count * width * hidden_here,
        name="up_forward",
    )
    down = whole(cube, down_parts, step_bits(steps - 1), [activated])

    hidden_grad, mid_own = call(
        down_backward,
        (tall, wide),
        (feed_grad, down, slope, up),
        flops=4 * token_count * width * hidden_here,
        name="down_backward",
    )
    up_grad, feed_own = call(
        down_forward,
        (shape((width, hidden_here)), wide),
        (normed_mid, hidden_grad, activated, down),
        flops=4 * token_count * width * hidden_here,
        name="down_forward",
    )
    feed_other = other_core(feed_own)
    mid_other = tie(other_core(mid_own), feed_own)

    def back_bits(step):
        return [order[-1 - step] for order in cube.orders]

    def alone(parts):
        return [[p] for p in parts]

    both_grads = [list(pair) for pair in zip(cut(cube, down_grad), cut(cube, up_grad))]
    both_grads = fold(cube, both_grads, back_bits(0))

    mixed, packed_grad, pre_own, middle_grad, mid_gain_grad = call(
        functools.partial(attention_backward, *by_row),
        (
            wide,
            shape((token_count, 3 * half_width)),
            wide,
            shape((token_count, width), F32),
            vector,
        ),
        (states, att_own, att_other, mid_own, mid_other, upstream, keep, gains, mix, first, packed, probs),
        after=[both_grads[0].value],
        scratch=[pltpu.VMEM((token_count, half_width), BF)],
        flops=10 * token_count * width * half_width,
        name="attention_backward",
    )
    (first_grad,) = call(
        projection_grads,
        (shape((width, 4 * half_width)),),
        (normed, packed_grad, mixed, context),
        flops=8 * token_count * width * half_width,
        name="projection_grads",
    )
    both_grads = fold(cube, alone(both_grads), back_bits(1), [first_grad])
    pre_other = other_core(tie(pre_own, both_grads[0].value))
    finished, logit_grad, router_grad = call(
        functools.partial(final_forward, *by_row),
        (wide, shape((token_count, 1), F32), vector),
        (states, upstream, att_own, att_other, feed_own, feed_other, gains, keep),
        after=[both_grads[0].value],
        name="final_forward",
    )
    total_grad, vector_grads = call(
        functools.partial(final_backward, *by_row),
        (wide, shape((width, 128))),
        (states, upstream, middle_grad, pre_own, pre_other, logit_grad, gains, mid_gain_grad, router_grad),
        scratch=[pltpu.VMEM((128, width), F32)],
        name="final_backward",
    )
    first_grads = alone(cut(cube, first_grad))
    first_grads[-1] += cut(cube, vector_grads)
    first_grads = fold(cube, first_grads, back_bits(0))
    result, done = put(tokens, chosen, finished, cube.bits, [first_grads[0].value])
    tokens_grad, _ = put(cotangent, chosen, total_grad, cube.bits, [done])
    for step in range(2, steps):
        both_grads = fold(cube, alone(both_grads), back_bits(step), [first_grad] if step == 2 else [])
    for step in range(1, steps):
        first_grads = fold(cube, alone(first_grads), back_bits(step), [done] if step == 1 else [])
    both_grads, first_grads = [both_grads], [first_grads]
    for bit in cube.far:
        both_grads = [fold(cube, both_grads, [bit])]
        first_grads = [fold(cube, first_grads, [bit])]
    (both_grad,), (first_grad,) = both_grads[0], first_grads[0]
    up_out, down_out = call(
        functools.partial(sum_second, cuts),
        (shape((own_rows, hidden_here), F32),) * 2,
        (both_grad.value, both_grad.sent),
        name="sum_second",
    )
    attention_out, mixing_out, vector_out = call(
        sum_first,
        (
            shape((3, own_rows, half_width), F32),
            shape((own_rows, half_width), F32),
            shape((128, own_rows), F32),
        ),
        (first_grad.value, first_grad.sent),
        name="sum_first",
    )
    return (
        result,
        tokens_grad,
        attention_out,
        mixing_out.T,
        up_out,
        down_out.T,
        vector_out[0],
        vector_out[1],
        vector_out[2],
    )


def solution(mesh):
    in_specs = (
        P("dp", None, "mp"),
        P("dp", None),
        P("dp", None),
        P("dp", None),
        P(None, "dp", "mp"),
        P("mp", "dp"),
        P("dp", "mp"),
        P("mp", "dp"),
        P("dp"),
        P("dp"),
        P("dp"),
        P("dp", None, "mp"),
    )
    out_specs = (
        P("dp", None, "mp"),
        P("dp", None, "mp"),
        P(None, "dp", "mp"),
        P("mp", "dp"),
        P("dp", "mp"),
        P("mp", "dp"),
        P("dp"),
        P("dp"),
        P("dp"),
    )
    count = mesh.shape["dp"]

    def body(*args):
        return shards(*args, count)

    return jax.shard_map(body, mesh=mesh, in_specs=in_specs, out_specs=out_specs, check_vma=False)
```

```python
import functools
import math

import jax
import jax.numpy as jnp
from jax import lax
from jax.experimental import pallas as pl
from jax.experimental.pallas import tpu as pltpu
from jax.sharding import PartitionSpec as P

HD = 64
EPSILON = 1e-06
BF = jnp.bfloat16
F32 = jnp.float32
VMEM_SPARE = 10 << 20


def mm(a, b):
    return jnp.dot(a, b, preferred_element_type=F32)


def mm_nt(a, b):
    return lax.dot_general(a, b, (((1,), (1,)), ((), ())), preferred_element_type=F32)


def mm_tn(a, b):
    return lax.dot_general(a, b, (((0,), (0,)), ((), ())), preferred_element_type=F32)


def inverse_rms(values):
    return lax.rsqrt(jnp.mean(values * values, axis=-1, keepdims=True) + EPSILON)


def call(kernel, outs, args, after=(), bits=None, scratch=(), flops=0, name=None):
    moved = sum(v.size * v.dtype.itemsize for v in (*args, *outs))
    scalars = [] if bits is None else [bits]
    count = len(scalars) + len(args)

    def body(*refs):
        kernel(*refs[:count], *refs[count + len(after) :])

    return pl.pallas_call(
        body,
        out_shape=outs,
        in_specs=[pl.BlockSpec(memory_space=pltpu.SMEM)] * len(scalars)
        + [pl.BlockSpec(memory_space=pltpu.VMEM)] * len(args)
        + [pl.BlockSpec(memory_space=pl.ANY)] * len(after),
        out_specs=[pl.BlockSpec(memory_space=pltpu.VMEM)] * len(outs),
        scratch_shapes=scratch,
        compiler_params=pltpu.CompilerParams(vmem_limit_bytes=VMEM_SPARE),
        cost_estimate=pl.CostEstimate(flops=flops, bytes_accessed=moved, transcendentals=0),
        name=name,
    )(*scalars, *args, *after)


def shape(dims, dtype=BF):
    return jax.ShapeDtypeStruct(tuple(dims), dtype)


def first_head(width=2 * HD):
    return lax.broadcasted_iota(jnp.int32, (1, width), 1) < HD


def attention_forward(rows, sel, states_ref, weights_ref, bias_ref, normed_ref, packed_ref, probs_ref, context_ref, gains_ref):
    width = states_ref.shape[1]
    half = context_ref.shape[1]
    gains_ref[...] = weights_ref[:, 4 * half :].astype(F32).T[:8]
    gain = gains_ref[0:1, :]
    scale = HD ** (-0.5)

    for row in range(rows):
        here = slice(row * sel, (row + 1) * sel)
        states = states_ref[here, :].astype(F32)
        normed_ref[here, :] = (states * inverse_rms(states) * gain).astype(BF)
    for start in range(0, 3 * half, 384):
        packed_ref[:, start : start + 384] = mm(normed_ref[...], weights_ref[:, start : start + 384]).astype(BF)
    first = first_head()

    @pl.loop(0, rows, unroll=True)
    def _(row):
        here = pl.ds(pl.multiple_of(row * sel, sel), sel)
        bias = bias_ref[row]
        for pair in range(half // (2 * HD)):
            at = pair * 2 * HD
            queries = packed_ref[here, at : at + 2 * HD]
            keys = packed_ref[here, half + at : half + at + 2 * HD]
            vals = packed_ref[here, 2 * half + at : 2 * half + at + 2 * HD]
            found = []
            for head in range(2):
                mine = first if head == 0 else ~first
                scores = mm_nt(jnp.where(mine, queries, jnp.zeros_like(queries)), keys) * scale + bias
                exponent = jnp.exp(scores - jnp.max(scores, axis=-1, keepdims=True))
                probs = exponent / jnp.sum(exponent, axis=-1, keepdims=True)
                probs_ref[row, 2 * pair + head] = probs
                found.append(mm(probs.astype(BF), vals))
            context_ref[here, at : at + 2 * HD] = jnp.where(first, found[0], found[1]).astype(BF)


def mix_forward(context_ref, mix_ref, out_ref):
    out_ref[...] = mm_nt(context_ref[...], mix_ref[...]).astype(BF)


def up_forward(
    rows, sel, states_ref, upstream_ref, own_ref, other_ref, up_ref, gains_ref, keep_ref,
    normed_ref, activated_ref, slope_ref, feed_grad_ref, grad_ref,
):
    mid_gain, router = gains_ref[1:2, :], gains_ref[2:3, :]
    c, a = (2.0 / math.pi) ** 0.5, 0.044715

    @pl.loop(0, rows)
    def _(row):
        here = pl.ds(pl.multiple_of(row * sel, sel), sel)
        states = states_ref[here, :].astype(F32)
        prob = jax.nn.sigmoid(jnp.sum(states * router, axis=-1, keepdims=True))
        gate = prob * keep_ref[here, :]
        feed_grad_ref[here, :] = (gate * upstream_ref[here, :].astype(F32)).astype(BF)
        middle = states + (own_ref[here, :].astype(F32) + other_ref[here, :].astype(F32))
        normed = (middle * inverse_rms(middle) * mid_gain).astype(BF)
        normed_ref[here, :] = normed

    upright_grad = feed_grad_ref[...].T
    chunk = 256
    for at in range(0, up_ref.shape[1], chunk):
        here = slice(at, at + chunk)
        hidden = mm(normed_ref[...], up_ref[:, here])
        square = hidden * hidden
        share = 0.5 * jnp.tanh(hidden * (c + c * a * square)) + 0.5
        activated = hidden * share
        activated_ref[:, here] = activated.astype(BF)
        slope = share + activated * (1.0 - share) * (2.0 * c + 6.0 * a * c * square)
        slope_ref[:, here] = slope.astype(BF)
        grad_ref[:, here] = mm(upright_grad, activated_ref[:, here]).astype(BF)


def down_backward(feed_grad_ref, down_ref, slope_ref, up_ref, hidden_grad_ref, out_ref):
    chunk = 256
    for at in range(0, down_ref.shape[1], chunk):
        here = slice(at, at + chunk)
        act_grad = mm(feed_grad_ref[...], down_ref[:, here])
        hidden_grad_ref[:, here] = (act_grad * slope_ref[:, here].astype(F32)).astype(BF)
    for at in range(0, out_ref.shape[1], chunk):
        here = slice(at, at + chunk)
        out_ref[:, here] = mm_nt(hidden_grad_ref[...], up_ref[here, :]).astype(BF)


def down_forward(normed_ref, hidden_grad_ref, activated_ref, down_ref, grad_ref, out_ref):
    upright_normed = normed_ref[...].T
    chunk = 256
    for at in range(0, grad_ref.shape[1], chunk):
        here = slice(at, at + chunk)
        grad_ref[:, here] = mm(upright_normed, hidden_grad_ref[:, here]).astype(BF)
    for at in range(0, out_ref.shape[1], chunk):
        here = slice(at, at + chunk)
        out_ref[:, here] = mm_nt(activated_ref[...], down_ref[here, :]).astype(BF)


def norm_backward(values, grads, gain):
    rho = inverse_rms(values)
    unit = values * rho
    scaled = grads * gain
    back = rho * (scaled - unit * jnp.mean(scaled * unit, axis=-1, keepdims=True))
    return back, jnp.sum(grads * unit, axis=0, keepdims=True)


def attention_backward(
    rows, sel, states_ref, own_ref, other_ref, mid_own_ref, mid_other_ref, upstream_ref, keep_ref, gains_ref,
    mix_ref, weights_ref, packed_ref, probs_ref,
    mixed_ref, packed_grad_ref, out_ref, middle_grad_ref, gain_grad_ref, context_grad_ref,
):
    mid_gain, router = gains_ref[1:2, :], gains_ref[2:3, :]
    half = mix_ref.shape[1]
    scale = HD ** (-0.5)
    gain_grad_ref[...] = jnp.zeros_like(gain_grad_ref)

    @pl.loop(0, rows)
    def _(row):
        here = pl.ds(pl.multiple_of(row * sel, sel), sel)
        states = states_ref[here, :].astype(F32)
        middle = states + (own_ref[here, :].astype(F32) + other_ref[here, :].astype(F32))
        mid_in = mid_own_ref[here, :].astype(F32) + mid_other_ref[here, :].astype(F32)
        middle_grad, gain_grad = norm_backward(middle, mid_in, mid_gain)
        gain_grad_ref[0:1, :] += gain_grad
        middle_grad_ref[here, :] = middle_grad
        gate = jax.nn.sigmoid(jnp.sum(states * router, axis=-1, keepdims=True)) * keep_ref[here, :]
        mixed = (gate * upstream_ref[here, :].astype(F32) + middle_grad).astype(BF)
        mixed_ref[here, :] = mixed

    context_grad_ref[...] = mm(mixed_ref[...], mix_ref[...]).astype(BF)
    first = first_head()

    @pl.loop(0, rows, unroll=True)
    def _(row):
        here = pl.ds(pl.multiple_of(row * sel, sel), sel)
        for pair in range(half // (2 * HD)):
            at = pair * 2 * HD
            queries = packed_ref[here, at : at + 2 * HD]
            keys = packed_ref[here, half + at : half + at + 2 * HD]
            vals = packed_ref[here, 2 * half + at : 2 * half + at + 2 * HD]
            grads = context_grad_ref[here, at : at + 2 * HD]
            queries_up, grads_up = queries.T, grads.T
            by_query, by_key, by_value = [], [], []
            for head in range(2):
                mine = first if head == 0 else ~first
                lanes = slice(head * HD, (head + 1) * HD)
                probs = probs_ref[row, 2 * pair + head]
                prob_grad = mm_nt(jnp.where(mine, grads, jnp.zeros_like(grads)), vals)
                centre = jnp.sum(probs * prob_grad, axis=-1, keepdims=True)
                score_grad = (probs * (prob_grad - centre)).astype(BF)
                by_query.append(mm(score_grad, keys))
                by_key.append(mm(queries_up[lanes], score_grad))
                by_value.append(mm(grads_up[lanes], probs.astype(BF)))
            packed_grad_ref[here, at : at + 2 * HD] = (
                jnp.where(first, by_query[0], by_query[1]) * scale
            ).astype(BF)
            packed_grad_ref[here, half + at : half + at + 2 * HD] = (
                (jnp.concatenate(by_key, axis=0) * scale).astype(BF).T
            )
            packed_grad_ref[here, 2 * half + at : 2 * half + at + 2 * HD] = (
                jnp.concatenate(by_value, axis=0).astype(BF).T
            )

    chunk = 256
    for at in range(0, out_ref.shape[1], chunk):
        here = slice(at, at + chunk)
        out_ref[:, here] = mm_nt(packed_grad_ref[...], weights_ref[here, : 3 * half]).astype(BF)


def projection_grads(normed_ref, packed_grad_ref, mixed_ref, context_ref, grad_ref):
    wide, chunk = packed_grad_ref.shape[1], 384
    upright_normed, upright_mixed = normed_ref[...].T, mixed_ref[...].T
    for at in range(0, wide, chunk):
        here = slice(at, at + chunk)
        grad_ref[:, here] = mm(upright_normed, packed_grad_ref[:, here]).astype(BF)
    grad_ref[:, wide:] = mm(upright_mixed, context_ref[...]).astype(BF)


def final_forward(
    rows, sel, states_ref, upstream_ref, own_ref, other_ref, feed_own_ref, feed_other_ref, gains_ref, keep_ref,
    finished_ref, logit_grad_ref, router_grad_ref,
):
    router = gains_ref[2:3, :]
    router_grad_ref[...] = jnp.zeros_like(router_grad_ref)

    @pl.loop(0, rows)
    def _(row):
        here = pl.ds(pl.multiple_of(row * sel, sel), sel)
        states = states_ref[here, :].astype(F32)
        attended = own_ref[here, :].astype(F32) + other_ref[here, :].astype(F32)
        branch = attended + (feed_own_ref[here, :].astype(F32) + feed_other_ref[here, :].astype(F32))
        prob = jax.nn.sigmoid(jnp.sum(states * router, axis=-1, keepdims=True))
        keep = keep_ref[here, :]
        finished_ref[here, :] = (states + prob * keep * branch).astype(BF)
        gate_grad = jnp.sum(upstream_ref[here, :].astype(F32) * branch, axis=-1, keepdims=True)
        logit_grad = gate_grad * keep * prob * (1.0 - prob)
        logit_grad_ref[here, :] = logit_grad
        router_grad_ref[0:1, :] += jnp.sum(logit_grad * states, axis=0, keepdims=True)


def final_backward(
    rows, sel, states_ref, upstream_ref, middle_grad_ref, pre_own_ref, pre_other_ref, logit_grad_ref, gains_ref,
    mid_gain_grad_ref, router_grad_ref, total_ref, vectors_ref, lines_ref,
):
    pre_gain, router = gains_ref[0:1, :], gains_ref[2:3, :]
    lines_ref[...] = jnp.zeros_like(lines_ref)
    lines_ref[1:2, :] = mid_gain_grad_ref[0:1, :]
    lines_ref[2:3, :] = router_grad_ref[0:1, :]

    @pl.loop(0, rows)
    def _(row):
        here = pl.ds(pl.multiple_of(row * sel, sel), sel)
        states = states_ref[here, :].astype(F32)
        pre_in = pre_own_ref[here, :].astype(F32) + pre_other_ref[here, :].astype(F32)
        back, gain_grad = norm_backward(states, pre_in, pre_gain)
        lines_ref[0:1, :] += gain_grad
        total = upstream_ref[here, :].astype(F32) + logit_grad_ref[here, :] * router
        total_ref[here, :] = (total + middle_grad_ref[here, :] + back).astype(BF)

    vectors_ref[...] = lines_ref[...].T.astype(BF)


def upright(row):
    return jnp.broadcast_to(row, (8, row.shape[1])).T[:, :1]


def one_hot_rows(chosen_ref, sel, length):
    row = pl.ds(pl.program_id(0), 1)
    chosen = upright(chosen_ref[row, :].astype(F32)).astype(jnp.int32)
    return jnp.where(chosen == lax.broadcasted_iota(jnp.int32, (sel, length), 1), 1.0, 0.0).astype(BF)


def pick_rows(base_ref, chosen_ref, picked_ref):
    one_hot = one_hot_rows(chosen_ref, picked_ref.shape[1], base_ref.shape[1])
    picked_ref[0] = mm(one_hot, base_ref[0]).astype(BF)


def pick_and_mask(base_ref, chosen_ref, segments_ref, present_ref, picked_ref, bias_ref, keep_ref):
    sel, length = picked_ref.shape[1], base_ref.shape[1]
    row = pl.ds(pl.program_id(0), 1)
    one_hot = one_hot_rows(chosen_ref, sel, length)
    picked_ref[0] = mm(one_hot, base_ref[0]).astype(BF)
    both = jnp.concatenate(
        [segments_ref[row, :].astype(F32), present_ref[row, :].astype(F32), jnp.zeros((6, length), F32)], axis=0
    ).astype(BF)
    along = mm_nt(both, one_hot)
    down = along.T
    slot = lax.broadcasted_iota(jnp.int32, (sel, sel), 0)
    seen = lax.broadcasted_iota(jnp.int32, (sel, sel), 1)
    open_key = (along[1:2, :] > 0.5) | (slot == seen)
    permitted = (seen <= slot) & (down[:, 0:1] == along[0:1, :]) & open_key
    bias_ref[0] = jnp.where(permitted, 0.0, -1e30)
    keep_ref[...] = down[:, 1:2]


def select(base, tables, mask=False, after=()):
    rows, length, half = base.shape
    sel = tables[0].shape[1]
    count = 1 + len(tables)
    kernel = pick_and_mask if mask else pick_rows

    def body(*refs):
        kernel(*refs[:count], *refs[count + len(after) :])

    outs = [shape((rows, sel, half)), shape((rows, sel, sel), F32), shape((rows * sel, 1), F32)]
    specs = [
        pl.BlockSpec((1, sel, half), lambda row: (row, 0, 0)),
        pl.BlockSpec((1, sel, sel), lambda row: (row, 0, 0)),
        pl.BlockSpec((sel, 1), lambda row: (row, 0)),
    ]
    return pl.pallas_call(
        body,
        grid=(rows,),
        out_shape=outs if mask else outs[:1],
        in_specs=[pl.BlockSpec((1, length, half), lambda row: (row, 0, 0))]
        + [pl.BlockSpec(v.shape, lambda row: (0, 0)) for v in tables]
        + [pl.BlockSpec(memory_space=pl.ANY)] * len(after),
        out_specs=specs if mask else specs[:1],
        compiler_params=pltpu.CompilerParams(vmem_limit_bytes=2 * VMEM_SPARE),
        cost_estimate=pl.CostEstimate(
            flops=2 * rows * sel * length * half, bytes_accessed=2 * base.size, transcendentals=0
        ),
        name="select_rows",
    )(base, *tables, *after)


def put_rows(bits_ref, chosen_ref, values_ref, base_ref, out_ref):
    long, half = out_ref.shape[1:]
    sel = values_ref.shape[0]
    first = pl.program_id(1) * long
    chosen = chosen_ref[pl.ds(pl.program_id(0), 1), :]
    hit = first + lax.broadcasted_iota(jnp.int32, (long, sel), 0) == chosen
    one_hot = jnp.where(hit, 1.0, 0.0).astype(BF)
    offset = pl.multiple_of(bits_ref[-1 + bits_ref.shape[0]] * half, half)
    values = values_ref[:, pl.ds(offset, half)]
    placed = mm(one_hot, jnp.concatenate([values, jnp.ones((sel, 128), BF)], axis=1))
    taken = placed[:, half:] > 0.5
    for at in range(0, half, 128):
        here = slice(at, at + 128)
        out_ref[0, :, here] = jnp.where(taken, placed[:, here].astype(BF), base_ref[0, :, here])


def put(base, chosen, values, bits, after=()):
    rows, length, half = base.shape
    sel = chosen.shape[1]
    long = length // 2

    def body(*refs):
        put_rows(*refs[:4], refs[-2])
        refs[-1][...] = jnp.zeros_like(refs[-1])

    return pl.pallas_call(
        body,
        grid=(rows, length // long),
        out_shape=(shape(base.shape), shape((8, 128), F32)),
        in_specs=[
            pl.BlockSpec(memory_space=pltpu.SMEM),
            pl.BlockSpec(chosen.shape, lambda row, part: (0, 0)),
            pl.BlockSpec((sel, values.shape[1]), lambda row, part: (row, 0)),
            pl.BlockSpec((1, long, half), lambda row, part: (row, part, 0)),
        ]
        + [pl.BlockSpec(memory_space=pl.ANY)] * len(after),
        out_specs=[
            pl.BlockSpec((1, long, half), lambda row, part: (row, part, 0)),
            pl.BlockSpec((8, 128), lambda row, part: (0, 0)),
        ],
        compiler_params=pltpu.CompilerParams(vmem_limit_bytes=24 << 20),
        cost_estimate=pl.CostEstimate(
            flops=2 * rows * sel * length * half, bytes_accessed=4 * base.size, transcendentals=0
        ),
        name="put_rows",
    )(bits, chosen, values, base, *after)


def first_columns(attention_ref, mixing_ref, vectors_ref, out_ref):
    half = attention_ref.shape[2]
    for k in range(3):
        out_ref[:, k * half : (k + 1) * half] = attention_ref[k]
    out_ref[:, 3 * half : 4 * half] = mixing_ref[...]
    out_ref[:, 4 * half :] = vectors_ref[...]


def second_columns(cuts, expand_ref, contract_ref, out_ref):
    at = 0
    for start, end in cuts:
        out_ref[:, at : at + end - start] = expand_ref[:, start:end]
        at += end - start
        out_ref[:, at : at + end - start] = contract_ref[:, start:end]
        at += end - start


def untouched(*refs):
    pass


def tie(value, *others):
    if not others:
        return value
    anywhere = pl.BlockSpec(memory_space=pl.ANY)
    return pl.pallas_call(
        untouched,
        out_shape=jax.ShapeDtypeStruct(value.shape, value.dtype),
        in_specs=[anywhere] * (1 + len(others)),
        out_specs=anywhere,
        input_output_aliases={0: 0},
        compiler_params=pltpu.CompilerParams(vmem_limit_bytes=1 << 20),
        cost_estimate=pl.CostEstimate(flops=0, bytes_accessed=0, transcendentals=0),
    )(value, *others)


class Cube:
    def __init__(self, count):
        self.count, self.depth = count, count.bit_length() - 1
        index = lax.axis_index("dp").astype(jnp.int32)
        self.bits = jnp.append(
            (index >> jnp.arange(self.depth)) & 1, lax.axis_index("mp").astype(jnp.int32)
        )
        short = self.depth // 3
        self.x, self.y = list(range(short)), list(range(short, 2 * short))
        self.z = list(range(2 * short, self.depth))
        self.far = self.z[1:]
        near = [self.x, self.y, self.z[:1]]
        self.orders = [sum(near[k:] + near[:k], []) for k in range(3)]

    def swap(self, value, bit):
        return lax.ppermute(value, "dp", [(i, i ^ (1 << bit)) for i in range(self.count)])


class Part:
    def __init__(self, value, bits, sent=None, start=0, width=None):
        self.value, self.bits, self.sent = value, list(bits), sent
        self.start, self.width = start, width or value.shape[2]

    def columns(self, start, end):
        return Part(self.value, self.bits, self.sent, self.start + start, end - start)


def thirds(width):
    ends = [(k * width // 3 + 64) // 128 * 128 for k in range(4)]
    return list(zip(ends, ends[1:]))


def start_exchange(cube, part, bit):
    part.sent = cube.swap(part.value, bit)
    return part


def stack_parts(plan, bits_ref, *refs):
    ins, outs = refs[: 2 * len(plan)], refs[2 * len(plan) :]
    for k, (bit, blocks) in enumerate(plan):
        mine = bits_ref[bit]
        for block in range(blocks):
            outs[k][mine, block] = ins[2 * k][block]
            outs[k][1 - mine, block] = ins[2 * k + 1][block]


def stack(cube, parts, bits, after=()):
    outs, args, plan = [], [], []
    for part, bit in zip(parts, bits):
        outs.append(shape((2,) + part.value.shape))
        args += [part.value, part.sent]
        plan.append((bit, part.value.shape[0]))
    found = call(functools.partial(stack_parts, plan), outs, args, after, cube.bits, name="stack_parts")
    return [
        Part(v.reshape((-1,) + v.shape[2:]), [bit] + part.bits) for v, part, bit in zip(found, parts, bits)
    ]


def split_columns(plan, own_ref, *out_refs):
    for ref, (start, end) in zip(out_refs, plan):
        ref[...] = own_ref[:, :, start:end]


def whole_rows(plan, bits_ref, *refs):
    ins, out_ref = refs[:-1], refs[-1]
    column = 0
    for k, (bit, places, start, width) in enumerate(plan):
        mine = bits_ref[bit]
        for block, place in enumerate(places):
            here = slice(column, column + width)
            out_ref[place + (mine << bit), :, here] = ins[2 * k][block, :, start : start + width]
            out_ref[place + ((1 - mine) << bit), :, here] = ins[2 * k + 1][block, :, start : start + width]
        column += width


def whole(cube, parts, bits, after=()):
    args, plan, width = [], [], 0
    for part, bit in zip(parts, bits):
        places = []
        for block in range(part.value.shape[0]):
            digits = [(block >> k) & 1 for k in range(len(part.bits))][::-1]
            places.append(sum(digit << b for digit, b in zip(digits, part.bits)))
        args += [part.value, part.sent]
        plan.append((bit, places, part.start, part.width))
        width += part.width
    rows = parts[0].value.shape[1]
    (found,) = call(
        functools.partial(whole_rows, plan),
        (shape((cube.count, rows, width)),),
        args,
        after,
        cube.bits,
        name="whole_rows",
    )
    return found.reshape(-1, width)


def fold_parts(plan, bits_ref, *refs):
    refs = list(refs)
    taken = [[(refs.pop(0), refs.pop(0) if sent else None) for sent, _, _ in sources] for _, _, sources in plan]
    for (bit, (high, low), sources), ins in zip(plan, taken):
        sent_ref, kept_ref = refs.pop(0), refs.pop(0)
        mine = bits_ref[bit]
        column = 0
        for (_, start, width), (value_ref, other_ref) in zip(sources, ins):
            there = slice(start, start + width)
            here = slice(column, column + width)
            for a in range(high):
                for b in range(low):
                    for index, out_ref in ((1 - mine, sent_ref), (mine, kept_ref)):
                        found = value_ref[a, index, b, :, there].astype(F32)
                        if other_ref is not None:
                            found += other_ref[a, index, b, :, there].astype(F32)
                        out_ref[a * low + b, :, here] = found.astype(out_ref.dtype)
            column += width


def fold(cube, groups, bits, after=()):
    args, outs, plan = [], [], []
    for sources, bit in zip(groups, bits):
        at = sources[0].bits.index(bit)
        high, low = 1 << at, 1 << (len(sources[0].bits) - at - 1)
        listed = []
        for part in sources:
            for value in (part.value, part.sent):
                if value is not None:
                    args.append(value.reshape((high, 2, low) + value.shape[1:]))
            listed.append((part.sent is not None, part.start, part.width))
        plan.append((bit, (high, low), listed))
        dims = (high * low, sources[0].value.shape[1], sum(p.width for p in sources))
        outs += [shape(dims), shape(dims, F32)]
    found = call(functools.partial(fold_parts, plan), outs, args, after, cube.bits, name="fold_parts")
    done = []
    for k, (sources, bit) in enumerate(zip(groups, bits)):
        left = [b for b in sources[0].bits if b != bit]
        done.append(Part(found[2 * k + 1], left, cube.swap(found[2 * k], bit)))
    return done


def cut(cube, total):
    blocks = total.reshape(cube.count, -1, total.shape[1])
    bits = list(range(cube.depth))[::-1]
    return [Part(blocks, bits, None, start, end - start) for start, end in thirds(total.shape[1]) if end > start]


def arrived(parts):
    return [p.sent for p in parts]


def sum_first(value_ref, sent_ref, attention_ref, mixing_ref, vectors_ref):
    half = attention_ref.shape[2]
    total = value_ref[0] + sent_ref[0].astype(F32)
    for k in range(3):
        attention_ref[k] = total[:, k * half : (k + 1) * half]
    mixing_ref[...] = total[:, 3 * half : 4 * half]
    vectors_ref[...] = total[:, 4 * half :].T


def sum_second(cuts, value_ref, sent_ref, expand_ref, contract_ref):
    at = 0
    for start, end in cuts:
        for side in range(2):
            width = end - start
            total = value_ref[0, :, at : at + width] + sent_ref[0, :, at : at + width].astype(F32)
            (expand_ref if side else contract_ref)[:, start:end] = total
            at += width


def other_core(value):
    return lax.ppermute(value, "mp", [(0, 1), (1, 0)])


def both_halves(value):
    other = other_core(value)
    low = lax.axis_index("mp") == 0
    return jnp.concatenate([jnp.where(low, value, other), jnp.where(low, other, value)], axis=-1)


def shards(
    tokens,
    segments,
    present,
    chosen,
    attention,
    mixing,
    expand,
    contract,
    prenorm,
    midnorm,
    router,
    cotangent,
    count,
):
    cube = Cube(count)
    row_count, length, half_width = tokens.shape
    sel_count = chosen.shape[1]
    token_count = row_count * sel_count
    own_rows = mixing.shape[1]
    width = 2 * half_width
    hidden_here = expand.shape[1]
    heads_here = half_width // HD
    by_row = (row_count, sel_count)

    vectors = jnp.pad(jnp.stack([prenorm, midnorm, router], axis=1), ((0, 0), (0, 125)))
    cuts = thirds(hidden_here)
    (first_own,) = call(
        first_columns, (shape((own_rows, 4 * half_width + 128)),), (attention, mixing.T, vectors), name="first_columns"
    )
    first_far = start_exchange(cube, Part(first_own[None], []), cube.far[-1])
    (second_own,) = call(
        functools.partial(second_columns, cuts),
        (shape((own_rows, 2 * hidden_here)),),
        (expand, contract.T),
        name="second_columns",
    )
    picked, bias, keep = select(tokens, [chosen, segments, present], True)

    def spread(far, after, begin=()):
        for bit in cube.far[-2::-1]:
            far = start_exchange(cube, stack(cube, [far], [far_bit(far)], after)[0], bit)
        column = stack(cube, [far], [far_bit(far)], after)[0]
        ends = thirds(column.width)
        found = call(
            functools.partial(split_columns, ends),
            [shape(column.value.shape[:2] + (end - start,)) for start, end in ends],
            [column.value],
            begin,
            name="split_columns",
        )
        return [Part(v, column.bits) for v in found]

    def far_bit(part):
        return cube.far[-1 - len(part.bits)]

    def step_bits(step):
        return [order[step] for order in cube.orders]

    def send(parts, step):
        return [start_exchange(cube, p, bit) for p, bit in zip(parts, step_bits(step))]

    steps = len(cube.orders[0])
    first_parts = spread(first_far, [picked])
    states = both_halves(tie(picked, first_parts[0].value)).reshape(token_count, width)
    first_parts = send(first_parts, 0)
    second_far = start_exchange(cube, Part(tie(second_own, *arrived([first_far]))[None], []), cube.far[-1])
    for step in range(1, steps):
        if step == steps - 1:
            (picked_grads,) = select(cotangent, [chosen], False, [first_parts[0].value])
            after = arrived([second_far]) + [picked_grads]
        else:
            after = [states] if step == 1 else []
        first_parts = send(stack(cube, first_parts, step_bits(step - 1), after), step)
    first_last = [p.value for p in first_parts]
    first = whole(cube, first_parts, step_bits(steps - 1))
    mix = first[:, 3 * half_width : 4 * half_width]
    second_parts = send(spread(second_far, [], first_last[:1]), 0)
    second_begun = []
    for step in range(1, steps - 1):
        second_parts = stack(cube, second_parts, step_bits(step - 1), [first] if step == 1 else [])
        second_begun = second_begun or [p.value for p in second_parts]
        second_parts = send(second_parts, step)
    upstream = both_halves(tie(picked_grads, *second_begun)).reshape(token_count, width)
    second_parts = stack(cube, second_parts, step_bits(steps - 2))
    each = hidden_here // 3
    up_parts, down_parts = [], []
    for p in second_parts:
        up_parts.append(Part(p.value[..., :each], p.bits))
        down_parts.append(Part(p.value[..., each:], p.bits))
    up = whole(cube, send(up_parts, steps - 1), step_bits(steps - 1))
    down_parts = send(down_parts, steps - 1)

    wide = shape((token_count, width))
    tall = shape((token_count, hidden_here))
    vector = shape((8, width), F32)
    normed, packed, probs, context, gains = call(
        functools.partial(attention_forward, *by_row),
        (
            wide,
            shape((token_count, 3 * half_width)),
            shape((row_count, heads_here, sel_count, sel_count), F32),
            shape((token_count, half_width)),
            vector,
        ),
        (states, first, bias),
        after=second_begun,
        flops=token_count * width * half_width * 6,
        name="attention_forward",
    )
    (att_own,) = call(
        mix_forward, (wide,), (context, mix), flops=2 * token_count * width * half_width, name="mix_forward"
    )
    att_other = other_core(att_own)
    normed_mid, activated, slope, feed_grad, down_grad = call(
        functools.partial(up_forward, *by_row),
        (wide, tall, tall, wide, shape((width, hidden_here))),
        (states, upstream, att_own, att_other, up, gains, keep),
        flops=4 * token_count * width * hidden_here,
        name="up_forward",
    )
    down = whole(cube, down_parts, step_bits(steps - 1), [activated])

    hidden_grad, mid_own = call(
        down_backward,
        (tall, wide),
        (feed_grad, down, slope, up),
        flops=4 * token_count * width * hidden_here,
        name="down_backward",
    )
    up_grad, feed_own = call(
        down_forward,
        (shape((width, hidden_here)), wide),
        (normed_mid, hidden_grad, activated, down),
        flops=4 * token_count * width * hidden_here,
        name="down_forward",
    )
    feed_other = other_core(feed_own)
    mid_other = tie(other_core(mid_own), feed_own)

    def back_bits(step):
        return [order[-1 - step] for order in cube.orders]

    def alone(parts):
        return [[p] for p in parts]

    both_grads = [list(pair) for pair in zip(cut(cube, down_grad), cut(cube, up_grad))]
    both_grads = fold(cube, both_grads, back_bits(0))

    mixed, packed_grad, pre_own, middle_grad, mid_gain_grad = call(
        functools.partial(attention_backward, *by_row),
        (
            wide,
            shape((token_count, 3 * half_width)),
            wide,
            shape((token_count, width), F32),
            vector,
        ),
        (states, att_own, att_other, mid_own, mid_other, upstream, keep, gains, mix, first, packed, probs),
        after=[both_grads[0].value],
        scratch=[pltpu.VMEM((token_count, half_width), BF)],
        flops=10 * token_count * width * half_width,
        name="attention_backward",
    )
    (first_grad,) = call(
        projection_grads,
        (shape((width, 4 * half_width)),),
        (normed, packed_grad, mixed, context),
        flops=8 * token_count * width * half_width,
        name="projection_grads",
    )
    finished, logit_grad, router_grad = call(
        functools.partial(final_forward, *by_row),
        (wide, shape((token_count, 1), F32), vector),
        (states, upstream, att_own, att_other, feed_own, feed_other, gains, keep),
        after=[first_grad],
        name="final_forward",
    )
    both_grads = fold(cube, alone(both_grads), back_bits(1), [logit_grad])
    pre_other = other_core(tie(pre_own, both_grads[0].value))
    total_grad, vector_grads = call(
        functools.partial(final_backward, *by_row),
        (wide, shape((width, 128))),
        (states, upstream, middle_grad, pre_own, pre_other, logit_grad, gains, mid_gain_grad, router_grad),
        scratch=[pltpu.VMEM((128, width), F32)],
        name="final_backward",
    )
    first_grads = alone(cut(cube, first_grad))
    first_grads[-1] += cut(cube, vector_grads)
    first_grads = fold(cube, first_grads, back_bits(0))
    for step in range(2, steps):
        both_grads = fold(cube, alone(both_grads), back_bits(step), [first_grad] if step == 2 else [])
    first_grads = fold(cube, alone(first_grads), back_bits(1))
    both_grads = [both_grads]
    for bit in cube.far:
        both_grads = [fold(cube, both_grads, [bit])]
    result, done = put(tokens, chosen, finished, cube.bits, [both_grads[0][0].value])
    tokens_grad, _ = put(cotangent, chosen, total_grad, cube.bits, [done])
    for step in range(2, steps):
        first_grads = fold(cube, alone(first_grads), back_bits(step), [done] if step == 2 else [])
    first_grads = [first_grads]
    for bit in cube.far:
        first_grads = [fold(cube, first_grads, [bit])]
    (both_grad,), (first_grad,) = both_grads[0], first_grads[0]
    up_out, down_out = call(
        functools.partial(sum_second, cuts),
        (shape((own_rows, hidden_here), F32),) * 2,
        (both_grad.value, both_grad.sent),
        name="sum_second",
    )
    attention_out, mixing_out, vector_out = call(
        sum_first,
        (
            shape((3, own_rows, half_width), F32),
            shape((own_rows, half_width), F32),
            shape((128, own_rows), F32),
        ),
        (first_grad.value, first_grad.sent),
        name="sum_first",
    )
    return (
        result,
        tokens_grad,
        attention_out,
        mixing_out.T,
        up_out,
        down_out.T,
        vector_out[0],
        vector_out[1],
        vector_out[2],
    )


def solution(mesh):
    in_specs = (
        P("dp", None, "mp"),
        P("dp", None),
        P("dp", None),
        P("dp", None),
        P(None, "dp", "mp"),
        P("mp", "dp"),
        P("dp", "mp"),
        P("mp", "dp"),
        P("dp"),
        P("dp"),
        P("dp"),
        P("dp", None, "mp"),
    )
    out_specs = (
        P("dp", None, "mp"),
        P("dp", None, "mp"),
        P(None, "dp", "mp"),
        P("mp", "dp"),
        P("dp", "mp"),
        P("mp", "dp"),
        P("dp"),
        P("dp"),
        P("dp"),
    )
    count = mesh.shape["dp"]

    def body(*args):
        return shards(*args, count)

    return jax.shard_map(body, mesh=mesh, in_specs=in_specs, out_specs=out_specs, check_vma=False)
```

```python
import functools
import math

import jax
import jax.numpy as jnp
from jax import lax
from jax.experimental import pallas as pl
from jax.experimental.pallas import tpu as pltpu
from jax.sharding import PartitionSpec as P

HD = 64
EPSILON = 1e-06
BF = jnp.bfloat16
F32 = jnp.float32
VMEM_SPARE = 10 << 20


def mm(a, b):
    return jnp.dot(a, b, preferred_element_type=F32)


def mm_nt(a, b):
    return lax.dot_general(a, b, (((1,), (1,)), ((), ())), preferred_element_type=F32)


def mm_tn(a, b):
    return lax.dot_general(a, b, (((0,), (0,)), ((), ())), preferred_element_type=F32)


def inverse_rms(values):
    return lax.rsqrt(jnp.mean(values * values, axis=-1, keepdims=True) + EPSILON)


def call(kernel, outs, args, after=(), bits=None, scratch=(), flops=0, name=None):
    moved = sum(v.size * v.dtype.itemsize for v in (*args, *outs))
    scalars = [] if bits is None else [bits]
    count = len(scalars) + len(args)

    def body(*refs):
        kernel(*refs[:count], *refs[count + len(after) :])

    return pl.pallas_call(
        body,
        out_shape=outs,
        in_specs=[pl.BlockSpec(memory_space=pltpu.SMEM)] * len(scalars)
        + [pl.BlockSpec(memory_space=pltpu.VMEM)] * len(args)
        + [pl.BlockSpec(memory_space=pl.ANY)] * len(after),
        out_specs=[pl.BlockSpec(memory_space=pltpu.VMEM)] * len(outs),
        scratch_shapes=scratch,
        compiler_params=pltpu.CompilerParams(vmem_limit_bytes=VMEM_SPARE),
        cost_estimate=pl.CostEstimate(flops=flops, bytes_accessed=moved, transcendentals=0),
        name=name,
    )(*scalars, *args, *after)


def shape(dims, dtype=BF):
    return jax.ShapeDtypeStruct(tuple(dims), dtype)


def first_head(width=2 * HD):
    return lax.broadcasted_iota(jnp.int32, (1, width), 1) < HD


def attention_forward(rows, sel, states_ref, weights_ref, bias_ref, normed_ref, packed_ref, probs_ref, context_ref, gains_ref):
    width = states_ref.shape[1]
    half = context_ref.shape[1]
    gains_ref[...] = weights_ref[:, 4 * half :].astype(F32).T[:8]
    gain = gains_ref[0:1, :]
    scale = HD ** (-0.5)

    for row in range(rows):
        here = slice(row * sel, (row + 1) * sel)
        states = states_ref[here, :].astype(F32)
        normed_ref[here, :] = (states * inverse_rms(states) * gain).astype(BF)
    for start in range(0, 3 * half, 384):
        packed_ref[:, start : start + 384] = mm(normed_ref[...], weights_ref[:, start : start + 384]).astype(BF)
    first = first_head()

    @pl.loop(0, rows, unroll=True)
    def _(row):
        here = pl.ds(pl.multiple_of(row * sel, sel), sel)
        bias = bias_ref[row]
        for pair in range(half // (2 * HD)):
            at = pair * 2 * HD
            queries = packed_ref[here, at : at + 2 * HD]
            keys = packed_ref[here, half + at : half + at + 2 * HD]
            vals = packed_ref[here, 2 * half + at : 2 * half + at + 2 * HD]
            found = []
            for head in range(2):
                mine = first if head == 0 else ~first
                scores = mm_nt(jnp.where(mine, queries, jnp.zeros_like(queries)), keys) * scale + bias
                exponent = jnp.exp(scores - jnp.max(scores, axis=-1, keepdims=True))
                probs = exponent / jnp.sum(exponent, axis=-1, keepdims=True)
                probs_ref[row, 2 * pair + head] = probs
                found.append(mm(probs.astype(BF), vals))
            context_ref[here, at : at + 2 * HD] = jnp.where(first, found[0], found[1]).astype(BF)


def mix_forward(context_ref, mix_ref, out_ref):
    out_ref[...] = mm_nt(context_ref[...], mix_ref[...]).astype(BF)


def up_forward(
    rows, sel, states_ref, upstream_ref, own_ref, other_ref, up_ref, gains_ref, keep_ref,
    normed_ref, activated_ref, slope_ref, feed_grad_ref, grad_ref,
):
    mid_gain, router = gains_ref[1:2, :], gains_ref[2:3, :]
    c, a = (2.0 / math.pi) ** 0.5, 0.044715

    @pl.loop(0, rows)
    def _(row):
        here = pl.ds(pl.multiple_of(row * sel, sel), sel)
        states = states_ref[here, :].astype(F32)
        prob = jax.nn.sigmoid(jnp.sum(states * router, axis=-1, keepdims=True))
        gate = prob * keep_ref[here, :]
        feed_grad_ref[here, :] = (gate * upstream_ref[here, :].astype(F32)).astype(BF)
        middle = states + (own_ref[here, :].astype(F32) + other_ref[here, :].astype(F32))
        normed = (middle * inverse_rms(middle) * mid_gain).astype(BF)
        normed_ref[here, :] = normed

    upright_grad = feed_grad_ref[...].T
    chunk = 256
    for at in range(0, up_ref.shape[1], chunk):
        here = slice(at, at + chunk)
        hidden = mm(normed_ref[...], up_ref[:, here])
        square = hidden * hidden
        share = 0.5 * jnp.tanh(hidden * (c + c * a * square)) + 0.5
        activated = hidden * share
        activated_ref[:, here] = activated.astype(BF)
        slope = share + activated * (1.0 - share) * (2.0 * c + 6.0 * a * c * square)
        slope_ref[:, here] = slope.astype(BF)
        grad_ref[:, here] = mm(upright_grad, activated_ref[:, here]).astype(BF)


def down_backward(feed_grad_ref, down_ref, slope_ref, up_ref, hidden_grad_ref, out_ref):
    chunk = 256
    for at in range(0, down_ref.shape[1], chunk):
        here = slice(at, at + chunk)
        act_grad = mm(feed_grad_ref[...], down_ref[:, here])
        hidden_grad_ref[:, here] = (act_grad * slope_ref[:, here].astype(F32)).astype(BF)
    for at in range(0, out_ref.shape[1], chunk):
        here = slice(at, at + chunk)
        out_ref[:, here] = mm_nt(hidden_grad_ref[...], up_ref[here, :]).astype(BF)


def down_forward(normed_ref, hidden_grad_ref, activated_ref, down_ref, grad_ref, out_ref):
    upright_normed = normed_ref[...].T
    chunk = 256
    for at in range(0, grad_ref.shape[1], chunk):
        here = slice(at, at + chunk)
        grad_ref[:, here] = mm(upright_normed, hidden_grad_ref[:, here]).astype(BF)
    for at in range(0, out_ref.shape[1], chunk):
        here = slice(at, at + chunk)
        out_ref[:, here] = mm_nt(activated_ref[...], down_ref[here, :]).astype(BF)


def norm_backward(values, grads, gain):
    rho = inverse_rms(values)
    unit = values * rho
    scaled = grads * gain
    back = rho * (scaled - unit * jnp.mean(scaled * unit, axis=-1, keepdims=True))
    return back, jnp.sum(grads * unit, axis=0, keepdims=True)


def attention_backward(
    rows, sel, states_ref, own_ref, other_ref, mid_own_ref, mid_other_ref, upstream_ref, keep_ref, gains_ref,
    mix_ref, weights_ref, packed_ref, probs_ref,
    mixed_ref, packed_grad_ref, out_ref, middle_grad_ref, gain_grad_ref, context_grad_ref,
):
    mid_gain, router = gains_ref[1:2, :], gains_ref[2:3, :]
    half = mix_ref.shape[1]
    scale = HD ** (-0.5)
    gain_grad_ref[...] = jnp.zeros_like(gain_grad_ref)

    @pl.loop(0, rows)
    def _(row):
        here = pl.ds(pl.multiple_of(row * sel, sel), sel)
        states = states_ref[here, :].astype(F32)
        middle = states + (own_ref[here, :].astype(F32) + other_ref[here, :].astype(F32))
        mid_in = mid_own_ref[here, :].astype(F32) + mid_other_ref[here, :].astype(F32)
        middle_grad, gain_grad = norm_backward(middle, mid_in, mid_gain)
        gain_grad_ref[0:1, :] += gain_grad
        middle_grad_ref[here, :] = middle_grad
        gate = jax.nn.sigmoid(jnp.sum(states * router, axis=-1, keepdims=True)) * keep_ref[here, :]
        mixed = (gate * upstream_ref[here, :].astype(F32) + middle_grad).astype(BF)
        mixed_ref[here, :] = mixed

    context_grad_ref[...] = mm(mixed_ref[...], mix_ref[...]).astype(BF)
    first = first_head()

    @pl.loop(0, rows, unroll=True)
    def _(row):
        here = pl.ds(pl.multiple_of(row * sel, sel), sel)
        for pair in range(half // (2 * HD)):
            at = pair * 2 * HD
            queries = packed_ref[here, at : at + 2 * HD]
            keys = packed_ref[here, half + at : half + at + 2 * HD]
            vals = packed_ref[here, 2 * half + at : 2 * half + at + 2 * HD]
            grads = context_grad_ref[here, at : at + 2 * HD]
            queries_up, grads_up = queries.T, grads.T
            by_query, by_key, by_value = [], [], []
            for head in range(2):
                mine = first if head == 0 else ~first
                lanes = slice(head * HD, (head + 1) * HD)
                probs = probs_ref[row, 2 * pair + head]
                prob_grad = mm_nt(jnp.where(mine, grads, jnp.zeros_like(grads)), vals)
                centre = jnp.sum(probs * prob_grad, axis=-1, keepdims=True)
                score_grad = (probs * (prob_grad - centre)).astype(BF)
                by_query.append(mm(score_grad, keys))
                by_key.append(mm(queries_up[lanes], score_grad))
                by_value.append(mm(grads_up[lanes], probs.astype(BF)))
            packed_grad_ref[here, at : at + 2 * HD] = (
                jnp.where(first, by_query[0], by_query[1]) * scale
            ).astype(BF)
            packed_grad_ref[here, half + at : half + at + 2 * HD] = (
                (jnp.concatenate(by_key, axis=0) * scale).astype(BF).T
            )
            packed_grad_ref[here, 2 * half + at : 2 * half + at + 2 * HD] = (
                jnp.concatenate(by_value, axis=0).astype(BF).T
            )

    chunk = 256
    for at in range(0, out_ref.shape[1], chunk):
        here = slice(at, at + chunk)
        out_ref[:, here] = mm_nt(packed_grad_ref[...], weights_ref[here, : 3 * half]).astype(BF)


def projection_grads(normed_ref, packed_grad_ref, mixed_ref, context_ref, grad_ref):
    wide, chunk = packed_grad_ref.shape[1], 384
    upright_normed, upright_mixed = normed_ref[...].T, mixed_ref[...].T
    for at in range(0, wide, chunk):
        here = slice(at, at + chunk)
        grad_ref[:, here] = mm(upright_normed, packed_grad_ref[:, here]).astype(BF)
    grad_ref[:, wide:] = mm(upright_mixed, context_ref[...]).astype(BF)


def final_forward(
    rows, sel, states_ref, upstream_ref, own_ref, other_ref, feed_own_ref, feed_other_ref, gains_ref, keep_ref,
    finished_ref, logit_grad_ref, router_grad_ref,
):
    router = gains_ref[2:3, :]
    router_grad_ref[...] = jnp.zeros_like(router_grad_ref)

    @pl.loop(0, rows)
    def _(row):
        here = pl.ds(pl.multiple_of(row * sel, sel), sel)
        states = states_ref[here, :].astype(F32)
        attended = own_ref[here, :].astype(F32) + other_ref[here, :].astype(F32)
        branch = attended + (feed_own_ref[here, :].astype(F32) + feed_other_ref[here, :].astype(F32))
        prob = jax.nn.sigmoid(jnp.sum(states * router, axis=-1, keepdims=True))
        keep = keep_ref[here, :]
        finished_ref[here, :] = (states + prob * keep * branch).astype(BF)
        gate_grad = jnp.sum(upstream_ref[here, :].astype(F32) * branch, axis=-1, keepdims=True)
        logit_grad = gate_grad * keep * prob * (1.0 - prob)
        logit_grad_ref[here, :] = logit_grad
        router_grad_ref[0:1, :] += jnp.sum(logit_grad * states, axis=0, keepdims=True)


def final_backward(
    rows, sel, states_ref, upstream_ref, middle_grad_ref, pre_own_ref, pre_other_ref, logit_grad_ref, gains_ref,
    mid_gain_grad_ref, router_grad_ref, total_ref, vectors_ref, lines_ref,
):
    pre_gain, router = gains_ref[0:1, :], gains_ref[2:3, :]
    lines_ref[...] = jnp.zeros_like(lines_ref)
    lines_ref[1:2, :] = mid_gain_grad_ref[0:1, :]
    lines_ref[2:3, :] = router_grad_ref[0:1, :]

    @pl.loop(0, rows)
    def _(row):
        here = pl.ds(pl.multiple_of(row * sel, sel), sel)
        states = states_ref[here, :].astype(F32)
        pre_in = pre_own_ref[here, :].astype(F32) + pre_other_ref[here, :].astype(F32)
        back, gain_grad = norm_backward(states, pre_in, pre_gain)
        lines_ref[0:1, :] += gain_grad
        total = upstream_ref[here, :].astype(F32) + logit_grad_ref[here, :] * router
        total_ref[here, :] = (total + middle_grad_ref[here, :] + back).astype(BF)

    vectors_ref[...] = lines_ref[...].T.astype(BF)


def upright(row):
    return jnp.broadcast_to(row, (8, row.shape[1])).T[:, :1]


def one_hot_rows(chosen_ref, sel, length):
    row = pl.ds(pl.program_id(0), 1)
    chosen = upright(chosen_ref[row, :].astype(F32)).astype(jnp.int32)
    return jnp.where(chosen == lax.broadcasted_iota(jnp.int32, (sel, length), 1), 1.0, 0.0).astype(BF)


def pick_rows(base_ref, chosen_ref, picked_ref):
    one_hot = one_hot_rows(chosen_ref, picked_ref.shape[1], base_ref.shape[1])
    picked_ref[0] = mm(one_hot, base_ref[0]).astype(BF)


def pick_and_mask(base_ref, chosen_ref, segments_ref, present_ref, picked_ref, bias_ref, keep_ref):
    sel, length = picked_ref.shape[1], base_ref.shape[1]
    row = pl.ds(pl.program_id(0), 1)
    one_hot = one_hot_rows(chosen_ref, sel, length)
    picked_ref[0] = mm(one_hot, base_ref[0]).astype(BF)
    both = jnp.concatenate(
        [segments_ref[row, :].astype(F32), present_ref[row, :].astype(F32), jnp.zeros((6, length), F32)], axis=0
    ).astype(BF)
    along = mm_nt(both, one_hot)
    down = along.T
    slot = lax.broadcasted_iota(jnp.int32, (sel, sel), 0)
    seen = lax.broadcasted_iota(jnp.int32, (sel, sel), 1)
    open_key = (along[1:2, :] > 0.5) | (slot == seen)
    permitted = (seen <= slot) & (down[:, 0:1] == along[0:1, :]) & open_key
    bias_ref[0] = jnp.where(permitted, 0.0, -1e30)
    keep_ref[...] = down[:, 1:2]


def select(base, tables, mask=False, after=()):
    rows, length, half = base.shape
    sel = tables[0].shape[1]
    count = 1 + len(tables)
    kernel = pick_and_mask if mask else pick_rows

    def body(*refs):
        kernel(*refs[:count], *refs[count + len(after) :])

    outs = [shape((rows, sel, half)), shape((rows, sel, sel), F32), shape((rows * sel, 1), F32)]
    specs = [
        pl.BlockSpec((1, sel, half), lambda row: (row, 0, 0)),
        pl.BlockSpec((1, sel, sel), lambda row: (row, 0, 0)),
        pl.BlockSpec((sel, 1), lambda row: (row, 0)),
    ]
    return pl.pallas_call(
        body,
        grid=(rows,),
        out_shape=outs if mask else outs[:1],
        in_specs=[pl.BlockSpec((1, length, half), lambda row: (row, 0, 0))]
        + [pl.BlockSpec(v.shape, lambda row: (0, 0)) for v in tables]
        + [pl.BlockSpec(memory_space=pl.ANY)] * len(after),
        out_specs=specs if mask else specs[:1],
        compiler_params=pltpu.CompilerParams(vmem_limit_bytes=2 * VMEM_SPARE),
        cost_estimate=pl.CostEstimate(
            flops=2 * rows * sel * length * half, bytes_accessed=2 * base.size, transcendentals=0
        ),
        name="select_rows",
    )(base, *tables, *after)


def put_rows(bits_ref, chosen_ref, values_ref, base_ref, out_ref):
    long, half = out_ref.shape[1:]
    sel = values_ref.shape[0]
    first = pl.program_id(1) * long
    chosen = chosen_ref[pl.ds(pl.program_id(0), 1), :]
    hit = first + lax.broadcasted_iota(jnp.int32, (long, sel), 0) == chosen
    one_hot = jnp.where(hit, 1.0, 0.0).astype(BF)
    offset = pl.multiple_of(bits_ref[-1 + bits_ref.shape[0]] * half, half)
    values = values_ref[:, pl.ds(offset, half)]
    placed = mm(one_hot, jnp.concatenate([values, jnp.ones((sel, 128), BF)], axis=1))
    taken = placed[:, half:] > 0.5
    for at in range(0, half, 128):
        here = slice(at, at + 128)
        out_ref[0, :, here] = jnp.where(taken, placed[:, here].astype(BF), base_ref[0, :, here])


def put(base, chosen, values, bits, after=()):
    rows, length, half = base.shape
    sel = chosen.shape[1]
    long = length // 2

    def body(*refs):
        put_rows(*refs[:4], refs[-2])
        refs[-1][...] = jnp.zeros_like(refs[-1])

    return pl.pallas_call(
        body,
        grid=(rows, length // long),
        out_shape=(shape(base.shape), shape((8, 128), F32)),
        in_specs=[
            pl.BlockSpec(memory_space=pltpu.SMEM),
            pl.BlockSpec(chosen.shape, lambda row, part: (0, 0)),
            pl.BlockSpec((sel, values.shape[1]), lambda row, part: (row, 0)),
            pl.BlockSpec((1, long, half), lambda row, part: (row, part, 0)),
        ]
        + [pl.BlockSpec(memory_space=pl.ANY)] * len(after),
        out_specs=[
            pl.BlockSpec((1, long, half), lambda row, part: (row, part, 0)),
            pl.BlockSpec((8, 128), lambda row, part: (0, 0)),
        ],
        compiler_params=pltpu.CompilerParams(vmem_limit_bytes=24 << 20),
        cost_estimate=pl.CostEstimate(
            flops=2 * rows * sel * length * half, bytes_accessed=4 * base.size, transcendentals=0
        ),
        name="put_rows",
    )(bits, chosen, values, base, *after)


def first_columns(attention_ref, mixing_ref, vectors_ref, out_ref):
    half = attention_ref.shape[2]
    for k in range(3):
        out_ref[:, k * half : (k + 1) * half] = attention_ref[k]
    out_ref[:, 3 * half : 4 * half] = mixing_ref[...]
    out_ref[:, 4 * half :] = vectors_ref[...]


def second_columns(cuts, expand_ref, contract_ref, out_ref):
    at = 0
    for start, end in cuts:
        out_ref[:, at : at + end - start] = expand_ref[:, start:end]
        at += end - start
        out_ref[:, at : at + end - start] = contract_ref[:, start:end]
        at += end - start


def untouched(*refs):
    pass


def tie(value, *others):
    if not others:
        return value
    anywhere = pl.BlockSpec(memory_space=pl.ANY)
    return pl.pallas_call(
        untouched,
        out_shape=jax.ShapeDtypeStruct(value.shape, value.dtype),
        in_specs=[anywhere] * (1 + len(others)),
        out_specs=anywhere,
        input_output_aliases={0: 0},
        compiler_params=pltpu.CompilerParams(vmem_limit_bytes=1 << 20),
        cost_estimate=pl.CostEstimate(flops=0, bytes_accessed=0, transcendentals=0),
    )(value, *others)


class Cube:
    def __init__(self, count):
        self.count, self.depth = count, count.bit_length() - 1
        index = lax.axis_index("dp").astype(jnp.int32)
        self.bits = jnp.append(
            (index >> jnp.arange(self.depth)) & 1, lax.axis_index("mp").astype(jnp.int32)
        )
        short = self.depth // 3
        self.x, self.y = list(range(short)), list(range(short, 2 * short))
        self.z = list(range(2 * short, self.depth))
        self.far = self.z[1:]
        near = [self.x, self.y, self.z[:1]]
        self.orders = [sum(near[k:] + near[:k], []) for k in range(3)]

    def swap(self, value, bit):
        return lax.ppermute(value, "dp", [(i, i ^ (1 << bit)) for i in range(self.count)])


class Part:
    def __init__(self, value, bits, sent=None, start=0, width=None):
        self.value, self.bits, self.sent = value, list(bits), sent
        self.start, self.width = start, width or value.shape[2]

    def columns(self, start, end):
        return Part(self.value, self.bits, self.sent, self.start + start, end - start)


def thirds(width):
    ends = [(k * width // 3 + 64) // 128 * 128 for k in range(4)]
    return list(zip(ends, ends[1:]))


def start_exchange(cube, part, bit):
    part.sent = cube.swap(part.value, bit)
    return part


def stack_parts(plan, bits_ref, *refs):
    ins, outs = refs[: 2 * len(plan)], refs[2 * len(plan) :]
    for k, (bit, blocks) in enumerate(plan):
        mine = bits_ref[bit]
        for block in range(blocks):
            outs[k][mine, block] = ins[2 * k][block]
            outs[k][1 - mine, block] = ins[2 * k + 1][block]


def stack(cube, parts, bits, after=()):
    outs, args, plan = [], [], []
    for part, bit in zip(parts, bits):
        outs.append(shape((2,) + part.value.shape))
        args += [part.value, part.sent]
        plan.append((bit, part.value.shape[0]))
    found = call(functools.partial(stack_parts, plan), outs, args, after, cube.bits, name="stack_parts")
    return [
        Part(v.reshape((-1,) + v.shape[2:]), [bit] + part.bits) for v, part, bit in zip(found, parts, bits)
    ]


def split_columns(plan, own_ref, *out_refs):
    for ref, (start, end) in zip(out_refs, plan):
        ref[...] = own_ref[:, :, start:end]


def whole_rows(plan, bits_ref, *refs):
    ins, out_ref = refs[:-1], refs[-1]
    column = 0
    for k, (bit, places, start, width) in enumerate(plan):
        mine = bits_ref[bit]
        for block, place in enumerate(places):
            here = slice(column, column + width)
            out_ref[place + (mine << bit), :, here] = ins[2 * k][block, :, start : start + width]
            out_ref[place + ((1 - mine) << bit), :, here] = ins[2 * k + 1][block, :, start : start + width]
        column += width


def whole(cube, parts, bits, after=()):
    args, plan, width = [], [], 0
    for part, bit in zip(parts, bits):
        places = []
        for block in range(part.value.shape[0]):
            digits = [(block >> k) & 1 for k in range(len(part.bits))][::-1]
            places.append(sum(digit << b for digit, b in zip(digits, part.bits)))
        args += [part.value, part.sent]
        plan.append((bit, places, part.start, part.width))
        width += part.width
    rows = parts[0].value.shape[1]
    (found,) = call(
        functools.partial(whole_rows, plan),
        (shape((cube.count, rows, width)),),
        args,
        after,
        cube.bits,
        name="whole_rows",
    )
    return found.reshape(-1, width)


def fold_parts(plan, bits_ref, *refs):
    refs = list(refs)
    taken = [[(refs.pop(0), refs.pop(0) if sent else None) for sent, _, _ in sources] for _, _, sources in plan]
    for (bit, (high, low), sources), ins in zip(plan, taken):
        sent_ref, kept_ref = refs.pop(0), refs.pop(0)
        mine = bits_ref[bit]
        column = 0
        for (_, start, width), (value_ref, other_ref) in zip(sources, ins):
            there = slice(start, start + width)
            here = slice(column, column + width)
            for a in range(high):
                for b in range(low):
                    for index, out_ref in ((1 - mine, sent_ref), (mine, kept_ref)):
                        found = value_ref[a, index, b, :, there].astype(F32)
                        if other_ref is not None:
                            found += other_ref[a, index, b, :, there].astype(F32)
                        out_ref[a * low + b, :, here] = found.astype(out_ref.dtype)
            column += width


def fold(cube, groups, bits, after=()):
    args, outs, plan = [], [], []
    for sources, bit in zip(groups, bits):
        at = sources[0].bits.index(bit)
        high, low = 1 << at, 1 << (len(sources[0].bits) - at - 1)
        listed = []
        for part in sources:
            for value in (part.value, part.sent):
                if value is not None:
                    args.append(value.reshape((high, 2, low) + value.shape[1:]))
            listed.append((part.sent is not None, part.start, part.width))
        plan.append((bit, (high, low), listed))
        dims = (high * low, sources[0].value.shape[1], sum(p.width for p in sources))
        outs += [shape(dims), shape(dims, F32)]
    found = call(functools.partial(fold_parts, plan), outs, args, after, cube.bits, name="fold_parts")
    done = []
    for k, (sources, bit) in enumerate(zip(groups, bits)):
        left = [b for b in sources[0].bits if b != bit]
        done.append(Part(found[2 * k + 1], left, cube.swap(found[2 * k], bit)))
    return done


def cut(cube, total, ends=None):
    blocks = total.reshape(cube.count, -1, total.shape[1])
    bits = list(range(cube.depth))[::-1]
    ranges = ends or thirds(total.shape[1])
    return [Part(blocks, bits, None, start, end - start) for start, end in ranges if end > start]


def arrived(parts):
    return [p.sent for p in parts]


def sum_first(value_ref, sent_ref, attention_ref, mixing_ref, vectors_ref):
    half = attention_ref.shape[2]
    total = value_ref[0] + sent_ref[0].astype(F32)
    for k in range(3):
        attention_ref[k] = total[:, k * half : (k + 1) * half]
    mixing_ref[...] = total[:, 3 * half : 4 * half]
    vectors_ref[...] = total[:, 4 * half :].T


def sum_second(cuts, value_ref, sent_ref, expand_ref, contract_ref):
    at = 0
    for start, end in cuts:
        for side in range(2):
            width = end - start
            total = value_ref[0, :, at : at + width] + sent_ref[0, :, at : at + width].astype(F32)
            (expand_ref if side else contract_ref)[:, start:end] = total
            at += width


def other_core(value):
    return lax.ppermute(value, "mp", [(0, 1), (1, 0)])


def both_halves(value):
    other = other_core(value)
    low = lax.axis_index("mp") == 0
    return jnp.concatenate([jnp.where(low, value, other), jnp.where(low, other, value)], axis=-1)


def shards(
    tokens,
    segments,
    present,
    chosen,
    attention,
    mixing,
    expand,
    contract,
    prenorm,
    midnorm,
    router,
    cotangent,
    count,
):
    cube = Cube(count)
    row_count, length, half_width = tokens.shape
    sel_count = chosen.shape[1]
    token_count = row_count * sel_count
    own_rows = mixing.shape[1]
    width = 2 * half_width
    hidden_here = expand.shape[1]
    heads_here = half_width // HD
    by_row = (row_count, sel_count)

    vectors = jnp.pad(jnp.stack([prenorm, midnorm, router], axis=1), ((0, 0), (0, 125)))
    cuts = thirds(hidden_here)
    (first_own,) = call(
        first_columns, (shape((own_rows, 4 * half_width + 128)),), (attention, mixing.T, vectors), name="first_columns"
    )
    first_far = start_exchange(cube, Part(first_own[None], []), cube.far[-1])
    (second_own,) = call(
        functools.partial(second_columns, cuts),
        (shape((own_rows, 2 * hidden_here)),),
        (expand, contract.T),
        name="second_columns",
    )
    picked, bias, keep = select(tokens, [chosen, segments, present], True)

    def spread(far, after, begin=()):
        for bit in cube.far[-2::-1]:
            far = start_exchange(cube, stack(cube, [far], [far_bit(far)], after)[0], bit)
        column = stack(cube, [far], [far_bit(far)], after)[0]
        ends = thirds(column.width)
        found = call(
            functools.partial(split_columns, ends),
            [shape(column.value.shape[:2] + (end - start,)) for start, end in ends],
            [column.value],
            begin,
            name="split_columns",
        )
        return [Part(v, column.bits) for v in found]

    def far_bit(part):
        return cube.far[-1 - len(part.bits)]

    def step_bits(step):
        return [order[step] for order in cube.orders]

    def send(parts, step):
        return [start_exchange(cube, p, bit) for p, bit in zip(parts, step_bits(step))]

    steps = len(cube.orders[0])
    first_parts = spread(first_far, [picked])
    states = both_halves(tie(picked, first_parts[0].value)).reshape(token_count, width)
    first_parts = send(first_parts, 0)
    second_far = start_exchange(cube, Part(tie(second_own, *arrived([first_far]))[None], []), cube.far[-1])
    for step in range(1, steps):
        if step == steps - 1:
            (picked_grads,) = select(cotangent, [chosen], False, [first_parts[0].value])
            after = arrived([second_far]) + [picked_grads]
        else:
            after = [states] if step == 1 else []
        first_parts = send(stack(cube, first_parts, step_bits(step - 1), after), step)
    first_last = [p.value for p in first_parts]
    first = whole(cube, first_parts, step_bits(steps - 1))
    mix = first[:, 3 * half_width : 4 * half_width]
    second_parts = send(spread(second_far, [], first_last[:1]), 0)
    second_begun = []
    for step in range(1, steps - 1):
        second_parts = stack(cube, second_parts, step_bits(step - 1), [first] if step == 1 else [])
        second_begun = second_begun or [p.value for p in second_parts]
        second_parts = send(second_parts, step)
    upstream = both_halves(tie(picked_grads, *second_begun)).reshape(token_count, width)
    second_parts = stack(cube, second_parts, step_bits(steps - 2))
    each = hidden_here // 3
    up_parts, down_parts = [], []
    for p in second_parts:
        up_parts.append(Part(p.value[..., :each], p.bits))
        down_parts.append(Part(p.value[..., each:], p.bits))
    up = whole(cube, send(up_parts, steps - 1), step_bits(steps - 1))
    down_parts = send(down_parts, steps - 1)

    wide = shape((token_count, width))
    tall = shape((token_count, hidden_here))
    vector = shape((8, width), F32)
    normed, packed, probs, context, gains = call(
        functools.partial(attention_forward, *by_row),
        (
            wide,
            shape((token_count, 3 * half_width)),
            shape((row_count, heads_here, sel_count, sel_count), F32),
            shape((token_count, half_width)),
            vector,
        ),
        (states, first, bias),
        after=second_begun,
        flops=token_count * width * half_width * 6,
        name="attention_forward",
    )
    (att_own,) = call(
        mix_forward, (wide,), (context, mix), flops=2 * token_count * width * half_width, name="mix_forward"
    )
    att_other = other_core(att_own)
    normed_mid, activated, slope, feed_grad, down_grad = call(
        functools.partial(up_forward, *by_row),
        (wide, tall, tall, wide, shape((width, hidden_here))),
        (states, upstream, att_own, att_other, up, gains, keep),
        flops=4 * token_count * width * hidden_here,
        name="up_forward",
    )
    down = whole(cube, down_parts, step_bits(steps - 1), [activated])

    hidden_grad, mid_own = call(
        down_backward,
        (tall, wide),
        (feed_grad, down, slope, up),
        flops=4 * token_count * width * hidden_here,
        name="down_backward",
    )
    up_grad, feed_own = call(
        down_forward,
        (shape((width, hidden_here)), wide),
        (normed_mid, hidden_grad, activated, down),
        flops=4 * token_count * width * hidden_here,
        name="down_forward",
    )
    feed_other = other_core(feed_own)
    mid_other = tie(other_core(mid_own), feed_own)

    def back_bits(step):
        return [order[-1 - step] for order in cube.orders]

    def alone(parts):
        return [[p] for p in parts]

    both_grads = [list(pair) for pair in zip(cut(cube, down_grad), cut(cube, up_grad))]
    both_grads = fold(cube, both_grads, back_bits(0))

    mixed, packed_grad, pre_own, middle_grad, mid_gain_grad = call(
        functools.partial(attention_backward, *by_row),
        (
            wide,
            shape((token_count, 3 * half_width)),
            wide,
            shape((token_count, width), F32),
            vector,
        ),
        (states, att_own, att_other, mid_own, mid_other, upstream, keep, gains, mix, first, packed, probs),
        after=[both_grads[0].value],
        scratch=[pltpu.VMEM((token_count, half_width), BF)],
        flops=10 * token_count * width * half_width,
        name="attention_backward",
    )
    (first_grad,) = call(
        projection_grads,
        (shape((width, 4 * half_width)),),
        (normed, packed_grad, mixed, context),
        flops=8 * token_count * width * half_width,
        name="projection_grads",
    )
    finished, logit_grad, router_grad = call(
        functools.partial(final_forward, *by_row),
        (wide, shape((token_count, 1), F32), vector),
        (states, upstream, att_own, att_other, feed_own, feed_other, gains, keep),
        after=[first_grad],
        name="final_forward",
    )
    both_grads = fold(cube, alone(both_grads), back_bits(1), [logit_grad])
    pre_other = other_core(tie(pre_own, both_grads[0].value))
    total_grad, vector_grads = call(
        functools.partial(final_backward, *by_row),
        (wide, shape((width, 128))),
        (states, upstream, middle_grad, pre_own, pre_other, logit_grad, gains, mid_gain_grad, router_grad),
        scratch=[pltpu.VMEM((128, width), F32)],
        name="final_backward",
    )
    ends = [half_width * k // 3 // 128 * 128 for k in (0, 5, 8, 12)]
    first_grads = alone(cut(cube, first_grad, list(zip(ends, ends[1:]))))
    first_grads[-1] += cut(cube, vector_grads)
    first_grads = fold(cube, first_grads, back_bits(0))
    for step in range(2, steps):
        both_grads = fold(cube, alone(both_grads), back_bits(step), [first_grad] if step == 2 else [])
    first_grads = fold(cube, alone(first_grads), back_bits(1))
    both_grads = [both_grads]
    for bit in cube.far:
        both_grads = [fold(cube, both_grads, [bit])]
    result, done = put(tokens, chosen, finished, cube.bits, [both_grads[0][0].value])
    tokens_grad, _ = put(cotangent, chosen, total_grad, cube.bits, [done])
    for step in range(2, steps):
        first_grads = fold(cube, alone(first_grads), back_bits(step), [done] if step == 2 else [])
    first_grads = [first_grads]
    for bit in cube.far:
        first_grads = [fold(cube, first_grads, [bit])]
    (both_grad,), (first_grad,) = both_grads[0], first_grads[0]
    up_out, down_out = call(
        functools.partial(sum_second, cuts),
        (shape((own_rows, hidden_here), F32),) * 2,
        (both_grad.value, both_grad.sent),
        name="sum_second",
    )
    attention_out, mixing_out, vector_out = call(
        sum_first,
        (
            shape((3, own_rows, half_width), F32),
            shape((own_rows, half_width), F32),
            shape((128, own_rows), F32),
        ),
        (first_grad.value, first_grad.sent),
        name="sum_first",
    )
    return (
        result,
        tokens_grad,
        attention_out,
        mixing_out.T,
        up_out,
        down_out.T,
        vector_out[0],
        vector_out[1],
        vector_out[2],
    )


def solution(mesh):
    in_specs = (
        P("dp", None, "mp"),
        P("dp", None),
        P("dp", None),
        P("dp", None),
        P(None, "dp", "mp"),
        P("mp", "dp"),
        P("dp", "mp"),
        P("mp", "dp"),
        P("dp"),
        P("dp"),
        P("dp"),
        P("dp", None, "mp"),
    )
    out_specs = (
        P("dp", None, "mp"),
        P("dp", None, "mp"),
        P(None, "dp", "mp"),
        P("mp", "dp"),
        P("dp", "mp"),
        P("mp", "dp"),
        P("dp"),
        P("dp"),
        P("dp"),
    )
    count = mesh.shape["dp"]

    def body(*args):
        return shards(*args, count)

    return jax.shard_map(body, mesh=mesh, in_specs=in_specs, out_specs=out_specs, check_vma=False)
```
